32 devices in a mesh: grp: 2 (over y), row: 16 (over z, x, core).
Axes of the slice: x: 2, y: 2, z: 4, core: 2. Of those that a mesh axis runs over, the one named last changes fastest.
Arguments:
- features: float32 [128, 32, 512], P(('grp', 'row')), parts along dimension 0, may hold values from -6 to 6
- cotangent: float32 [128, 32, 512], P(('grp', 'row')), parts along dimension 0, may hold values from -8 to 8
- kernel: float32 [7, 7, 512], replicated, may hold values from -0.875 to 0.875
- norm_gain: float32 [512], replicated, may hold values from 0.1 to 1.9
- norm_bias: float32 [512], replicated, may hold values from -3 to 3
- in_weight: float32 [512, 2048], P('row'), may hold values from -0.25 to 0.25
- in_bias: float32 [2048], replicated, may hold values from -3 to 3
- out_weight: float32 [512, 2048], P('row'), may hold values from -0.125 to 0.125
- layer_scale: float32 [512], replicated, may hold values from 0.3 to 1.5
Outputs:
- output: float32 [128, 32, 512], P(('grp', 'row')), parts along dimension 0
- input_grad: float32 [128, 32, 512], P(('grp', 'row')), parts along dimension 0
- in_weight_grad: float32 [1024, 2048], P(('grp', 'row')), parts along dimension 0
- out_weight_grad: float32 [1024, 2048], P(('grp', 'row')), parts along dimension 0
- kernel_grad: float32 [14, 7, 512], P('grp'), parts along dimension 0
- gain_grad: float32 [1024], P('grp'), parts along dimension 0
- bias_grad: float32 [1024], P('grp'), parts along dimension 0
- in_bias_grad: float32 [4096], P('grp'), parts along dimension 0
- scale_grad: float32 [1024], P('grp'), parts along dimension 0
The draws below stay inside these ranges and needn't reach their ends.
There are 2 independent parts, one for each index of `grp`. The reference program is written for one: setup_inputs(seed, part) draws one part's arguments, and reference() takes and returns one part's arrays. A program takes and returns all parts, laid end to end along the dimension named above; an argument that names none is the same for every part. Nothing has to cross between parts.
All inputs are finite; a program needn't handle non-finite values.
Results may differ from the reference program's by a relative error of at most 0.0071.
Values may be sent and summed in bfloat16 or wider, within the bound.
No kernel may reach another device: no remote copies, remote signals or barrier semaphores. Data moves between devices by JAX's collectives and lax.ppermute only.
A program may use at most 64 MiB of HBM per device.

```python
import math
import jax
import jax.numpy as jnp
from jax import lax

C = 512
FF = 2048
COLS = 32
TAPS = 7
ROWS = 64


def strengthened(entries, stream_key, source, target, shards_of, factor):
    def block_of(dim):
        return (jnp.arange(entries.shape[dim]) // (entries.shape[dim] // shards_of)).reshape((-1,) + (1,) * (entries.ndim - 1 - dim))

    first = jax.random.permutation(stream_key, shards_of)[block_of(target)]
    other_side = (block_of(target) + shards_of // 2) % shards_of
    return jnp.where((block_of(source) == first) | (block_of(source) == other_side), factor * entries, entries)


def steps_of(rng, dims, split, smallest, high):
    loudness, own = 1.0, jax.random.fold_in(rng, 6)
    for dim, parts in split:
        draws = jnp.exp(jax.random.uniform(jax.random.fold_in(own, dim), (parts,), jnp.float32, smallest / len(split), high / len(split)))
        loudness = loudness * jnp.repeat(draws, dims[dim] // parts).reshape([-1 if axis == dim else 1 for axis in range(len(dims))])
    return loudness


def scatter_about(rng, extent, spread, limit, cuts=(), dtype=jnp.bfloat16):
    gain = steps_of(rng, extent, cuts, -0.22, 0.18) if cuts else 1.0
    result = jax.random.normal(rng, extent, jnp.float32) * spread * gain
    return jnp.minimum(jnp.maximum(result, -limit), limit).astype(dtype)


def noise_with(rng, shape, scale, bound, pieces, heavy, held_as=jnp.bfloat16):
    result = scale * jax.random.normal(rng, shape, jnp.float32)
    if pieces:
        result = result * steps_of(rng, shape, pieces, -0.22, 0.18)
    return jnp.clip(strengthened(result, jax.random.fold_in(rng, 3), *heavy), -bound, bound).astype(held_as)


def setup_inputs(seed: int = 0, part: int = 0) -> dict:
    key_of = jax.random.split(jax.random.key(seed), 10)
    part_splits = jax.random.split(jax.random.fold_in(key_of[9], part), 10)
    return {
        "features": scatter_about(part_splits[0], (ROWS, COLS, C), 1.0, 6.0, ((0, 16),), jnp.float32),
        "cotangent": noise_with(part_splits[1], (ROWS, COLS, C), 1.0, 8.0, ((0, 16),), (0, 2, 16, 2.0), jnp.float32),
        "kernel": scatter_about(key_of[2], (TAPS, TAPS, C), (TAPS * TAPS) ** -0.5, 0.875, (), jnp.float32),
        "norm_gain": jnp.clip(1.0 + 0.18 * jax.random.normal(key_of[3], (C,), jnp.float32), 0.1, 1.9),
        "norm_bias": scatter_about(key_of[4], (C,), 0.5, 3.0, (), jnp.float32),
        "in_weight": scatter_about(key_of[5], (C, FF), C ** -0.5, 0.25, ((0, 16),), jnp.float32),
        "in_bias": scatter_about(key_of[6], (FF,), 0.5, 3.0, (), jnp.float32),
        "out_weight": scatter_about(key_of[7], (C, FF), FF ** -0.5, 0.125, ((0, 16),), jnp.float32),
        "layer_scale": jnp.clip(jnp.exp(jax.random.uniform(key_of[8], (C,), jnp.float32, math.log(0.3), math.log(1.5))), 0.3, 1.5),
    }


def conv_taps(padded, kernel, row_count, col_count):
    running = jnp.zeros((row_count, col_count, padded.shape[2]), jnp.float32)
    for tap_row in range(7):
        for tap_col in range(7):
            running = running + padded[tap_row:tap_row + row_count, tap_col:tap_col + col_count] * kernel[tap_row, tap_col]
    return running

def reference(features, cotangent, kernel, norm_gain, norm_bias, in_weight, in_bias, out_weight, layer_scale):
    row_count, col_count, channels = features.shape
    hidden_count = in_weight.shape[1]
    norm_scale = 1.0 / math.sqrt(row_count * col_count)
    padded = jnp.pad(features, ((3, 3), (3, 3), (0, 0)))
    convolved = conv_taps(padded, kernel, row_count, col_count).reshape(-1, channels)
    pixel_count = row_count * col_count
    block_size = math.gcd(pixel_count, 8192)
    block_total = pixel_count // block_size
    in_narrow = in_weight.astype(jnp.bfloat16)
    out_narrow = out_weight.astype(jnp.bfloat16)
    conv_blocks = convolved.reshape(block_total, block_size, channels)
    input_blocks = features.reshape(block_total, block_size, channels)
    cotan_blocks = cotangent.reshape(block_total, block_size, channels)

    def step_block(running, inputs):
        conv_part, input_part, cotan_part = inputs
        average = lax.optimization_barrier(jnp.mean(conv_part, axis=1, keepdims=True))
        centred = conv_part - average
        inv_std = lax.rsqrt(lax.optimization_barrier(jnp.mean(centred * centred, axis=1, keepdims=True)) + 1e-06)
        normed = centred * inv_std
        normed_out = (normed * norm_gain + norm_bias).astype(jnp.bfloat16)
        preact = jnp.dot(normed_out, in_narrow, preferred_element_type=jnp.float32) + in_bias
        cdf_value = 0.5 * (1.0 + jax.scipy.special.erf(preact * 0.7071067811865476))
        activated = (preact * cdf_value).astype(jnp.bfloat16)
        mixed = lax.dot_general(activated, out_narrow, (((1,), (1,)), ((), ())), preferred_element_type=jnp.float32)
        output_part = input_part + layer_scale * mixed
        scale_term = lax.optimization_barrier(jnp.sum(cotan_part * mixed, axis=0))
        branch_grad = (layer_scale * cotan_part).astype(jnp.bfloat16)
        out_term = lax.dot_general(branch_grad, activated, (((0,), (0,)), ((), ())), preferred_element_type=jnp.float32)
        act_grad = jnp.dot(branch_grad, out_narrow, preferred_element_type=jnp.float32)
        gelu_slope = cdf_value + preact * jnp.exp(-0.5 * preact * preact) * 0.3989422804014327
        hidden_grad = act_grad * gelu_slope
        in_bias_term = lax.optimization_barrier(jnp.sum(hidden_grad, axis=0))
        hidden_narrow = hidden_grad.astype(jnp.bfloat16)
        in_term = lax.dot_general(normed_out, hidden_narrow, (((0,), (0,)), ((), ())), preferred_element_type=jnp.float32)
        out_grad = lax.dot_general(hidden_narrow, in_narrow, (((1,), (1,)), ((), ())), preferred_element_type=jnp.float32)
        gain_term = lax.optimization_barrier(jnp.sum(out_grad * normed, axis=0))
        bias_term = lax.optimization_barrier(jnp.sum(out_grad, axis=0))
        normed_grad = out_grad * norm_gain
        conv_grad = inv_std * (normed_grad - lax.optimization_barrier(jnp.mean(normed_grad, axis=1, keepdims=True)) - normed * lax.optimization_barrier(jnp.mean(normed_grad * normed, axis=1, keepdims=True)))
        updated = (running[0] + in_term, running[1] + out_term, running[2] + gain_term, running[3] + bias_term, running[4] + in_bias_term, running[5] + scale_term)
        return (updated, (output_part, conv_grad))
    initial = (jnp.zeros((channels, hidden_count), jnp.float32), jnp.zeros((channels, hidden_count), jnp.float32), jnp.zeros((channels,), jnp.float32), jnp.zeros((channels,), jnp.float32), jnp.zeros((hidden_count,), jnp.float32), jnp.zeros((channels,), jnp.float32))
    sums, stacked = lax.scan(step_block, initial, (conv_blocks, input_blocks, cotan_blocks))
    output = stacked[0].reshape(row_count, col_count, channels)
    conv_grad = stacked[1].reshape(row_count, col_count, channels)
    grad_padded = jnp.pad(conv_grad, ((3, 3), (3, 3), (0, 0)))
    input_grad = cotangent
    kernel_rows = []
    for tap_row in range(7):
        tap_list = []
        for tap_col in range(7):
            input_grad = input_grad + kernel[tap_row, tap_col] * grad_padded[6 - tap_row:6 - tap_row + row_count, 6 - tap_col:6 - tap_col + col_count]
            tap_list.append(lax.optimization_barrier(jnp.sum(padded[tap_row:tap_row + row_count, tap_col:tap_col + col_count] * conv_grad, axis=(0, 1))))
        kernel_rows.append(jnp.stack(tap_list))
    kernel_grad = norm_scale * jnp.stack(kernel_rows)
    return (output, input_grad, norm_scale * sums[0], norm_scale * sums[1], kernel_grad, norm_scale * sums[2], norm_scale * sums[3], norm_scale * sums[4], norm_scale * sums[5])
```

```python
import itertools
import math

import jax
import jax.numpy as jnp
from jax import lax
from jax.sharding import PartitionSpec as P

NARROW = jnp.bfloat16
WIDE = jnp.float32


def swap(value, bit):
    count = lax.axis_size("row")
    return lax.ppermute(value, "row", [(i, i ^ bit) for i in range(count)])


def shift(value, step):
    count = lax.axis_size("row")
    pairs = [(i, i + step) for i in range(count) if 0 <= i + step < count]
    return lax.ppermute(value, "row", pairs)


def conv_taps(padded, kernel, row_count, col_count):
    running = jnp.zeros((row_count, col_count, padded.shape[2]), jnp.float32)
    for tap_row in range(7):
        for tap_col in range(7):
            running = (
                running
                + padded[tap_row : tap_row + row_count, tap_col : tap_col + col_count]
                * kernel[tap_row, tap_col]
            )
    return running


def rimmed(block, low, high):
    joined = jnp.concatenate([low.astype(WIDE), block, high.astype(WIDE)], axis=0)
    return jnp.pad(joined, ((0, 0), (3, 3), (0, 0)))


def dot(left, right, dims):
    return lax.dot_general(left, right, (dims, ((), ())), preferred_element_type=WIDE)


def flipped(blocks, axis, bit_set):
    return jnp.where(bit_set == 1, jnp.flip(blocks, axis), blocks)


def canonical(blocks, me, bit_count):
    tail = blocks.shape[1:]
    blocks = blocks.reshape((2,) * bit_count + tail)
    for place in range(bit_count):
        blocks = flipped(blocks, bit_count - 1 - place, (me >> place) & 1)
    return blocks.reshape((2**bit_count,) + tail)


def per_device(
    features, cotangent, kernel, norm_gain, norm_bias, in_weight, in_bias, out_weight, layer_scale
):
    row_count, col_count, channels = features.shape
    own_rows, hidden_count = in_weight.shape
    pixels = row_count * col_count
    count = lax.axis_size("row")
    bit_count = count.bit_length() - 1
    me = lax.axis_index("row")
    far = count // 2
    core_bit = me & 1
    far_bit = me >> (bit_count - 1)
    quarter = hidden_count // 4
    mine = 2 * far_bit + core_bit
    norm_scale = 1.0 / math.sqrt(pixels * count)
    peers = list(range(1, count // 4))

    both = jnp.stack([in_weight, out_weight]).astype(NARROW)
    both = both.reshape(2, own_rows, 2, 2, quarter)
    keep = lax.dynamic_index_in_dim(both, core_bit, 3, keepdims=False)
    give = lax.dynamic_index_in_dim(both, 1 - core_bit, 3, keepdims=False)
    got = swap(give, 1)
    pair = jnp.stack([keep, got])
    stay = lax.dynamic_index_in_dim(pair, far_bit, 3, keepdims=False)
    leave = lax.dynamic_index_in_dim(pair, 1 - far_bit, 3, keepdims=False)
    got = swap(leave, far)
    block = jnp.stack([stay, got])

    narrow_rim = features.astype(NARROW)
    low = shift(narrow_rim[row_count - 3 :], 1)
    high = shift(narrow_rim[:3], -1)

    flat_input = features.reshape(-1, channels)
    flat_cotan = cotangent.reshape(-1, channels)
    branch_grad = (layer_scale * flat_cotan).astype(NARROW)

    def group_gather(value):
        two = jnp.stack([value, swap(value, far)])
        four = jnp.stack([two, swap(two, 1)])
        return four.reshape(-1, channels)

    branch_all = group_gather(branch_grad)
    gathered = [block] + [swap(block, 2 * p) for p in peers]
    weights = jnp.stack(gathered)
    weights = jnp.moveaxis(weights, 0, 1).reshape(count, 2, own_rows, quarter)
    weights = canonical(weights, me, bit_count)
    weights = jnp.moveaxis(weights, 1, 0).reshape(2, channels, quarter)
    in_narrow, out_narrow = weights[0], weights[1]

    padded = rimmed(features, low, high)
    convolved = conv_taps(padded, kernel, row_count, col_count).reshape(-1, channels)
    average = jnp.mean(convolved, axis=1, keepdims=True)
    centred = convolved - average
    inv_std = lax.rsqrt(jnp.mean(centred * centred, axis=1, keepdims=True) + 1e-06)
    normed = centred * inv_std
    normed_out = (normed * norm_gain + norm_bias).astype(NARROW)
    normed_all = group_gather(normed_out)

    bias_part = lax.dynamic_slice_in_dim(in_bias, mine * quarter, quarter)
    preact = dot(normed_all, in_narrow, ((1,), (0,))) + bias_part
    cdf_value = 0.5 * (1.0 + jax.scipy.special.erf(preact * 0.7071067811865476))
    activated = (preact * cdf_value).astype(NARROW)
    act_grad = dot(branch_all, out_narrow, ((1,), (0,)))
    gelu_slope = cdf_value + preact * jnp.exp(-0.5 * preact * preact) * 0.3989422804014327
    hidden_grad = act_grad * gelu_slope
    in_bias_part = jnp.sum(hidden_grad, axis=0)
    hidden_narrow = hidden_grad.astype(NARROW)

    def group_sum(partial):
        partial = partial.reshape(2, 2, pixels, channels)
        got = swap(partial[1].astype(NARROW), 1)
        half = partial[0] + got.astype(WIDE)
        got = swap(half[1].astype(NARROW), far)
        return half[0] + got.astype(WIDE)

    out_grad = group_sum(dot(hidden_narrow, in_narrow, ((1,), (1,))))
    mixed = group_sum(dot(activated, out_narrow, ((1,), (1,))))
    output = (flat_input + layer_scale * mixed).reshape(row_count, col_count, channels)
    scale_term = jnp.sum(flat_cotan * mixed, axis=0)

    grads = norm_scale * jnp.stack(
        [
            dot(normed_all, hidden_narrow, ((0,), (0,))),
            dot(branch_all, activated, ((0,), (0,))),
        ]
    )
    grads = jnp.moveaxis(grads.reshape(2, count, own_rows, quarter), 1, 0)
    grads = canonical(grads, me, bit_count)
    grads = grads.reshape(2, count // 4, 2, 2, own_rows, quarter)
    total = grads[:, 0]
    for p in peers:
        total = total + swap(grads[:, p].astype(NARROW), 2 * p).astype(WIDE)
    got = swap(total[1].astype(NARROW), far).astype(WIDE)
    halves = flipped(jnp.stack([total[0], got]), 0, far_bit)
    got = swap(halves[:, 1].astype(NARROW), 1).astype(WIDE)
    quarters = flipped(jnp.stack([halves[:, 0], got], axis=1), 1, core_bit)
    final = jnp.transpose(quarters, (2, 3, 0, 1, 4)).reshape(2, own_rows, hidden_count)
    in_weight_grad, out_weight_grad = final[0], final[1]

    gain_term = jnp.sum(out_grad * normed, axis=0)
    bias_term = jnp.sum(out_grad, axis=0)
    normed_grad = out_grad * norm_gain
    conv_grad = inv_std * (
        normed_grad
        - jnp.mean(normed_grad, axis=1, keepdims=True)
        - normed * jnp.mean(normed_grad * normed, axis=1, keepdims=True)
    )
    conv_grid = conv_grad.reshape(row_count, col_count, channels)
    narrow_grid = conv_grid.astype(NARROW)
    grad_low = shift(narrow_grid[row_count - 3 :], 1)
    grad_high = shift(narrow_grid[:3], -1)

    kernel_rows = []
    for tap_row in range(7):
        for tap_col in range(7):
            kernel_rows.append(
                jnp.sum(
                    padded[tap_row : tap_row + row_count, tap_col : tap_col + col_count]
                    * conv_grid,
                    axis=(0, 1),
                )
            )
    in_bias_term = lax.dynamic_update_slice_in_dim(
        jnp.zeros((hidden_count,), WIDE), in_bias_part, mine * quarter, 0
    )
    small = jnp.concatenate(
        [
            jnp.concatenate(kernel_rows),
            gain_term,
            bias_term,
            scale_term,
            in_bias_term,
        ]
    )
    small = norm_scale * small
    lengths = (49 * channels, channels, channels, channels, hidden_count)
    small = small.reshape(2, -1, 128)
    stay = lax.dynamic_index_in_dim(small, core_bit, 0, keepdims=False)
    leave = lax.dynamic_index_in_dim(small, 1 - core_bit, 0, keepdims=False)
    half = stay + swap(leave, 1)
    for place in range(1, bit_count):
        half = half + swap(half, 1 << place)
    small = flipped(jnp.stack([half, swap(half, 1)]), 0, core_bit).reshape(-1)
    ends = list(itertools.accumulate(lengths))
    parts = [small[end - size : end] for end, size in zip(ends, lengths)]

    grad_padded = rimmed(conv_grid, grad_low, grad_high)
    input_grad = cotangent
    for tap_row in range(7):
        for tap_col in range(7):
            input_grad = (
                input_grad
                + kernel[tap_row, tap_col]
                * grad_padded[
                    6 - tap_row : 6 - tap_row + row_count, 6 - tap_col : 6 - tap_col + col_count
                ]
            )
    return (
        output,
        input_grad,
        in_weight_grad,
        out_weight_grad,
        parts[0].reshape(7, 7, channels),
        parts[1],
        parts[2],
        parts[4],
        parts[3],
    )


def solution(mesh):
    return jax.shard_map(
        per_device,
        mesh=mesh,
        in_specs=(
            P(("grp", "row"), None, None),
            P(("grp", "row"), None, None),
            P(),
            P(),
            P(),
            P("row", None),
            P(),
            P("row", None),
            P(),
        ),
        out_specs=(
            P(("grp", "row"), None, None),
            P(("grp", "row"), None, None),
            P(("grp", "row"), None),
            P(("grp", "row"), None),
            P("grp", None, None),
            P("grp"),
            P("grp"),
            P("grp"),
            P("grp"),
        ),
        check_vma=False,
    )
```

```python
import functools
import math

import jax
import jax.numpy as jnp
from jax import lax
from jax.experimental import pallas as pl
from jax.experimental.pallas import tpu as pltpu
from jax.sharding import PartitionSpec as P

NARROW = jnp.bfloat16
WIDE = jnp.float32
TAPS = 7
RIM = 3
EDGE = 8
LANES = 128
SMALL_ROWS = 28


def swap(value, bit):
    count = lax.axis_size("row")
    return lax.ppermute(value, "row", [(i, i ^ bit) for i in range(count)])


def shift(value, step):
    count = lax.axis_size("row")
    pairs = [(i, i + step) for i in range(count) if 0 <= i + step < count]
    return lax.ppermute(value, "row", pairs)


def shaped(shape, dtype=WIDE):
    return jax.ShapeDtypeStruct(shape, dtype)


def run(body, outs, *operands, scratch=(), mib=16, flops=0):
    size = sum(math.prod(x.shape) * x.dtype.itemsize for x in (*operands, *outs))
    return pl.pallas_call(
        body,
        out_shape=outs,
        scratch_shapes=scratch,
        compiler_params=pltpu.CompilerParams(vmem_limit_bytes=mib * 2**20),
        cost_estimate=pl.CostEstimate(flops=flops, bytes_accessed=size, transcendentals=0),
    )(*operands)


def place():
    me = lax.axis_index("row")
    half = lax.axis_size("row") // 2
    return me, lax.rem(me, 2), lax.div(me, half)


def dot(left, right, dims):
    return lax.dot_general(left, right, (dims, ((), ())), preferred_element_type=WIDE)


def split_body(inw, outw, cotan, scale, feats, own, core, far, both, branch, first, last):
    _, core_bit, far_bit = place()
    quarter = own.shape[-1]
    rows = feats.shape[0]
    for target, c, z in (
        (own, core_bit, far_bit),
        (core, 1 - core_bit, far_bit),
        (far, core_bit, 1 - far_bit),
        (both, 1 - core_bit, 1 - far_bit),
    ):
        lanes = pl.ds(pl.multiple_of((2 * z + c) * quarter, quarter), quarter)
        target[0] = inw[:, lanes].astype(NARROW)
        target[1] = outw[:, lanes].astype(NARROW)
    branch[...] = (scale[...] * cotan[...]).astype(NARROW)
    first[...] = feats[:RIM].astype(NARROW)
    last[...] = feats[rows - RIM :].astype(NARROW)


def fill(padded, block, low, high):
    rows, cols, _ = block.shape
    padded[:, :EDGE, :] = jnp.zeros_like(padded[:, :EDGE, :])
    padded[:, EDGE + cols :, :] = jnp.zeros_like(padded[:, EDGE + cols :, :])
    inner = slice(EDGE, EDGE + cols)
    padded[:RIM, inner, :] = low[...].astype(WIDE)
    padded[RIM : RIM + rows, inner, :] = block[...]
    padded[RIM + rows :, inner, :] = high[...].astype(WIDE)


def taps_sum(padded, kernel, lanes, rows, cols, mirrored, start):
    total = list(start)
    for tap_col in range(TAPS):
        for row in range(rows + TAPS - 1):
            line = padded[row, pl.ds(EDGE - RIM + tap_col, cols), lanes]
            for out in range(rows):
                tap_row = row - out
                if 0 <= tap_row < TAPS:
                    if mirrored:
                        tap = kernel[TAPS - 1 - tap_row, pl.ds(TAPS - 1 - tap_col, 1), lanes]
                    else:
                        tap = kernel[tap_row, pl.ds(tap_col, 1), lanes]
                    total[out] = total[out] + line * tap
    return total


def conv_body(feats, low, high, kernel, gain, bias, normed, inv, narrow, padded, result):
    rows, cols, channels = feats.shape
    fill(padded, feats, low, high)

    @pl.loop(0, channels // LANES)
    def _(step):
        lanes = pl.ds(pl.multiple_of(step * LANES, LANES), LANES)
        zero = [jnp.zeros((cols, LANES), WIDE)] * rows
        total = taps_sum(padded, kernel, lanes, rows, cols, False, zero)
        for row in range(rows):
            result[pl.ds(row * cols, cols), lanes] = total[row]

    value = result[...]
    centred = value - jnp.mean(value, axis=1, keepdims=True)
    spread = lax.rsqrt(jnp.mean(centred * centred, axis=1, keepdims=True) + 1e-06)
    value = centred * spread
    normed[...] = value
    inv[...] = jnp.broadcast_to(spread, inv.shape)
    narrow[...] = (value * gain[...] + bias[...]).astype(NARROW)


def hidden_body(copied, *refs):
    count = lax.axis_size("row")
    me, _, far_bit = place()
    mine = 2 * far_bit + lax.rem(me, 2)
    normed, branch, in_bias = refs[:2], refs[2:4], refs[4]
    outs = 5 + (count // 2 if copied else 1)
    pieces = refs[5:outs]
    keep, send, active, hidden, out_narrow, bias_part, in_narrow = refs[outs:]
    half = normed[0].shape[0]
    if copied:
        own = pieces[0].shape[2]
        for pattern in range(count // 4):
            for z in range(2):
                piece = pieces[2 * pattern + z]
                for c in range(2):
                    device = jnp.bitwise_xor(me, z * (count // 2) + 2 * pattern + c)
                    rows = pl.ds(pl.multiple_of(device * own, own), own)
                    in_narrow[rows, :] = piece[c, 0]
                    out_narrow[rows, :] = piece[c, 1]
    else:
        in_narrow[...] = pieces[0][0]
        out_narrow[...] = pieces[0][1]
    bias_row = in_bias[pl.ds(mine, 1), :]
    total = jnp.zeros_like(bias_row)
    for side in (1, 0):
        preact = dot(normed[side][...], in_narrow[...], ((1,), (0,))) + bias_row
        act_grad = dot(branch[side][...], out_narrow[...], ((1,), (0,)))
        cdf = 0.5 * (1.0 + lax.erf(preact * 0.7071067811865476))
        rows = pl.ds(side * half, half)
        active[rows, :] = (preact * cdf).astype(NARROW)
        slope = cdf + preact * jnp.exp(-0.5 * preact * preact) * 0.3989422804014327
        grad = act_grad * slope
        total = total + jnp.sum(grad, axis=0, keepdims=True)
        narrow = grad.astype(NARROW)
        hidden[rows, :] = narrow
        out_grad = dot(narrow, in_narrow[...], ((1,), (1,)))
        if side:
            send[...] = out_grad.astype(NARROW)
        else:
            keep[...] = out_grad
    bias_part[...] = total


def weight_body(copied, norm_scale, *refs):
    count = lax.axis_size("row")
    me, _, _ = place()
    normed, branch = refs[:2], refs[2:4]
    active, hidden, out_narrow, scale = refs[4:8]
    outs = refs[8:-1]
    holder = refs[-1]
    half = normed[0].shape[0]
    first, second = pl.ds(0, half), pl.ds(half, half)
    for which, (left, right) in enumerate(((normed, hidden), (branch, active))):
        grad = dot(left[0][...], right[first, :], ((0,), (0,)))
        grad = grad + dot(left[1][...], right[second, :], ((0,), (0,)))
        holder[which] = norm_scale * grad
    if copied:
        own = outs[0].shape[3]
        for pattern in range(count // 4):
            for z in range(2):
                for c in range(2):
                    device = jnp.bitwise_xor(me, z * (count // 2) + 2 * pattern + c)
                    rows = pl.ds(pl.multiple_of(device * own, own), own)
                    for which in range(2):
                        target = outs[pattern]
                        target[z, c, which] = holder[which, rows, :].astype(target.dtype)
        rest = outs[count // 4 :]
    else:
        outs[0][...] = holder[...]
        rest = outs[1:]
    mixed_keep, mixed_send, scale_part = rest
    total = jnp.zeros_like(scale_part)
    for side, rows in enumerate((first, second)):
        mixed = dot(active[rows, :], out_narrow[...], ((1,), (1,)))
        total = total + jnp.sum(mixed * branch[side][...].astype(WIDE), axis=0, keepdims=True)
        if side:
            mixed_send[...] = mixed.astype(NARROW)
        else:
            mixed_keep[...] = mixed
    scale_part[...] = total / scale[...]


def fold_body(kept, got, stay, leave):
    size = stay.shape[0]
    stay[...] = kept[:size] + got[:size].astype(WIDE)
    leave[...] = (kept[size:] + got[size:].astype(WIDE)).astype(NARROW)


def norm_grad_body(kept, got, normed, inv, gain, grad, first, last, gain_part, bias_part):
    out_grad = kept[...] + got[...].astype(WIDE)
    value = normed[...]
    product = out_grad * value
    gain_part[...] = jnp.sum(product, axis=0, keepdims=True)
    bias_part[...] = jnp.sum(out_grad, axis=0, keepdims=True)
    normed_grad = out_grad * gain[...]
    mean = jnp.mean(normed_grad, axis=1, keepdims=True)
    along = jnp.mean(normed_grad * value, axis=1, keepdims=True)
    result = inv[:, :1] * (normed_grad - mean - value * along)
    grad[...] = result
    pixels = result.shape[0]
    rim = first.shape[0]
    first[...] = result[:rim].astype(NARROW)
    last[...] = result[pixels - rim :].astype(NARROW)


def kernel_grad_body(
    norm_scale, feats, low, high, grad, gain, bias, scale, in_bias, stay, leave, padded, small
):
    rows, cols, channels = feats.shape
    _, core_bit, far_bit = place()
    fill(padded, feats, low, high)

    def put(row, lanes, value):
        small[row // SMALL_ROWS, pl.ds(row % SMALL_ROWS, 1), lanes] = norm_scale * value

    @pl.loop(0, channels // LANES)
    def _(step):
        lanes = pl.ds(pl.multiple_of(step * LANES, LANES), LANES)
        own = [grad[pl.ds(row * cols, cols), lanes] for row in range(rows)]
        for tap_col in range(TAPS):
            totals = [jnp.zeros((8, LANES), WIDE)] * TAPS
            for row in range(rows + TAPS - 1):
                line = padded[row, pl.ds(EDGE - RIM + tap_col, cols), lanes]
                for out in range(rows):
                    tap_row = row - out
                    if 0 <= tap_row < TAPS:
                        product = line * own[out]
                        for part in range(cols // 8):
                            totals[tap_row] = totals[tap_row] + product[8 * part : 8 * part + 8]
            for tap_row in range(TAPS):
                value = jnp.sum(totals[tap_row], axis=0, keepdims=True)
                put(TAPS * tap_row + tap_col, lanes, value)

    everything = slice(None)
    row = TAPS * TAPS
    put(row, everything, gain[...])
    put(row + 1, everything, bias[...])
    put(row + 2, everything, scale[...])
    mine = 2 * far_bit + core_bit
    for part in range(4):
        own_part = jnp.where(mine == part, 1.0, 0.0)
        put(row + 3 + part, everything, own_part * in_bias[...])
    stay[...] = small[core_bit]
    leave[...] = small[1 - core_bit]


def input_grad_body(grad, low, high, kernel, cotan, result, padded):
    rows, cols, channels = grad.shape
    fill(padded, grad, low, high)

    @pl.loop(0, channels // LANES)
    def _(step):
        lanes = pl.ds(pl.multiple_of(step * LANES, LANES), LANES)
        start = [cotan[row, :, lanes] for row in range(rows)]
        total = taps_sum(padded, kernel, lanes, rows, cols, True, start)
        for row in range(rows):
            result[row, :, lanes] = total[row]


def output_body(feats, scale, kept, got, result):
    result[...] = feats[...] + scale[...] * (kept[...] + got[...].astype(WIDE))


def total_body(*refs):
    own, others, (stay, near, leave) = refs[0], refs[1:-3], refs[-3:]
    total = own[...]
    for other in others:
        total = total + other[...].astype(WIDE)
    stay[...] = total[0, 0]
    near[...] = total[0, 1].astype(NARROW)
    leave[...] = total[1].astype(NARROW)


def owner_body(stay, near, far, both, in_grad, out_grad):
    _, c, z = place()
    quarter = stay.shape[-1]
    for value, core, side in (
        (stay, c, z),
        (near, 1 - c, z),
        (far, c, 1 - z),
        (both, 1 - c, 1 - z),
    ):
        lanes = pl.ds(pl.multiple_of((2 * side + core) * quarter, quarter), quarter)
        in_grad[:, lanes] = value[0].astype(WIDE)
        out_grad[:, lanes] = value[1].astype(WIDE)


def small_body(mine, other, kernel_grad, gain, bias, scale, in_bias, held):
    _, core_bit, _ = place()
    held[core_bit] = mine[...]
    held[1 - core_bit] = other[...]

    def take(row):
        return held[row // SMALL_ROWS, pl.ds(row % SMALL_ROWS, 1), :]

    for tap_row in range(TAPS):
        for tap_col in range(TAPS):
            kernel_grad[tap_row, pl.ds(tap_col, 1), :] = take(TAPS * tap_row + tap_col)
    row = TAPS * TAPS
    gain[...] = take(row)
    bias[...] = take(row + 1)
    scale[...] = take(row + 2)
    quarter = take(row).shape[1]
    for part in range(4):
        in_bias[:, pl.ds(part * quarter, quarter)] = take(row + 3 + part)


def flipped(blocks, axis, bit_set):
    return jnp.where(bit_set == 1, jnp.flip(blocks, axis), blocks)


def canonical(blocks, me, bit_count):
    tail = blocks.shape[1:]
    blocks = blocks.reshape((2,) * bit_count + tail)
    for spot in range(bit_count):
        blocks = flipped(blocks, bit_count - 1 - spot, (me >> spot) & 1)
    return blocks.reshape((2**bit_count,) + tail)


def per_device(
    features, cotangent, kernel, norm_gain, norm_bias, in_weight, in_bias, out_weight, layer_scale
):
    row_count, col_count, channels = features.shape
    own_rows, hidden_count = in_weight.shape
    pixels = row_count * col_count
    count = lax.axis_size("row")
    bit_count = count.bit_length() - 1
    me = lax.axis_index("row")
    far = count // 2
    quarter = hidden_count // 4
    norm_scale = 1.0 / math.sqrt(pixels * count)
    patterns = count // 4
    copied = own_rows % 16 == 0
    flat_features = features.reshape(pixels, channels)
    flat_cotan = cotangent.reshape(pixels, channels)
    gain_row = norm_gain.reshape(1, channels)
    bias_row = norm_bias.reshape(1, channels)
    scale_row = layer_scale.reshape(1, channels)
    rim = (RIM, col_count, channels)
    padded = pltpu.VMEM((row_count + 2 * RIM, col_count + 2 * EDGE, channels), WIDE)
    conv_flops = 2 * TAPS * TAPS * pixels * channels

    piece = shaped((2, own_rows, quarter), NARROW)
    own, core, beyond, both, branch, first, last = run(
        split_body,
        (piece,) * 4 + (shaped((pixels, channels), NARROW), shaped(rim, NARROW), shaped(rim, NARROW)),
        in_weight,
        out_weight,
        flat_cotan,
        scale_row,
        features,
    )
    low = shift(last, 1)
    high = shift(first, -1)
    near = jnp.stack([own, swap(core, 1)])
    got = swap(jnp.stack([beyond, both]), far)
    distant = jnp.stack([got[0], swap(got[1], 1)])
    pieces = [near, distant]
    for p in range(1, patterns):
        pieces += [swap(near, 2 * p), swap(distant, 2 * p)]

    def group_gather(value):
        two = jnp.concatenate([value, swap(value, far)])
        return two, swap(two, 1)

    branch_all = group_gather(branch)
    normed, inv, normed_out = run(
        conv_body,
        (
            shaped((pixels, channels)),
            shaped((pixels, LANES)),
            shaped((pixels, channels), NARROW),
        ),
        features,
        low,
        high,
        kernel,
        gain_row,
        bias_row,
        scratch=(padded, pltpu.VMEM((pixels, channels), WIDE)),
        flops=conv_flops,
    )
    normed_all = group_gather(normed_out)

    if not copied:
        stacked = jnp.stack(pieces).reshape(patterns, 2, 2, 2, own_rows, quarter)
        stacked = jnp.moveaxis(stacked, 0, 1).reshape(count, 2, own_rows, quarter)
        stacked = jnp.moveaxis(canonical(stacked, me, bit_count), 1, 0)
        pieces = [stacked.reshape(2, channels, quarter)]
    group = 4 * pixels
    out_keep, out_send, active, hidden, out_narrow, in_bias_part = run(
        functools.partial(hidden_body, copied),
        (
            shaped((2 * pixels, channels)),
            shaped((2 * pixels, channels), NARROW),
            shaped((group, quarter), NARROW),
            shaped((group, quarter), NARROW),
            shaped((channels, quarter), NARROW),
            shaped((1, quarter)),
        ),
        *normed_all,
        *branch_all,
        in_bias.reshape(4, quarter),
        *pieces,
        scratch=(pltpu.VMEM((channels, quarter), NARROW),),
        mib=24,
        flops=6 * group * channels * quarter,
    )
    half = (shaped((pixels, channels)), shaped((pixels, channels), NARROW))
    out_stay, out_leave = run(fold_body, half, out_keep, swap(out_send, 1))
    out_got = swap(out_leave, far)

    grads = (2, 2, 2, own_rows, quarter)
    if copied:
        grad_shapes = (shaped(grads),) + (shaped(grads, NARROW),) * (patterns - 1)
    else:
        grad_shapes = (shaped((2, channels, quarter)),)
    *grad_parts, mixed_keep, mixed_send, scale_part = run(
        functools.partial(weight_body, copied, norm_scale),
        grad_shapes
        + (
            shaped((2 * pixels, channels)),
            shaped((2 * pixels, channels), NARROW),
            shaped((1, channels)),
        ),
        *normed_all,
        *branch_all,
        active,
        hidden,
        out_narrow,
        scale_row,
        scratch=(pltpu.VMEM((2, channels, quarter), WIDE),),
        mib=24,
        flops=6 * group * channels * quarter,
    )
    if not copied:
        parts = grad_parts[0].reshape(2, count, own_rows, quarter)
        parts = canonical(jnp.moveaxis(parts, 1, 0), me, bit_count)
        parts = parts.reshape(2, patterns, 2, 2, own_rows, quarter)
        grad_parts = [parts[:, 0]] + [parts[:, p].astype(NARROW) for p in range(1, patterns)]
    arrived = [swap(grad_parts[p], 2 * p) for p in range(1, patterns)]
    mixed_stay, mixed_leave = run(fold_body, half, mixed_keep, swap(mixed_send, 1))
    mixed_got = swap(mixed_leave, far)

    flat_rim = shaped((RIM * col_count, channels), NARROW)
    conv_grad, first, last, gain_part, bias_part = run(
        norm_grad_body,
        (
            shaped((pixels, channels)),
            flat_rim,
            flat_rim,
            shaped((1, channels)),
            shaped((1, channels)),
        ),
        out_stay,
        out_got,
        normed,
        inv,
        gain_row,
    )
    grad_low = shift(last, 1).reshape(rim)
    grad_high = shift(first, -1).reshape(rim)
    small = shaped((SMALL_ROWS, channels))
    stay, leave = run(
        functools.partial(kernel_grad_body, norm_scale),
        (small, small),
        features,
        low,
        high,
        conv_grad,
        gain_part,
        bias_part,
        scale_part,
        in_bias_part,
        scratch=(padded, pltpu.VMEM((2, SMALL_ROWS, channels), WIDE)),
        flops=conv_flops,
    )
    sums = stay + swap(leave, 1)
    for spot in range(1, bit_count):
        sums = sums + swap(sums, 1 << spot)

    input_grad = run(
        input_grad_body,
        (shaped(features.shape),),
        conv_grad.reshape(features.shape),
        grad_low,
        grad_high,
        kernel,
        cotangent,
        scratch=(padded,),
        flops=conv_flops,
    )[0]
    output = run(
        output_body,
        (shaped((pixels, channels)),),
        flat_features,
        scale_row,
        mixed_stay,
        mixed_got,
    )[0].reshape(features.shape)

    quarters = (2, own_rows, quarter)
    stay, near, leave = run(
        total_body,
        (shaped(quarters), shaped(quarters, NARROW), shaped((2,) + quarters, NARROW)),
        grad_parts[0],
        *arrived,
    )
    near_got = swap(near, 1)
    far_got = swap(leave, far)
    both_got = swap(far_got[1], 1)
    in_weight_grad, out_weight_grad = run(
        owner_body,
        (shaped((own_rows, hidden_count)),) * 2,
        stay,
        near_got,
        far_got[0],
        both_got,
    )
    kernel_grad, gain_grad, bias_grad, scale_grad, in_bias_grad = run(
        small_body,
        (
            shaped(kernel.shape),
            shaped((1, channels)),
            shaped((1, channels)),
            shaped((1, channels)),
            shaped((1, hidden_count)),
        ),
        sums,
        swap(sums, 1),
        scratch=(pltpu.VMEM((2, SMALL_ROWS, channels), WIDE),),
    )
    return (
        output,
        input_grad,
        in_weight_grad,
        out_weight_grad,
        kernel_grad,
        gain_grad.reshape(channels),
        bias_grad.reshape(channels),
        in_bias_grad.reshape(hidden_count),
        scale_grad.reshape(channels),
    )


def solution(mesh):
    return jax.shard_map(
        per_device,
        mesh=mesh,
        in_specs=(
            P(("grp", "row"), None, None),
            P(("grp", "row"), None, None),
            P(),
            P(),
            P(),
            P("row", None),
            P(),
            P("row", None),
            P(),
        ),
        out_specs=(
            P(("grp", "row"), None, None),
            P(("grp", "row"), None, None),
            P(("grp", "row"), None),
            P(("grp", "row"), None),
            P("grp", None, None),
            P("grp"),
            P("grp"),
            P("grp"),
            P("grp"),
        ),
        check_vma=False,
    )
```

```python
import functools
import math

import jax
import jax.numpy as jnp
from jax import lax
from jax.experimental import pallas as pl
from jax.experimental.pallas import tpu as pltpu
from jax.sharding import PartitionSpec as P

NARROW = jnp.bfloat16
WIDE = jnp.float32
TAPS = 7
RIM = 3
EDGE = 8
LANES = 128
SMALL_ROWS = 28


def swap(value, bit):
    count = lax.axis_size("row")
    return lax.ppermute(value, "row", [(i, i ^ bit) for i in range(count)])


def shift(value, step):
    count = lax.axis_size("row")
    pairs = [(i, i + step) for i in range(count) if 0 <= i + step < count]
    return lax.ppermute(value, "row", pairs)


def shaped(shape, dtype=WIDE):
    return jax.ShapeDtypeStruct(shape, dtype)


def swap_group(value):
    return lax.ppermute(value, "grp", [(0, 1), (1, 0)])


def run(body, outs, *operands, scratch=(), mib=16, order=0, apart=False):
    extra = {"in_specs": [pl.BlockSpec(memory_space=pltpu.HBM)] * len(operands)} if apart else {}
    return pl.pallas_call(
        body,
        out_shape=outs,
        **extra,
        scratch_shapes=scratch,
        compiler_params=pltpu.CompilerParams(vmem_limit_bytes=mib * 2**20),
        cost_estimate=pl.CostEstimate(flops=order * 10**9, bytes_accessed=0, transcendentals=0),
    )(*operands)


def place():
    me = lax.axis_index("row")
    return me, lax.rem(me, 2), lax.rem(lax.div(me, 2), 2)


def dot(left, right, dims):
    return lax.dot_general(left, right, (dims, ((), ())), preferred_element_type=WIDE)


def split_body(*refs):
    sources, outs, held, sems = refs[:5], refs[5:10], refs[10:15], refs[15]
    own, core, branch, first, last = outs
    copies = [
        pltpu.make_async_copy(source, copy, sems.at[k])
        for k, (source, copy) in enumerate(zip(sources, held))
    ]
    for copy in copies:
        copy.start()
    inw, outw, feats, cotan, scale = held
    _, c, x = place()
    quarter = own.shape[-1]
    rows = feats.shape[0]
    copies[0].wait()
    copies[1].wait()
    for target, part in (
        (own.at[0], 2 * x + c),
        (own.at[1], 2 * (1 - x) + c),
        (core.at[0], 2 * x + 1 - c),
        (core.at[1], 2 * (1 - x) + 1 - c),
    ):
        lanes = pl.ds(pl.multiple_of(part * quarter, quarter), quarter)
        target[0] = inw[:, lanes].astype(NARROW)
        target[1] = outw[:, lanes].astype(NARROW)
    copies[2].wait()
    first[...] = feats[:RIM].astype(NARROW)
    last[...] = feats[rows - RIM :].astype(NARROW)
    copies[3].wait()
    copies[4].wait()
    branch[...] = (scale[...] * cotan[...]).astype(NARROW)


def join_body(mine, other, *targets):
    which = lax.axis_index("grp")
    for side in range(2):
        full, sent = targets[2 * side : 2 * side + 2]
        full[:, 0] = mine[side]
        full[:, 1] = other[side]
        sent[...] = full[which]


def acts_body(normed, normed_got, branch, branch_got, acts):
    pixels = normed.shape[0]
    for which, (mine, got) in enumerate(((normed, normed_got), (branch, branch_got))):
        acts[which, :pixels] = mine[...]
        acts[which, pixels:] = got[...]


def stack_body(*refs):
    for place_in, ref in enumerate(refs[:-1]):
        refs[-1][place_in] = ref[...]


def fill(padded, block, low, high):
    rows, cols, _ = block.shape
    padded[:, :EDGE, :] = jnp.zeros_like(padded[:, :EDGE, :])
    padded[:, EDGE + cols :, :] = jnp.zeros_like(padded[:, EDGE + cols :, :])
    inner = slice(EDGE, EDGE + cols)
    padded[:RIM, inner, :] = low[...].astype(WIDE)
    padded[RIM : RIM + rows, inner, :] = block[...]
    padded[RIM + rows :, inner, :] = high[...].astype(WIDE)


def taps_sum(padded, kernel, lanes, rows, cols, mirrored, start):
    total = list(start)
    for tap_col in range(TAPS):
        for row in range(rows + TAPS - 1):
            line = padded[row, pl.ds(EDGE - RIM + tap_col, cols), lanes]
            for out in range(rows):
                tap_row = row - out
                if 0 <= tap_row < TAPS:
                    if mirrored:
                        tap = kernel[TAPS - 1 - tap_row, pl.ds(TAPS - 1 - tap_col, 1), lanes]
                    else:
                        tap = kernel[tap_row, pl.ds(tap_col, 1), lanes]
                    total[out] = total[out] + line * tap
    return total


def conv_body(feats, low, high, kernel, gain, bias, normed, inv, narrow, padded, result):
    rows, cols, channels = feats.shape
    fill(padded, feats, low, high)

    @pl.loop(0, channels // LANES)
    def _(step):
        lanes = pl.ds(pl.multiple_of(step * LANES, LANES), LANES)
        zero = [jnp.zeros((cols, LANES), WIDE)] * rows
        total = taps_sum(padded, kernel, lanes, rows, cols, False, zero)
        for row in range(rows):
            result[pl.ds(row * cols, cols), lanes] = total[row]

    value = result[...]
    centred = value - jnp.mean(value, axis=1, keepdims=True)
    spread = lax.rsqrt(jnp.mean(centred * centred, axis=1, keepdims=True) + 1e-06)
    value = centred * spread
    normed[...] = value
    inv[...] = jnp.broadcast_to(spread, inv.shape)
    narrow[...] = (value * gain[...] + bias[...]).astype(NARROW)


def hidden_body(copied, *refs):
    patterns = lax.axis_size("row") // 4
    me, _, _ = place()
    mine = lax.rem(me, 4)
    acts, in_bias = refs[:2], refs[2]
    pieces = refs[3:-7]
    keep, send, active, hidden, out_narrow, bias_part, weights = refs[-7:]
    half = acts[0].shape[1]
    if copied:
        own = pieces[0].shape[2]
        group = lax.axis_index("grp")
        for side in range(2):
            full, near, here, there = pieces[4 * side : 4 * side + 4]
            for pattern in range(patterns):
                for c in range(2):
                    device = jnp.bitwise_xor(me, 4 * pattern + 2 * side + c)
                    rows = pl.ds(pl.multiple_of(device * own, own), own)
                    if pattern < 2:
                        source = near if pattern else full
                        weights[0, rows, :] = source[0, c]
                        weights[1, rows, :] = source[1, c]
                    else:
                        weights[group, rows, :] = here[pattern - 2, c]
                        weights[1 - group, rows, :] = there[pattern - 2, c]
    else:
        weights[...] = pieces[0][...]
    in_narrow = weights.at[0]
    out_narrow[...] = weights[1]
    bias_row = in_bias[pl.ds(mine, 1), :]
    total = jnp.zeros_like(bias_row)
    for side in (1, 0):
        preact = dot(acts[side][0], in_narrow[...], ((1,), (0,))) + bias_row
        act_grad = dot(acts[side][1], out_narrow[...], ((1,), (0,)))
        cdf = 0.5 * (1.0 + lax.erf(preact * 0.7071067811865476))
        rows = pl.ds(side * half, half)
        active[rows, :] = (preact * cdf).astype(NARROW)
        slope = cdf + preact * jnp.exp(-0.5 * preact * preact) * 0.3989422804014327
        grad = act_grad * slope
        total = total + jnp.sum(grad, axis=0, keepdims=True)
        narrow = grad.astype(NARROW)
        hidden[rows, :] = narrow
        out_grad = dot(narrow, in_narrow[...], ((1,), (1,)))
        if side:
            send[...] = out_grad.astype(NARROW)
        else:
            keep[...] = out_grad
    bias_part[...] = total


def weight_body(norm_scale, *refs):
    acts = refs[:2]
    active, hidden, out_narrow, scale = refs[2:6]
    holder, mixed_keep, mixed_send, scale_part = refs[6:]
    half = acts[0].shape[1]
    first, second = pl.ds(0, half), pl.ds(half, half)
    for which, right in enumerate((hidden, active)):
        grad = dot(acts[0][which], right[first, :], ((0,), (0,)))
        grad = grad + dot(acts[1][which], right[second, :], ((0,), (0,)))
        holder[which] = norm_scale * grad
    total = jnp.zeros_like(scale_part)
    for side, rows in enumerate((first, second)):
        mixed = dot(active[rows, :], out_narrow[...], ((1,), (1,)))
        total = total + jnp.sum(mixed * acts[side][1].astype(WIDE), axis=0, keepdims=True)
        if side:
            mixed_send[...] = mixed.astype(NARROW)
        else:
            mixed_keep[...] = mixed
    scale_part[...] = total / scale[...]


def owners_body(holder, after, *targets):
    del after
    me, _, _ = place()
    own = targets[0].shape[2]
    for pattern, target in enumerate(targets):
        for c in range(2):
            device = jnp.bitwise_xor(me, 2 * pattern + c)
            rows = pl.ds(pl.multiple_of(device * own, own), own)
            for which in range(2):
                target[c, which] = holder[which, rows, :].astype(target.dtype)


def fold_body(kept, got, stay, leave):
    size = stay.shape[0]
    stay[...] = kept[:size] + got[:size].astype(WIDE)
    leave[...] = (kept[size:] + got[size:].astype(WIDE)).astype(NARROW)


def norm_grad_body(kept, got, normed, inv, gain, grad, first, last, gain_part, bias_part):
    out_grad = kept[...] + got[...].astype(WIDE)
    value = normed[...]
    product = out_grad * value
    gain_part[...] = jnp.sum(product, axis=0, keepdims=True)
    bias_part[...] = jnp.sum(out_grad, axis=0, keepdims=True)
    normed_grad = out_grad * gain[...]
    mean = jnp.mean(normed_grad, axis=1, keepdims=True)
    along = jnp.mean(normed_grad * value, axis=1, keepdims=True)
    result = inv[:, :1] * (normed_grad - mean - value * along)
    grad[...] = result
    pixels = result.shape[0]
    rim = first.shape[0]
    first[...] = result[:rim].astype(NARROW)
    last[...] = result[pixels - rim :].astype(NARROW)


def kernel_grad_body(
    norm_scale, feats, low, high, grad, gain, bias, scale, in_bias, stay, leave, padded, small
):
    rows, cols, channels = feats.shape
    me, core_bit, _ = place()
    fill(padded, feats, low, high)

    def put(row, lanes, value):
        small[row // SMALL_ROWS, pl.ds(row % SMALL_ROWS, 1), lanes] = norm_scale * value

    @pl.loop(0, channels // LANES)
    def _(step):
        lanes = pl.ds(pl.multiple_of(step * LANES, LANES), LANES)
        own = [grad[pl.ds(row * cols, cols), lanes] for row in range(rows)]
        for tap_col in range(TAPS):
            totals = [jnp.zeros((8, LANES), WIDE)] * TAPS
            for row in range(rows + TAPS - 1):
                line = padded[row, pl.ds(EDGE - RIM + tap_col, cols), lanes]
                for out in range(rows):
                    tap_row = row - out
                    if 0 <= tap_row < TAPS:
                        product = line * own[out]
                        for part in range(cols // 8):
                            totals[tap_row] = totals[tap_row] + product[8 * part : 8 * part + 8]
            for tap_row in range(TAPS):
                value = jnp.sum(totals[tap_row], axis=0, keepdims=True)
                put(TAPS * tap_row + tap_col, lanes, value)

    everything = slice(None)
    row = TAPS * TAPS
    put(row, everything, gain[...])
    put(row + 1, everything, bias[...])
    put(row + 2, everything, scale[...])
    mine = lax.rem(me, 4)
    for part in range(4):
        own_part = jnp.where(mine == part, 1.0, 0.0)
        put(row + 3 + part, everything, own_part * in_bias[...])
    stay[...] = small[core_bit]
    leave[...] = small[1 - core_bit]


def input_grad_body(grad, low, high, kernel, cotan, result, padded):
    rows, cols, channels = grad.shape
    fill(padded, grad, low, high)

    @pl.loop(0, channels // LANES)
    def _(step):
        lanes = pl.ds(pl.multiple_of(step * LANES, LANES), LANES)
        start = [cotan[row, :, lanes] for row in range(rows)]
        total = taps_sum(padded, kernel, lanes, rows, cols, True, start)
        for row in range(rows):
            result[row, :, lanes] = total[row]


def output_body(feats, scale, kept, got, result):
    result[...] = feats[...] + scale[...] * (kept[...] + got[...].astype(WIDE))


def total_body(turns, *refs):
    stay, leave = refs[-2:]
    for side in range(2):
        total = jnp.zeros(stay.shape[1:], WIDE)
        for part, turn in zip(refs, turns):
            if turn % 2 == side:
                total = total + part[...].astype(WIDE)
        stay[side] = total[0]
        leave[side] = total[1].astype(NARROW)


def owner_body(stay, got, in_grad, out_grad):
    _, c, x = place()
    quarter = stay.shape[-1]
    for value, part in (
        (stay[0], 2 * x + c),
        (stay[1], 2 * (1 - x) + c),
        (got[0], 2 * x + 1 - c),
        (got[1], 2 * (1 - x) + 1 - c),
    ):
        lanes = pl.ds(pl.multiple_of(part * quarter, quarter), quarter)
        in_grad[:, lanes] = value[0].astype(WIDE)
        out_grad[:, lanes] = value[1].astype(WIDE)


def small_body(mine, other, kernel_grad, gain, bias, scale, in_bias, held):
    _, core_bit, _ = place()
    held[core_bit] = mine[...]
    held[1 - core_bit] = other[...]

    def take(row):
        return held[row // SMALL_ROWS, pl.ds(row % SMALL_ROWS, 1), :]

    for tap_row in range(TAPS):
        for tap_col in range(TAPS):
            kernel_grad[tap_row, pl.ds(tap_col, 1), :] = take(TAPS * tap_row + tap_col)
    row = TAPS * TAPS
    gain[...] = take(row)
    bias[...] = take(row + 1)
    scale[...] = take(row + 2)
    quarter = take(row).shape[1]
    for part in range(4):
        in_bias[:, pl.ds(part * quarter, quarter)] = take(row + 3 + part)


def flipped(blocks, axis, bit_set):
    return jnp.where(bit_set == 1, jnp.flip(blocks, axis), blocks)


def canonical(blocks, me, bit_count):
    tail = blocks.shape[1:]
    blocks = blocks.reshape((2,) * bit_count + tail)
    for spot in range(bit_count):
        blocks = flipped(blocks, bit_count - 1 - spot, (me >> spot) & 1)
    return blocks.reshape((2**bit_count,) + tail)


def per_device(
    features, cotangent, kernel, norm_gain, norm_bias, in_weight, in_bias, out_weight, layer_scale
):
    row_count, col_count, channels = features.shape
    own_rows, hidden_count = in_weight.shape
    pixels = row_count * col_count
    count = lax.axis_size("row")
    bit_count = count.bit_length() - 1
    me = lax.axis_index("row")
    group_index = lax.axis_index("grp")
    quarter = hidden_count // 4
    norm_scale = 1.0 / math.sqrt(pixels * count)
    patterns = count // 4
    copied = own_rows % 16 == 0
    flat_features = features.reshape(pixels, channels)
    flat_cotan = cotangent.reshape(pixels, channels)
    gain_row = norm_gain.reshape(1, channels)
    bias_row = norm_bias.reshape(1, channels)
    scale_row = layer_scale.reshape(1, channels)
    rim = (RIM, col_count, channels)
    padded = pltpu.VMEM((row_count + 2 * RIM, col_count + 2 * EDGE, channels), WIDE)

    piece = (2, own_rows, quarter)
    sources = (in_weight, out_weight, features, flat_cotan, scale_row)
    own, core, branch, first, last = run(
        split_body,
        (
            shaped((2,) + piece, NARROW),
            shaped((2,) + piece, NARROW),
            shaped((pixels, channels), NARROW),
            shaped(rim, NARROW),
            shaped(rim, NARROW),
        ),
        *sources,
        scratch=tuple(pltpu.VMEM(x.shape, x.dtype) for x in sources)
        + (pltpu.SemaphoreType.DMA((len(sources),)),),
        mib=60,
        apart=True,
    )

    full_shape = shaped((2, 2, own_rows, quarter), NARROW)
    joined = run(
        join_body,
        (full_shape, shaped(piece, NARROW)) * 2,
        own,
        swap(core, 1),
    )
    low = shift(last, 1)
    high = shift(first, -1)
    pieces = []
    for side in range(2):
        full, sent = joined[2 * side : 2 * side + 2]
        here = [swap(sent, 4 * p + 2 * side) for p in range(2, patterns)]
        here = run(stack_body, (shaped((patterns - 2,) + piece, NARROW),), *here, order=8)[0]
        near = swap(full, 4 + 2 * side)
        pieces += [swap(full, 2) if side else full, near, here, swap_group(here)]

    branch_got = swap(branch, 2)
    normed, inv, normed_out = run(
        conv_body,
        (
            shaped((pixels, channels)),
            shaped((pixels, LANES)),
            shaped((pixels, channels), NARROW),
        ),
        features,
        low,
        high,
        kernel,
        gain_row,
        bias_row,
        scratch=(padded, pltpu.VMEM((pixels, channels), WIDE)),
    )
    group_shape = (2, 2 * pixels, channels)
    acts = run(
        acts_body,
        (shaped(group_shape, NARROW),),
        normed_out,
        swap(normed_out, 2),
        branch,
        branch_got,
    )[0]
    acts_got = swap(acts, 1)

    if not copied:
        lines = []
        for pattern in range(patterns):
            for side in range(2):
                full, near, here, there = pieces[4 * side : 4 * side + 4]
                if pattern < 2:
                    lines.append(near if pattern else full)
                else:
                    pair = jnp.stack([here[pattern - 2], there[pattern - 2]])
                    lines.append(flipped(pair, 0, group_index))
        lines = jnp.moveaxis(jnp.stack(lines), 1, 2).reshape(count, 2, own_rows, quarter)
        lines = jnp.moveaxis(canonical(lines, me, bit_count), 1, 0)
        pieces = [lines.reshape(2, channels, quarter)]
    group = 4 * pixels
    out_keep, out_send, active, hidden, out_narrow, in_bias_part = run(
        functools.partial(hidden_body, copied),
        (
            shaped((2 * pixels, channels)),
            shaped((2 * pixels, channels), NARROW),
            shaped((group, quarter), NARROW),
            shaped((group, quarter), NARROW),
            shaped((channels, quarter), NARROW),
            shaped((1, quarter)),
        ),
        acts,
        acts_got,
        in_bias.reshape(4, quarter),
        *pieces,
        scratch=(pltpu.VMEM((2, channels, quarter), NARROW),),
        mib=24,
    )
    half = (shaped((pixels, channels)), shaped((pixels, channels), NARROW))
    out_stay, out_leave = run(fold_body, half, out_keep, swap(out_send, 1))
    out_got = swap(out_leave, 2)

    owned = (2, 2, own_rows, quarter)
    holder, mixed_keep, mixed_send, scale_part = run(
        functools.partial(weight_body, norm_scale),
        (
            shaped((2, channels, quarter)),
            shaped((2 * pixels, channels)),
            shaped((2 * pixels, channels), NARROW),
            shaped((1, channels)),
        ),
        acts,
        acts_got,
        active,
        hidden,
        out_narrow,
        scale_row,
        mib=24,
    )
    kinds = (WIDE,) + (NARROW,) * (2 * patterns - 1)
    if copied:
        parts = run(owners_body, tuple(shaped(owned, kind) for kind in kinds), holder, out_leave)
    else:
        parts = holder.reshape(2, count, own_rows, quarter)
        parts = canonical(jnp.moveaxis(parts, 1, 0), me, bit_count)
        parts = parts.reshape(2 * patterns, 2, 2, own_rows, quarter)
        parts = [parts[p].astype(kind) for p, kind in enumerate(kinds)]
    turns = (*range(4, 2 * patterns), 2, 3, 1, 0)
    parts = [swap(parts[p], 2 * p) if p else parts[p] for p in turns]
    flat_rim = shaped((RIM * col_count, channels), NARROW)
    conv_grad, first, last, gain_part, bias_part = run(
        norm_grad_body,
        (
            shaped((pixels, channels)),
            flat_rim,
            flat_rim,
            shaped((1, channels)),
            shaped((1, channels)),
        ),
        out_stay,
        out_got,
        normed,
        inv,
        gain_row,
    )
    grad_low = shift(last, 1).reshape(rim)
    grad_high = shift(first, -1).reshape(rim)
    small = shaped((SMALL_ROWS, channels))
    stay, leave = run(
        functools.partial(kernel_grad_body, norm_scale),
        (small, small),
        features,
        low,
        high,
        conv_grad,
        gain_part,
        bias_part,
        scale_part,
        in_bias_part,
        scratch=(padded, pltpu.VMEM((2, SMALL_ROWS, channels), WIDE)),
    )
    sums = stay + swap(leave, 1)
    for spot in range(1, bit_count):
        sums = sums + swap(sums, 1 << spot)
        if spot == 1:
            sums, mixed_send = lax.optimization_barrier((sums, mixed_send))
    mixed_stay, mixed_leave = run(fold_body, half, mixed_keep, swap(mixed_send, 1))
    mixed_got = swap(mixed_leave, 2)

    input_grad = run(
        input_grad_body,
        (shaped(features.shape),),
        conv_grad.reshape(features.shape),
        grad_low,
        grad_high,
        kernel,
        cotangent,
        scratch=(padded,),
    )[0]
    output = run(
        output_body,
        (shaped((pixels, channels)),),
        flat_features,
        scale_row,
        mixed_stay,
        mixed_got,
    )[0].reshape(features.shape)

    stay, leave = run(
        functools.partial(total_body, turns),
        (shaped((2,) + piece), shaped((2,) + piece, NARROW)),
        *parts,
        order=20,
    )
    in_weight_grad, out_weight_grad = run(
        owner_body, (shaped((own_rows, hidden_count)),) * 2, stay, swap(leave, 1)
    )
    kernel_grad, gain_grad, bias_grad, scale_grad, in_bias_grad = run(
        small_body,
        (
            shaped(kernel.shape),
            shaped((1, channels)),
            shaped((1, channels)),
            shaped((1, channels)),
            shaped((1, hidden_count)),
        ),
        sums,
        swap(sums, 1),
        scratch=(pltpu.VMEM((2, SMALL_ROWS, channels), WIDE),),
    )
    return (
        output,
        input_grad,
        in_weight_grad,
        out_weight_grad,
        kernel_grad,
        gain_grad.reshape(channels),
        bias_grad.reshape(channels),
        in_bias_grad.reshape(hidden_count),
        scale_grad.reshape(channels),
    )


def solution(mesh):
    return jax.shard_map(
        per_device,
        mesh=mesh,
        in_specs=(
            P(("grp", "row"), None, None),
            P(("grp", "row"), None, None),
            P(),
            P(),
            P(),
            P("row", None),
            P(),
            P("row", None),
            P(),
        ),
        out_specs=(
            P(("grp", "row"), None, None),
            P(("grp", "row"), None, None),
            P(("grp", "row"), None),
            P(("grp", "row"), None),
            P("grp", None, None),
            P("grp"),
            P("grp"),
            P("grp"),
            P("grp"),
        ),
        check_vma=False,
    )
```

```python
import functools
import math

import jax
import jax.numpy as jnp
from jax import lax
from jax.experimental import pallas as pl
from jax.experimental.pallas import tpu as pltpu
from jax.sharding import PartitionSpec as P

NARROW = jnp.bfloat16
WIDE = jnp.float32
TAPS = 7
RIM = 3
EDGE = 8
LANES = 128
SMALL_ROWS = 28


def swap(value, bit):
    count = lax.axis_size("row")
    return lax.ppermute(value, "row", [(i, i ^ bit) for i in range(count)])


def swap_rim(value):
    count = lax.axis_size("row")
    pairs = [(i, i + 1) for i in range(1, count - 1, 2)]
    return lax.ppermute(value, "row", pairs + [(j, i) for i, j in pairs])


def shaped(shape, dtype=WIDE):
    return jax.ShapeDtypeStruct(shape, dtype)


def swap_group(value):
    return lax.ppermute(value, "grp", [(0, 1), (1, 0)])


def run(body, outs, *operands, scratch=(), mib=16, order=0, apart=False):
    extra = {}
    if apart:
        extra = {"in_specs": [pl.BlockSpec(memory_space=pltpu.HBM)] * len(operands)}
        operands = [pltpu.with_memory_space_constraint(x, pltpu.HBM) for x in operands]
    return pl.pallas_call(
        body,
        out_shape=outs,
        **extra,
        scratch_shapes=scratch,
        compiler_params=pltpu.CompilerParams(vmem_limit_bytes=mib * 2**20),
        cost_estimate=pl.CostEstimate(flops=order * 10**9, bytes_accessed=0, transcendentals=0),
    )(*operands)


def place():
    me = lax.axis_index("row")
    return me, lax.rem(me, 2), lax.rem(lax.div(me, 2), 2)


def dot(left, right, dims):
    return lax.dot_general(left, right, (dims, ((), ())), preferred_element_type=WIDE)


def split_body(*refs):
    inw_hbm, outw_hbm, in_bias_hbm = refs[:3]
    own, core, outer, branch, bias_part = refs[9:14]
    inw, outw, in_bias, sems = refs[20:]
    feats, cotan, scale = refs[14:17]
    pairs = list(zip(refs[3:9], refs[14:20]))
    pairs += [(inw_hbm, inw), (outw_hbm, outw), (in_bias_hbm, in_bias)]
    copies = [pltpu.make_async_copy(a, b, sems.at[k]) for k, (a, b) in enumerate(pairs)]
    for copy in copies[6:] + copies[:6]:
        copy.start()
    me, c, x = place()
    even = c == 0
    quarter = own.shape[-1]
    rows, cols, channels = feats.shape
    own_rows = inw.shape[0]
    copies[6].wait()
    copies[7].wait()
    for side in range(2):
        for part, near in ((2 * jnp.bitwise_xor(x, side) + c, True), (2 * jnp.bitwise_xor(x, side) + 1 - c, False)):
            lanes = pl.ds(pl.multiple_of(part * quarter, quarter), quarter)
            for which, source in enumerate((inw, outw)):
                value = source[:, lanes].astype(NARROW)
                if near:
                    own[side, which] = value
                else:
                    core[pl.ds((2 * side + which) * own_rows, own_rows), :] = value
    copies[0].wait()
    first = feats[:RIM].astype(NARROW).reshape(RIM * cols, channels)
    last = feats[rows - RIM :].astype(NARROW).reshape(RIM * cols, channels)
    core[4 * own_rows :, :] = jnp.where(even, last, first)
    outer[...] = jnp.where(even, first, last)
    copies[1].wait()
    copies[2].wait()
    branch[...] = (scale[...] * cotan[...].reshape(branch.shape)).astype(NARROW)
    copies[8].wait()
    lanes = pl.ds(pl.multiple_of(lax.rem(me, 4) * quarter, quarter), quarter)
    bias_part[...] = in_bias[:, lanes]
    for copy in copies[3:6]:
        copy.wait()


def join_body(mine, other, *targets):
    group = lax.axis_index("grp")
    for side in range(2):
        full, sent = targets[2 * side : 2 * side + 2]
        own_rows = mine.shape[2]
        for which in range(2):
            full[which, 0] = mine[side, which]
            full[which, 1] = other[pl.ds((2 * side + which) * own_rows, own_rows), :]
        sent[...] = full[group]


def acts_body(mine, got, acts):
    pixels = mine.shape[1]
    acts[:, :pixels] = mine[...]
    acts[:, pixels:] = got[...]


def stack_body(*refs):
    for place_in, ref in enumerate(refs[:-1]):
        refs[-1][place_in] = ref[...]


def fill(padded, block, inner, outer):
    rows, cols, channels = block.shape
    _, c, _ = place()
    padded[:, :EDGE, :] = jnp.zeros_like(padded[:, :EDGE, :])
    padded[:, EDGE + cols :, :] = jnp.zeros_like(padded[:, EDGE + cols :, :])
    middle = slice(EDGE, EDGE + cols)
    inner = inner.astype(WIDE).reshape(RIM, cols, channels)
    outer = outer.astype(WIDE).reshape(RIM, cols, channels)
    padded[:RIM, middle, :] = jnp.where(c == 0, outer, inner)
    padded[RIM : RIM + rows, middle, :] = block
    padded[RIM + rows :, middle, :] = jnp.where(c == 0, inner, outer)


def taps_sum(padded, kernel, lanes, rows, cols, mirrored, start):
    total = list(start)
    for tap_col in range(TAPS):
        for row in range(rows + TAPS - 1):
            line = padded[row, pl.ds(EDGE - RIM + tap_col, cols), lanes]
            for out in range(rows):
                tap_row = row - out
                if 0 <= tap_row < TAPS:
                    if mirrored:
                        tap = kernel[TAPS - 1 - tap_row, pl.ds(TAPS - 1 - tap_col, 1), lanes]
                    else:
                        tap = kernel[tap_row, pl.ds(tap_col, 1), lanes]
                    total[out] = total[out] + line * tap
    return total


def conv_body(
    feats, core_got, outer, kernel, gain, bias, branch, normed, inv, acts, padded, result
):
    rows, cols, channels = feats.shape
    start = core_got.shape[0] - RIM * cols
    fill(padded, feats[...], core_got[start:, :], outer[...])

    @pl.loop(0, channels // LANES)
    def _(step):
        lanes = pl.ds(pl.multiple_of(step * LANES, LANES), LANES)
        zero = [jnp.zeros((cols, LANES), WIDE)] * rows
        total = taps_sum(padded, kernel, lanes, rows, cols, False, zero)
        for row in range(rows):
            result[pl.ds(row * cols, cols), lanes] = total[row]

    value = result[...]
    centred = value - jnp.mean(value, axis=1, keepdims=True)
    spread = lax.rsqrt(jnp.mean(centred * centred, axis=1, keepdims=True) + 1e-06)
    value = centred * spread
    normed[...] = value
    inv[...] = jnp.broadcast_to(spread, inv.shape)
    acts[0] = (value * gain[...] + bias[...]).astype(NARROW)
    acts[1] = branch[...]


def hidden_body(copied, *refs):
    patterns = lax.axis_size("row") // 4
    me, _, _ = place()
    acts, in_bias = refs[:2], refs[2]
    scale = refs[3]
    pieces = refs[4:-7]
    keep, send, active, hidden, scale_part, bias_part, weights = refs[-7:]
    half = acts[0].shape[1]
    if copied:
        own = pieces[0].shape[2]
        group = lax.axis_index("grp")
        for side in range(2):
            full, near, here, there = pieces[4 * side : 4 * side + 4]
            for pattern in range(patterns):
                for c in range(2):
                    device = jnp.bitwise_xor(me, 4 * pattern + 2 * side + c)
                    rows = pl.ds(pl.multiple_of(device * own, own), own)
                    if pattern < 2:
                        source = near if pattern else full
                        weights[0, rows, :] = source[0, c]
                        weights[1, rows, :] = source[1, c]
                    else:
                        weights[group, rows, :] = here[pattern - 2, c]
                        weights[1 - group, rows, :] = there[pattern - 2, c]
    else:
        weights[...] = pieces[0][...]
    in_narrow = weights.at[0]
    out_narrow = weights.at[1]
    bias_row = in_bias[...]
    total = jnp.zeros_like(bias_row)
    scale_total = jnp.zeros_like(scale_part)
    for side in (1, 0):
        preact = dot(acts[side][0], in_narrow[...], ((1,), (0,))) + bias_row
        act_grad = dot(acts[side][1], out_narrow[...], ((1,), (0,)))
        cdf = 0.5 * (1.0 + lax.erf(preact * 0.7071067811865476))
        rows = pl.ds(side * half, half)
        activated = (preact * cdf).astype(NARROW)
        active[rows, :] = activated
        slope = cdf + preact * jnp.exp(-0.5 * preact * preact) * 0.3989422804014327
        grad = act_grad * slope
        total = total + jnp.sum(grad, axis=0, keepdims=True)
        narrow = grad.astype(NARROW)
        hidden[rows, :] = narrow
        out_grad = dot(narrow, in_narrow[...], ((1,), (1,)))
        mixed = dot(activated, out_narrow[...], ((1,), (1,)))
        scale_total = scale_total + jnp.sum(
            mixed * acts[side][1].astype(WIDE), axis=0, keepdims=True
        )
        if side:
            send[0] = out_grad.astype(NARROW)
            send[1] = mixed.astype(NARROW)
        else:
            keep[0] = out_grad
            keep[1] = mixed
    bias_part[...] = total
    scale_part[...] = scale_total / scale[...]


def weight_body(norm_scale, *refs):
    acts, (active, hidden, holder) = refs[:2], refs[2:]
    half = acts[0].shape[1]
    first, second = pl.ds(0, half), pl.ds(half, half)
    for which, right in enumerate((hidden, active)):
        grad = dot(acts[0][which], right[first, :], ((0,), (0,)))
        grad = grad + dot(acts[1][which], right[second, :], ((0,), (0,)))
        holder[which] = norm_scale * grad


def owners_body(turns, holder, after, *targets):
    del after
    me, _, _ = place()
    own = targets[0].shape[2]
    for pattern, target in zip(turns, targets):
        for c in range(2):
            device = jnp.bitwise_xor(me, 2 * pattern + c)
            rows = pl.ds(pl.multiple_of(device * own, own), own)
            for which in range(2):
                target[c, which] = holder[which, rows, :].astype(target.dtype)


def fold_body(kept, got, stay, leave, mixed_stay, mixed_leave):
    size = stay.shape[0]
    for which, (near, away) in enumerate(((stay, leave), (mixed_stay, mixed_leave))):
        near[...] = kept[which, :size] + got[which, :size].astype(WIDE)
        away[...] = (kept[which, size:] + got[which, size:].astype(WIDE)).astype(NARROW)


def conv_grad_body(norm_scale, *refs):
    kept, got, normed, inv, gain, feats, core_got, outer, scale, in_bias = refs[:10]
    grad, rim_out, stay, leave, padded, small = refs[10:]
    rows, cols, channels = feats.shape
    me, c, _ = place()
    out_grad = kept[...] + got[...].astype(WIDE)
    value = normed[...]
    normed_grad = out_grad * gain[...]
    mean = jnp.mean(normed_grad, axis=1, keepdims=True)
    along = jnp.mean(normed_grad * value, axis=1, keepdims=True)
    result = inv[:, :1] * (normed_grad - mean - value * along)
    grad[...] = result
    pixels = rows * cols
    rim = RIM * cols
    rim_out[...] = jnp.where(c == 0, result[:rim], result[pixels - rim :]).astype(NARROW)
    leave[:rim, :] = jnp.where(c == 0, result[pixels - rim :], result[:rim])
    fill(padded, feats[...], core_got[core_got.shape[0] - rim :, :], outer[...])

    def put(row, lanes, total):
        small[row // SMALL_ROWS, pl.ds(row % SMALL_ROWS, 1), lanes] = norm_scale * total

    @pl.loop(0, channels // LANES)
    def _(step):
        lanes = pl.ds(pl.multiple_of(step * LANES, LANES), LANES)
        own = [grad[pl.ds(row * cols, cols), lanes] for row in range(rows)]
        for tap_col in range(TAPS):
            totals = [jnp.zeros((8, LANES), WIDE)] * TAPS
            for row in range(rows + TAPS - 1):
                line = padded[row, pl.ds(EDGE - RIM + tap_col, cols), lanes]
                for out in range(rows):
                    tap_row = row - out
                    if 0 <= tap_row < TAPS:
                        product = line * own[out]
                        for part in range(cols // 8):
                            totals[tap_row] = totals[tap_row] + product[8 * part : 8 * part + 8]
            for tap_row in range(TAPS):
                total = jnp.sum(totals[tap_row], axis=0, keepdims=True)
                put(TAPS * tap_row + tap_col, lanes, total)

    everything = slice(None)
    row = TAPS * TAPS
    put(row, everything, jnp.sum(out_grad * value, axis=0, keepdims=True))
    put(row + 1, everything, jnp.sum(out_grad, axis=0, keepdims=True))
    put(row + 2, everything, scale[...])
    for part in range(4):
        own_part = jnp.where(lax.rem(me, 4) == part, 1.0, 0.0)
        put(row + 3 + part, everything, own_part * in_bias[...])
    stay[...] = small[c]
    leave[rim:, :] = small[1 - c]


def input_grad_body(grad, core_got, outer, kernel, cotan, result, padded):
    rows, cols, channels = cotan.shape
    fill(padded, grad[...].reshape(cotan.shape), core_got[: RIM * cols, :], outer[...])

    @pl.loop(0, channels // LANES)
    def _(step):
        lanes = pl.ds(pl.multiple_of(step * LANES, LANES), LANES)
        start = [cotan[row, :, lanes] for row in range(rows)]
        total = taps_sum(padded, kernel, lanes, rows, cols, True, start)
        for row in range(rows):
            result[row, :, lanes] = total[row]


def output_body(feats, scale, kept, got, result):
    mixed = kept[...] + got[...].astype(WIDE)
    result[...] = feats[...] + (scale[...] * mixed).reshape(feats.shape)


def total_body(turns, *refs):
    stay, leave = refs[-2:]
    for side in range(2):
        total = jnp.zeros(stay.shape[1:], WIDE)
        for part, turn in zip(refs, turns):
            if turn % 2 == side:
                total = total + part[...].astype(WIDE)
        stay[side] = total[0]
        leave[side] = total[1].astype(NARROW)


def owner_body(stay, got, in_grad, out_grad):
    _, c, x = place()
    quarter = stay.shape[-1]
    for value, part in (
        (stay[0], 2 * x + c),
        (stay[1], 2 * (1 - x) + c),
        (got[0], 2 * x + 1 - c),
        (got[1], 2 * (1 - x) + 1 - c),
    ):
        lanes = pl.ds(pl.multiple_of(part * quarter, quarter), quarter)
        in_grad[:, lanes] = value[0].astype(WIDE)
        out_grad[:, lanes] = value[1].astype(WIDE)


def small_body(mine, other, kernel_grad, gain, bias, scale, in_bias, held):
    _, core_bit, _ = place()
    held[core_bit] = mine[...]
    held[1 - core_bit] = other[...]

    def take(row):
        return held[row // SMALL_ROWS, pl.ds(row % SMALL_ROWS, 1), :]

    for tap_row in range(TAPS):
        for tap_col in range(TAPS):
            kernel_grad[tap_row, pl.ds(tap_col, 1), :] = take(TAPS * tap_row + tap_col)
    row = TAPS * TAPS
    gain[...] = take(row)
    bias[...] = take(row + 1)
    scale[...] = take(row + 2)
    quarter = take(row).shape[1]
    for part in range(4):
        in_bias[:, pl.ds(part * quarter, quarter)] = take(row + 3 + part)


def flipped(blocks, axis, bit_set):
    return jnp.where(bit_set == 1, jnp.flip(blocks, axis), blocks)


def canonical(blocks, me, bit_count):
    tail = blocks.shape[1:]
    blocks = blocks.reshape((2,) * bit_count + tail)
    for spot in range(bit_count):
        blocks = flipped(blocks, bit_count - 1 - spot, (me >> spot) & 1)
    return blocks.reshape((2**bit_count,) + tail)


def per_device(
    features, cotangent, kernel, norm_gain, norm_bias, in_weight, in_bias, out_weight, layer_scale
):
    row_count, col_count, channels = features.shape
    own_rows, hidden_count = in_weight.shape
    pixels = row_count * col_count
    count = lax.axis_size("row")
    bit_count = count.bit_length() - 1
    me = lax.axis_index("row")
    group_index = lax.axis_index("grp")
    quarter = hidden_count // 4
    norm_scale = 1.0 / math.sqrt(pixels * count)
    patterns = count // 4
    copied = own_rows % 16 == 0
    gain_row = norm_gain.reshape(1, channels)
    bias_row = norm_bias.reshape(1, channels)
    scale_row = layer_scale.reshape(1, channels)
    rim = RIM * col_count
    padded = pltpu.VMEM((row_count + 2 * RIM, col_count + 2 * EDGE, channels), WIDE)

    piece = (2, own_rows, quarter)
    once = (features, cotangent, scale_row, kernel, gain_row, bias_row)
    own, core, outer, branch, in_bias_own, feats, cotan, scale, taps, gain, bias = run(
        split_body,
        (
            shaped((2,) + piece, NARROW),
            shaped((4 * own_rows + rim, channels), NARROW),
            shaped((rim, channels), NARROW),
            shaped((pixels, channels), NARROW),
            shaped((1, quarter)),
        )
        + tuple(shaped(x.shape) for x in once),
        in_weight,
        out_weight,
        in_bias.reshape(1, hidden_count),
        *once,
        scratch=(
            pltpu.VMEM(in_weight.shape, WIDE),
            pltpu.VMEM(out_weight.shape, WIDE),
            pltpu.VMEM((1, hidden_count), WIDE),
            pltpu.SemaphoreType.DMA((9,)),
        ),
        apart=True,
    )
    core_got = swap(core, 1)
    outer_got = swap_rim(outer)
    full_shape = shaped((2, 2, own_rows, quarter), NARROW)
    joined = run(
        join_body,
        (full_shape, shaped(piece, NARROW)) * 2,
        own,
        core_got,
    )
    pieces = []
    for side in range(2):
        full, sent = joined[2 * side : 2 * side + 2]
        here = [swap(sent, 4 * p + 2 * side) for p in range(2, patterns)]
        here = run(stack_body, (shaped((patterns - 2,) + piece, NARROW),), *here, order=8)[0]
        near = swap(full, 4 + 2 * side)
        pieces += [swap(full, 2) if side else full, near, here, swap_group(here)]

    normed, inv, acts = run(
        conv_body,
        (
            shaped((pixels, channels)),
            shaped((pixels, LANES)),
            shaped((2, pixels, channels), NARROW),
        ),
        feats,
        core_got,
        outer_got,
        taps,
        gain,
        bias,
        branch,
        scratch=(padded, pltpu.VMEM((pixels, channels), WIDE)),
    )
    acts = run(
        acts_body, (shaped((2, 2 * pixels, channels), NARROW),), acts, swap(acts, 2)
    )[0]
    acts_got = swap(acts, 1)

    if not copied:
        lines = []
        for pattern in range(patterns):
            for side in range(2):
                full, near, here, there = pieces[4 * side : 4 * side + 4]
                if pattern < 2:
                    lines.append(near if pattern else full)
                else:
                    pair = jnp.stack([here[pattern - 2], there[pattern - 2]])
                    lines.append(flipped(pair, 0, group_index))
        lines = jnp.moveaxis(jnp.stack(lines), 1, 2).reshape(count, 2, own_rows, quarter)
        lines = jnp.moveaxis(canonical(lines, me, bit_count), 1, 0)
        pieces = [lines.reshape(2, channels, quarter)]
    group = 4 * pixels
    both = (2, 2 * pixels, channels)
    keep, send, active, hidden, scale_part, in_bias_part = run(
        functools.partial(hidden_body, copied),
        (
            shaped(both),
            shaped(both, NARROW),
            shaped((group, quarter), NARROW),
            shaped((group, quarter), NARROW),
            shaped((1, channels)),
            shaped((1, quarter)),
        ),
        acts,
        acts_got,
        in_bias_own,
        scale,
        *pieces,
        scratch=(pltpu.VMEM((2, channels, quarter), NARROW),),
        mib=24,
    )
    half = (shaped((pixels, channels)), shaped((pixels, channels), NARROW))
    out_stay, out_leave, mixed_stay, mixed_leave = run(fold_body, half * 2, keep, swap(send, 1))
    out_got = swap(out_leave, 2)

    owned = (2, 2, own_rows, quarter)
    holder = run(
        functools.partial(weight_body, norm_scale),
        (shaped((2, channels, quarter)),),
        acts,
        acts_got,
        active,
        hidden,
        mib=24,
    )[0]
    conv_grad, rim_out, stay, leave = run(
        functools.partial(conv_grad_body, norm_scale),
        (
            shaped((pixels, channels)),
            shaped((rim, channels), NARROW),
            shaped((SMALL_ROWS, channels)),
            shaped((rim + SMALL_ROWS, channels)),
        ),
        out_stay,
        out_got,
        normed,
        inv,
        gain,
        feats,
        core_got,
        outer_got,
        scale_part,
        in_bias_part,
        scratch=(padded, pltpu.VMEM((2, SMALL_ROWS, channels), WIDE)),
    )
    rim_got = swap_rim(rim_out)
    leave_got = swap(leave, 1)
    sums = stay + leave_got[rim:]
    sums = sums + swap(sums, 2)
    early = sums
    for spot in range(2, bit_count):
        sums = sums + swap(sums, 1 << spot)

    turns = (*range(4, 2 * patterns), 2, 3, 1, 0)
    kinds = [NARROW if p else WIDE for p in turns]
    if copied:
        parts = []
        for some, after in ((slice(0, 2), out_leave), (slice(2, None), early)):
            parts += run(
                functools.partial(owners_body, turns[some]),
                tuple(shaped(owned, kind) for kind in kinds[some]),
                holder,
                after,
            )
    else:
        parts = holder.reshape(2, count, own_rows, quarter)
        parts = canonical(jnp.moveaxis(parts, 1, 0), me, bit_count)
        parts = parts.reshape(2 * patterns, 2, 2, own_rows, quarter)
        parts = [parts[p].astype(kind) for p, kind in zip(turns, kinds)]
    parts = [swap(part, 2 * p) if p else part for p, part in zip(turns, parts)]

    input_grad = run(
        input_grad_body,
        (shaped(features.shape),),
        conv_grad,
        leave_got,
        rim_got,
        taps,
        cotan,
        scratch=(padded,),
    )[0]
    output = run(
        output_body,
        (shaped(features.shape),),
        feats,
        scale,
        mixed_stay,
        swap(mixed_leave, 2),
    )[0]
    parts, input_grad, output = lax.optimization_barrier((parts, input_grad, output))

    stay, leave = run(
        functools.partial(total_body, turns),
        (shaped((2,) + piece), shaped((2,) + piece, NARROW)),
        *parts,
        order=20,
    )
    in_weight_grad, out_weight_grad = run(
        owner_body, (shaped((own_rows, hidden_count)),) * 2, stay, swap(leave, 1)
    )
    kernel_grad, gain_grad, bias_grad, scale_grad, in_bias_grad = run(
        small_body,
        (
            shaped(kernel.shape),
            shaped((1, channels)),
            shaped((1, channels)),
            shaped((1, channels)),
            shaped((1, hidden_count)),
        ),
        sums,
        swap(sums, 1),
        scratch=(pltpu.VMEM((2, SMALL_ROWS, channels), WIDE),),
    )
    return (
        output,
        input_grad,
        in_weight_grad,
        out_weight_grad,
        kernel_grad,
        gain_grad.reshape(channels),
        bias_grad.reshape(channels),
        in_bias_grad.reshape(hidden_count),
        scale_grad.reshape(channels),
    )


def solution(mesh):
    return jax.shard_map(
        per_device,
        mesh=mesh,
        in_specs=(
            P(("grp", "row"), None, None),
            P(("grp", "row"), None, None),
            P(),
            P(),
            P(),
            P("row", None),
            P(),
            P("row", None),
            P(),
        ),
        out_specs=(
            P(("grp", "row"), None, None),
            P(("grp", "row"), None, None),
            P(("grp", "row"), None),
            P(("grp", "row"), None),
            P("grp", None, None),
            P("grp"),
            P("grp"),
            P("grp"),
            P("grp"),
        ),
        check_vma=False,
    )
```

```python
import functools
import math

import jax
import jax.numpy as jnp
from jax import lax
from jax.experimental import pallas as pl
from jax.experimental.pallas import tpu as pltpu
from jax.sharding import PartitionSpec as P

NARROW = jnp.bfloat16
WIDE = jnp.float32
TAPS = 7
RIM = 3
EDGE = 8
LANES = 128
SMALL_ROWS = 28


def swap(value, bit):
    count = lax.axis_size("row")
    return lax.ppermute(value, "row", [(i, i ^ bit) for i in range(count)])


def swap_rim(value):
    count = lax.axis_size("row")
    pairs = [(i, i + 1) for i in range(1, count - 1, 2)]
    return lax.ppermute(value, "row", pairs + [(j, i) for i, j in pairs])


def shaped(shape, dtype=WIDE):
    return jax.ShapeDtypeStruct(shape, dtype)


def swap_group(value):
    return lax.ppermute(value, "grp", [(0, 1), (1, 0)])


def run(body, outs, *operands, scratch=(), mib=16, order=0, apart=False):
    extra = {}
    if apart:
        extra = {"in_specs": [pl.BlockSpec(memory_space=pltpu.HBM)] * len(operands)}
        operands = [pltpu.with_memory_space_constraint(x, pltpu.HBM) for x in operands]
    return pl.pallas_call(
        body,
        out_shape=outs,
        **extra,
        scratch_shapes=scratch,
        compiler_params=pltpu.CompilerParams(vmem_limit_bytes=mib * 2**20),
        cost_estimate=pl.CostEstimate(flops=order * 10**9, bytes_accessed=0, transcendentals=0),
    )(*operands)


def place():
    me = lax.axis_index("row")
    return me, lax.rem(me, 2), lax.rem(lax.div(me, 2), 2)


def dot(left, right, dims):
    return lax.dot_general(left, right, (dims, ((), ())), preferred_element_type=WIDE)


def split_body(*refs):
    inw_hbm, outw_hbm, in_bias_hbm = refs[:3]
    own, core, outer, branch, bias_part = refs[9:14]
    inw, outw, in_bias, sems = refs[20:]
    feats, cotan, scale = refs[14:17]
    pairs = list(zip(refs[3:9], refs[14:20]))
    pairs += [(inw_hbm, inw), (outw_hbm, outw), (in_bias_hbm, in_bias)]
    copies = [pltpu.make_async_copy(a, b, sems.at[k]) for k, (a, b) in enumerate(pairs)]
    for copy in copies[6:] + copies[:6]:
        copy.start()
    me, c, x = place()
    even = c == 0
    quarter = own.shape[-1]
    rows, cols, channels = feats.shape
    own_rows = inw.shape[0]
    copies[6].wait()
    copies[7].wait()
    for side in range(2):
        for part, near in ((2 * jnp.bitwise_xor(x, side) + c, True), (2 * jnp.bitwise_xor(x, side) + 1 - c, False)):
            lanes = pl.ds(pl.multiple_of(part * quarter, quarter), quarter)
            for which, source in enumerate((inw, outw)):
                value = source[:, lanes].astype(NARROW)
                if near:
                    own[side, which] = value
                else:
                    core[pl.ds((2 * side + which) * own_rows, own_rows), :] = value
    copies[0].wait()
    first = feats[:RIM].astype(NARROW).reshape(RIM * cols, channels)
    last = feats[rows - RIM :].astype(NARROW).reshape(RIM * cols, channels)
    core[4 * own_rows :, :] = jnp.where(even, last, first)
    outer[...] = jnp.where(even, first, last)
    copies[1].wait()
    copies[2].wait()
    branch[...] = (scale[...] * cotan[...].reshape(branch.shape)).astype(NARROW)
    copies[8].wait()
    lanes = pl.ds(pl.multiple_of(lax.rem(me, 4) * quarter, quarter), quarter)
    bias_part[...] = in_bias[:, lanes]
    for copy in copies[3:6]:
        copy.wait()


def join_body(mine, other, *targets):
    group = lax.axis_index("grp")
    for side in range(2):
        full, sent = targets[2 * side : 2 * side + 2]
        own_rows = mine.shape[2]
        for which in range(2):
            full[which, 0] = mine[side, which]
            full[which, 1] = other[pl.ds((2 * side + which) * own_rows, own_rows), :]
        sent[...] = full[group]


def acts_body(mine, got, *refs):
    acts = refs[-1]
    pixels = mine.shape[1]
    acts[:, :pixels] = mine[...]
    acts[:, pixels:] = got[...]


def stack_body(*refs):
    for place_in, ref in enumerate(refs[:-1]):
        refs[-1][place_in] = ref[...]


def fill(padded, block, inner, outer):
    rows, cols, channels = block.shape
    _, c, _ = place()
    padded[:, :EDGE, :] = jnp.zeros_like(padded[:, :EDGE, :])
    padded[:, EDGE + cols :, :] = jnp.zeros_like(padded[:, EDGE + cols :, :])
    middle = slice(EDGE, EDGE + cols)
    inner = inner.astype(WIDE).reshape(RIM, cols, channels)
    outer = outer.astype(WIDE).reshape(RIM, cols, channels)
    padded[:RIM, middle, :] = jnp.where(c == 0, outer, inner)
    padded[RIM : RIM + rows, middle, :] = block
    padded[RIM + rows :, middle, :] = jnp.where(c == 0, inner, outer)


def taps_sum(padded, kernel, lanes, rows, cols, mirrored, start):
    total = list(start)
    for tap_col in range(TAPS):
        for row in range(rows + TAPS - 1):
            line = padded[row, pl.ds(EDGE - RIM + tap_col, cols), lanes]
            for out in range(rows):
                tap_row = row - out
                if 0 <= tap_row < TAPS:
                    if mirrored:
                        tap = kernel[TAPS - 1 - tap_row, pl.ds(TAPS - 1 - tap_col, 1), lanes]
                    else:
                        tap = kernel[tap_row, pl.ds(tap_col, 1), lanes]
                    total[out] = total[out] + line * tap
    return total


def conv_body(
    feats, core_got, outer, kernel, gain, bias, branch, normed, inv, acts, padded, result
):
    rows, cols, channels = feats.shape
    start = core_got.shape[0] - RIM * cols
    fill(padded, feats[...], core_got[start:, :], outer[...])

    @pl.loop(0, channels // LANES)
    def _(step):
        lanes = pl.ds(pl.multiple_of(step * LANES, LANES), LANES)
        zero = [jnp.zeros((cols, LANES), WIDE)] * rows
        total = taps_sum(padded, kernel, lanes, rows, cols, False, zero)
        for row in range(rows):
            result[pl.ds(row * cols, cols), lanes] = total[row]

    value = result[...]
    centred = value - jnp.mean(value, axis=1, keepdims=True)
    spread = lax.rsqrt(jnp.mean(centred * centred, axis=1, keepdims=True) + 1e-06)
    value = centred * spread
    normed[...] = value
    inv[...] = jnp.broadcast_to(spread, inv.shape)
    acts[0] = (value * gain[...] + bias[...]).astype(NARROW)
    acts[1] = branch[...]


def hidden_body(copied, *refs):
    patterns = lax.axis_size("row") // 4
    me, _, _ = place()
    acts, in_bias = refs[:2], refs[2]
    scale = refs[3]
    pieces = refs[4:-7]
    keep, send, active, hidden, scale_part, bias_part, weights = refs[-7:]
    half = acts[0].shape[1]
    if copied:
        own = pieces[0].shape[2]
        group = lax.axis_index("grp")
        for side in range(2):
            full, near, here, there = pieces[4 * side : 4 * side + 4]
            for pattern in range(patterns):
                for c in range(2):
                    device = jnp.bitwise_xor(me, 4 * pattern + 2 * side + c)
                    rows = pl.ds(pl.multiple_of(device * own, own), own)
                    if pattern < 2:
                        source = near if pattern else full
                        weights[0, rows, :] = source[0, c]
                        weights[1, rows, :] = source[1, c]
                    else:
                        weights[group, rows, :] = here[pattern - 2, c]
                        weights[1 - group, rows, :] = there[pattern - 2, c]
    else:
        weights[...] = pieces[0][...]
    in_narrow = weights.at[0]
    out_narrow = weights.at[1]
    bias_row = in_bias[...]
    total = jnp.zeros_like(bias_row)
    scale_total = jnp.zeros_like(scale_part)
    for side in (1, 0):
        preact = dot(acts[side][0], in_narrow[...], ((1,), (0,))) + bias_row
        act_grad = dot(acts[side][1], out_narrow[...], ((1,), (0,)))
        cdf = 0.5 * (1.0 + lax.erf(preact * 0.7071067811865476))
        rows = pl.ds(side * half, half)
        activated = (preact * cdf).astype(NARROW)
        active[rows, :] = activated
        slope = cdf + preact * jnp.exp(-0.5 * preact * preact) * 0.3989422804014327
        grad = act_grad * slope
        total = total + jnp.sum(grad, axis=0, keepdims=True)
        narrow = grad.astype(NARROW)
        hidden[rows, :] = narrow
        out_grad = dot(narrow, in_narrow[...], ((1,), (1,)))
        mixed = dot(activated, out_narrow[...], ((1,), (1,)))
        scale_total = scale_total + jnp.sum(
            mixed * acts[side][1].astype(WIDE), axis=0, keepdims=True
        )
        if side:
            send[0] = out_grad.astype(NARROW)
            send[1] = mixed.astype(NARROW)
        else:
            keep[0] = out_grad
            keep[1] = mixed
    bias_part[...] = total
    scale_part[...] = scale_total / scale[...]


def weight_body(norm_scale, *refs):
    acts, (active, hidden, holder) = refs[:2], refs[2:]
    half = acts[0].shape[1]
    first, second = pl.ds(0, half), pl.ds(half, half)
    for which, right in enumerate((hidden, active)):
        grad = dot(acts[0][which], right[first, :], ((0,), (0,)))
        grad = grad + dot(acts[1][which], right[second, :], ((0,), (0,)))
        holder[which] = norm_scale * grad


def owners_body(turns, holder, after, *targets):
    me, _, _ = place()
    own = holder.shape[1] // lax.axis_size("row")
    for pattern, target in zip(turns, targets):
        for c in range(2):
            device = jnp.bitwise_xor(me, 2 * pattern + c)
            rows = pl.ds(pl.multiple_of(device * own, own), own)
            for which in range(2):
                start = (2 * c + which) * own
                target[start : start + own, :] = holder[which, rows, :].astype(target.dtype)
        if target.shape[0] > 4 * own:
            target[4 * own : 4 * own + SMALL_ROWS, :] = after[...].astype(target.dtype)
            rest = target.shape[0] - 4 * own - SMALL_ROWS
            target[4 * own + SMALL_ROWS :, :] = jnp.zeros((rest, target.shape[1]), target.dtype)


def fold_body(kept, got, stay, leave, mixed_stay, mixed_leave):
    size = stay.shape[0]
    for which, (near, away) in enumerate(((stay, leave), (mixed_stay, mixed_leave))):
        near[...] = kept[which, :size] + got[which, :size].astype(WIDE)
        away[...] = (kept[which, size:] + got[which, size:].astype(WIDE)).astype(NARROW)


def conv_grad_body(norm_scale, *refs):
    kept, got, normed, inv, gain, feats, core_got, outer, scale, in_bias = refs[:10]
    grad, inner_out, rim_out, stay, leave, padded, small = refs[10:]
    rows, cols, channels = feats.shape
    me, c, _ = place()
    out_grad = kept[...] + got[...].astype(WIDE)
    value = normed[...]
    normed_grad = out_grad * gain[...]
    mean = jnp.mean(normed_grad, axis=1, keepdims=True)
    along = jnp.mean(normed_grad * value, axis=1, keepdims=True)
    result = inv[:, :1] * (normed_grad - mean - value * along)
    grad[...] = result
    pixels = rows * cols
    rim = RIM * cols
    rim_out[...] = jnp.where(c == 0, result[:rim], result[pixels - rim :]).astype(NARROW)
    inner_out[...] = jnp.where(c == 0, result[pixels - rim :], result[:rim]).astype(NARROW)
    fill(padded, feats[...], core_got[core_got.shape[0] - rim :, :], outer[...])

    def put(row, lanes, total):
        small[row // SMALL_ROWS, pl.ds(row % SMALL_ROWS, 1), lanes] = norm_scale * total

    @pl.loop(0, channels // LANES)
    def _(step):
        lanes = pl.ds(pl.multiple_of(step * LANES, LANES), LANES)
        own = [grad[pl.ds(row * cols, cols), lanes] for row in range(rows)]
        for tap_col in range(TAPS):
            totals = [jnp.zeros((8, LANES), WIDE)] * TAPS
            for row in range(rows + TAPS - 1):
                line = padded[row, pl.ds(EDGE - RIM + tap_col, cols), lanes]
                for out in range(rows):
                    tap_row = row - out
                    if 0 <= tap_row < TAPS:
                        product = line * own[out]
                        for part in range(cols // 8):
                            totals[tap_row] = totals[tap_row] + product[8 * part : 8 * part + 8]
            for tap_row in range(TAPS):
                total = jnp.sum(totals[tap_row], axis=0, keepdims=True)
                put(TAPS * tap_row + tap_col, lanes, total)

    everything = slice(None)
    row = TAPS * TAPS
    put(row, everything, jnp.sum(out_grad * value, axis=0, keepdims=True))
    put(row + 1, everything, jnp.sum(out_grad, axis=0, keepdims=True))
    put(row + 2, everything, scale[...])
    for part in range(4):
        own_part = jnp.where(lax.rem(me, 4) == part, 1.0, 0.0)
        put(row + 3 + part, everything, own_part * in_bias[...])
    stay[...] = small[c]
    leave[...] = small[1 - c]


def input_grad_body(grad, inner, outer, kernel, cotan, result, padded):
    rows, cols, channels = cotan.shape
    fill(padded, grad[...].reshape(cotan.shape), inner[...], outer[...])

    @pl.loop(0, channels // LANES)
    def _(step):
        lanes = pl.ds(pl.multiple_of(step * LANES, LANES), LANES)
        start = [cotan[row, :, lanes] for row in range(rows)]
        total = taps_sum(padded, kernel, lanes, rows, cols, True, start)
        for row in range(rows):
            result[row, :, lanes] = total[row]


def output_body(feats, scale, kept, got, result):
    mixed = kept[...] + got[...].astype(WIDE)
    result[...] = feats[...] + (scale[...] * mixed).reshape(feats.shape)


def total_body(turns, *refs):
    parts, sums = refs[: len(turns)], refs[len(turns) : -3]
    stay, leave, half = refs[-3:]
    own = stay.shape[2]
    for side in range(2):
        total = jnp.zeros(parts[0].shape, WIDE)
        for part, turn in zip(parts, turns):
            if turn % 2 == side:
                total = total + part[...].astype(WIDE)
        for which in range(2):
            stay[side, which] = total[which * own : (which + 1) * own]
        leave[2 * side * own : 2 * (side + 1) * own, :] = total[2 * own :]
    total = sums[0][...]
    for one in sums[1:]:
        total = total + one[...].astype(WIDE)
    half[...] = total
    leave[4 * own :, :] = total


def final_body(stay, got, half, *refs):
    in_grad, out_grad, kernel_grad, gain, bias, scale, in_bias, held = refs
    _, c, x = place()
    quarter = stay.shape[-1]
    own = stay.shape[2]
    for side in range(2):
        part = 2 * jnp.bitwise_xor(x, side)
        near = pl.ds(pl.multiple_of((part + c) * quarter, quarter), quarter)
        far = pl.ds(pl.multiple_of((part + 1 - c) * quarter, quarter), quarter)
        for which, target in enumerate((in_grad, out_grad)):
            start = (2 * side + which) * own
            target[:, near] = stay[side, which]
            target[:, far] = got[start : start + own, :]
    held[c] = half[...]
    held[1 - c] = got[4 * own :, :]

    def take(row):
        return held[row // SMALL_ROWS, pl.ds(row % SMALL_ROWS, 1), :]

    for tap_row in range(TAPS):
        for tap_col in range(TAPS):
            kernel_grad[tap_row, pl.ds(tap_col, 1), :] = take(TAPS * tap_row + tap_col)
    row = TAPS * TAPS
    gain[...] = take(row)
    bias[...] = take(row + 1)
    scale[...] = take(row + 2)
    for part in range(4):
        in_bias[:, pl.ds(part * quarter, quarter)] = take(row + 3 + part)


def flipped(blocks, axis, bit_set):
    return jnp.where(bit_set == 1, jnp.flip(blocks, axis), blocks)


def canonical(blocks, me, bit_count):
    tail = blocks.shape[1:]
    blocks = blocks.reshape((2,) * bit_count + tail)
    for spot in range(bit_count):
        blocks = flipped(blocks, bit_count - 1 - spot, (me >> spot) & 1)
    return blocks.reshape((2**bit_count,) + tail)


def per_device(
    features, cotangent, kernel, norm_gain, norm_bias, in_weight, in_bias, out_weight, layer_scale
):
    row_count, col_count, channels = features.shape
    own_rows, hidden_count = in_weight.shape
    pixels = row_count * col_count
    count = lax.axis_size("row")
    bit_count = count.bit_length() - 1
    me = lax.axis_index("row")
    group_index = lax.axis_index("grp")
    quarter = hidden_count // 4
    norm_scale = 1.0 / math.sqrt(pixels * count)
    patterns = count // 4
    copied = own_rows % 16 == 0
    gain_row = norm_gain.reshape(1, channels)
    bias_row = norm_bias.reshape(1, channels)
    scale_row = layer_scale.reshape(1, channels)
    rim = RIM * col_count
    padded = pltpu.VMEM((row_count + 2 * RIM, col_count + 2 * EDGE, channels), WIDE)

    piece = (2, own_rows, quarter)
    once = (features, cotangent, scale_row, kernel, gain_row, bias_row)
    own, core, outer, branch, in_bias_own, feats, cotan, scale, taps, gain, bias = run(
        split_body,
        (
            shaped((2,) + piece, NARROW),
            shaped((4 * own_rows + rim, channels), NARROW),
            shaped((rim, channels), NARROW),
            shaped((pixels, channels), NARROW),
            shaped((1, quarter)),
        )
        + tuple(shaped(x.shape) for x in once),
        in_weight,
        out_weight,
        in_bias.reshape(1, hidden_count),
        *once,
        scratch=(
            pltpu.VMEM(in_weight.shape, WIDE),
            pltpu.VMEM(out_weight.shape, WIDE),
            pltpu.VMEM((1, hidden_count), WIDE),
            pltpu.SemaphoreType.DMA((9,)),
        ),
        apart=True,
    )
    core_got = swap(core, 1)
    outer_got = swap_rim(outer)
    full_shape = shaped((2, 2, own_rows, quarter), NARROW)
    joined = run(
        join_body,
        (full_shape, shaped(piece, NARROW)) * 2,
        own,
        core_got,
    )
    pieces = []
    for side in range(2):
        full, sent = joined[2 * side : 2 * side + 2]
        here = [swap(sent, 4 * p + 2 * side) for p in range(2, patterns)]
        here = run(stack_body, (shaped((patterns - 2,) + piece, NARROW),), *here, order=8)[0]
        near = swap(full, 4 + 2 * side)
        pieces += [swap(full, 2) if side else full, near, here, swap_group(here)]

    normed, inv, acts = run(
        conv_body,
        (
            shaped((pixels, channels)),
            shaped((pixels, LANES)),
            shaped((2, pixels, channels), NARROW),
        ),
        feats,
        core_got,
        outer_got,
        taps,
        gain,
        bias,
        branch,
        scratch=(padded, pltpu.VMEM((pixels, channels), WIDE)),
    )
    first_blocks = [pieces[k] for k in (1, 4, 5, 7)]
    acts = run(
        acts_body,
        (shaped((2, 2 * pixels, channels), NARROW),),
        acts,
        swap(acts, 2),
        *first_blocks,
    )[0]
    acts_got = swap(acts, 1)

    if not copied:
        lines = []
        for pattern in range(patterns):
            for side in range(2):
                full, near, here, there = pieces[4 * side : 4 * side + 4]
                if pattern < 2:
                    lines.append(near if pattern else full)
                else:
                    pair = jnp.stack([here[pattern - 2], there[pattern - 2]])
                    lines.append(flipped(pair, 0, group_index))
        lines = jnp.moveaxis(jnp.stack(lines), 1, 2).reshape(count, 2, own_rows, quarter)
        lines = jnp.moveaxis(canonical(lines, me, bit_count), 1, 0)
        pieces = [lines.reshape(2, channels, quarter)]
    group = 4 * pixels
    both = (2, 2 * pixels, channels)
    keep, send, active, hidden, scale_part, in_bias_part = run(
        functools.partial(hidden_body, copied),
        (
            shaped(both),
            shaped(both, NARROW),
            shaped((group, quarter), NARROW),
            shaped((group, quarter), NARROW),
            shaped((1, channels)),
            shaped((1, quarter)),
        ),
        acts,
        acts_got,
        in_bias_own,
        scale,
        *pieces,
        scratch=(pltpu.VMEM((2, channels, quarter), NARROW),),
        mib=24,
    )
    half = (shaped((pixels, channels)), shaped((pixels, channels), NARROW))
    out_stay, out_leave, mixed_stay, mixed_leave = run(fold_body, half * 2, keep, swap(send, 1))
    out_got = swap(out_leave, 2)

    holder = run(
        functools.partial(weight_body, norm_scale),
        (shaped((2, channels, quarter)),),
        acts,
        acts_got,
        active,
        hidden,
        mib=24,
    )[0]
    conv_grad, inner_out, rim_out, stay, leave = run(
        functools.partial(conv_grad_body, norm_scale),
        (
            shaped((pixels, channels)),
            shaped((rim, channels), NARROW),
            shaped((rim, channels), NARROW),
            shaped((SMALL_ROWS, channels)),
            shaped((SMALL_ROWS, channels)),
        ),
        out_stay,
        out_got,
        normed,
        inv,
        gain,
        feats,
        core_got,
        outer_got,
        scale_part,
        in_bias_part,
        scratch=(padded, pltpu.VMEM((2, SMALL_ROWS, channels), WIDE)),
    )
    rim_got = swap_rim(rim_out)
    inner_got = swap(inner_out, 1)
    sums = stay + swap(leave, 1)

    far_turns = (*range(2 * patterns - 1, 4, -2), 3, 1)
    near_turns = (*range(4, 2 * patterns, 2), 2, 0)
    owned = 4 * own_rows
    if copied:
        parts = run(
            functools.partial(owners_body, far_turns),
            (shaped((owned, quarter), NARROW),) * len(far_turns),
            holder,
            out_leave,
        )
    else:
        flat = holder.reshape(2, count, own_rows, quarter)
        flat = canonical(jnp.moveaxis(flat, 1, 0), me, bit_count)
        flat = flat.reshape(2 * patterns, owned, quarter)
        parts = [flat[p].astype(NARROW) for p in far_turns]
    far_parts = [swap(part, 2 * p) for p, part in zip(far_turns, parts)]
    sums, far_parts = lax.optimization_barrier((sums, far_parts))
    sums = sums + swap(sums, 2)
    if copied:
        joint = shaped((owned + 32, quarter), NARROW)
        *parts, near_own = run(
            functools.partial(owners_body, near_turns),
            (joint,) * (len(near_turns) - 1) + (shaped((owned, quarter)),),
            holder,
            sums,
        )
        parts = [swap(part, 2 * p) for p, part in zip(near_turns, parts)]
        sums_parts = [part[owned : owned + SMALL_ROWS] for part in parts]
        near_parts = [part[:owned] for part in parts] + [near_own]
    else:
        near_parts = [swap(flat[p].astype(NARROW), 2 * p) for p in near_turns[:-1]] + [flat[0]]
        sums_parts = [swap(sums.astype(NARROW), 2 * p) for p in near_turns[:-1]]

    input_grad = run(
        input_grad_body,
        (shaped(features.shape),),
        conv_grad,
        inner_got,
        rim_got,
        taps,
        cotan,
        scratch=(padded,),
    )[0]
    output = run(
        output_body,
        (shaped(features.shape),),
        feats,
        scale,
        mixed_stay,
        swap(mixed_leave, 2),
    )[0]
    parts = list(far_parts) + near_parts
    parts, input_grad, output = lax.optimization_barrier((parts, input_grad, output))

    stay, leave, half_sums = run(
        functools.partial(total_body, far_turns + near_turns),
        (
            shaped((2, 2, own_rows, quarter)),
            shaped((owned + SMALL_ROWS, quarter)),
            shaped((SMALL_ROWS, channels)),
        ),
        *parts,
        sums,
        *sums_parts,
    )
    (
        in_weight_grad,
        out_weight_grad,
        kernel_grad,
        gain_grad,
        bias_grad,
        scale_grad,
        in_bias_grad,
    ) = run(
        final_body,
        (
            shaped((own_rows, hidden_count)),
            shaped((own_rows, hidden_count)),
            shaped(kernel.shape),
            shaped((1, channels)),
            shaped((1, channels)),
            shaped((1, channels)),
            shaped((1, hidden_count)),
        ),
        stay,
        swap(leave, 1),
        half_sums,
        scratch=(pltpu.VMEM((2, SMALL_ROWS, channels), WIDE),),
    )
    return (
        output,
        input_grad,
        in_weight_grad,
        out_weight_grad,
        kernel_grad,
        gain_grad.reshape(channels),
        bias_grad.reshape(channels),
        in_bias_grad.reshape(hidden_count),
        scale_grad.reshape(channels),
    )


def solution(mesh):
    return jax.shard_map(
        per_device,
        mesh=mesh,
        in_specs=(
            P(("grp", "row"), None, None),
            P(("grp", "row"), None, None),
            P(),
            P(),
            P(),
            P("row", None),
            P(),
            P("row", None),
            P(),
        ),
        out_specs=(
            P(("grp", "row"), None, None),
            P(("grp", "row"), None, None),
            P(("grp", "row"), None),
            P(("grp", "row"), None),
            P("grp", None, None),
            P("grp"),
            P("grp"),
            P("grp"),
            P("grp"),
        ),
        check_vma=False,
    )
```

```python
import functools
import math

import jax
import jax.numpy as jnp
from jax import lax
from jax.experimental import pallas as pl
from jax.experimental.pallas import tpu as pltpu
from jax.sharding import PartitionSpec as P

NARROW = jnp.bfloat16
WIDE = jnp.float32
TAPS = 7
RIM = 3
EDGE = 8
LANES = 128
SMALL_ROWS = 28


def swap(value, bit):
    count = lax.axis_size("row")
    return lax.ppermute(value, "row", [(i, i ^ bit) for i in range(count)])


def swap_rim(value):
    count = lax.axis_size("row")
    pairs = [(i, i + 1) for i in range(1, count - 1, 2)]
    return lax.ppermute(value, "row", pairs + [(j, i) for i, j in pairs])


def shaped(shape, dtype=WIDE):
    return jax.ShapeDtypeStruct(shape, dtype)


def swap_group(value):
    return lax.ppermute(value, "grp", [(0, 1), (1, 0)])


def run(body, outs, *operands, scratch=(), mib=16, order=0, apart=False):
    extra = {}
    if apart:
        extra = {"in_specs": [pl.BlockSpec(memory_space=pltpu.HBM)] * len(operands)}
        operands = [pltpu.with_memory_space_constraint(x, pltpu.HBM) for x in operands]
    return pl.pallas_call(
        body,
        out_shape=outs,
        **extra,
        scratch_shapes=scratch,
        compiler_params=pltpu.CompilerParams(vmem_limit_bytes=mib * 2**20),
        cost_estimate=pl.CostEstimate(flops=order * 10**9, bytes_accessed=0, transcendentals=0),
    )(*operands)


def place():
    me = lax.axis_index("row")
    return me, lax.rem(me, 2), lax.rem(lax.div(me, 2), 2)


def dot(left, right, dims):
    return lax.dot_general(left, right, (dims, ((), ())), preferred_element_type=WIDE)


def split_body(*refs):
    inw_hbm, outw_hbm, in_bias_hbm = refs[:3]
    own, core, outer, branch, bias_part = refs[9:14]
    inw, outw, in_bias, sems = refs[20:]
    feats, cotan, scale = refs[14:17]
    pairs = list(zip(refs[3:9], refs[14:20]))
    pairs += [(inw_hbm, inw), (outw_hbm, outw), (in_bias_hbm, in_bias)]
    copies = [pltpu.make_async_copy(a, b, sems.at[k]) for k, (a, b) in enumerate(pairs)]
    for copy in copies[6:] + copies[:6]:
        copy.start()
    me, c, x = place()
    even = c == 0
    quarter = own.shape[-1]
    rows, cols, channels = feats.shape
    own_rows = inw.shape[0]
    copies[6].wait()
    copies[7].wait()
    for side in range(2):
        for part, near in ((2 * jnp.bitwise_xor(x, side) + c, True), (2 * jnp.bitwise_xor(x, side) + 1 - c, False)):
            lanes = pl.ds(pl.multiple_of(part * quarter, quarter), quarter)
            for which, source in enumerate((inw, outw)):
                value = source[:, lanes].astype(NARROW)
                if near:
                    own[side, which] = value
                else:
                    core[pl.ds((2 * side + which) * own_rows, own_rows), :] = value
    copies[0].wait()
    first = feats[:RIM].astype(NARROW).reshape(RIM * cols, channels)
    last = feats[rows - RIM :].astype(NARROW).reshape(RIM * cols, channels)
    core[4 * own_rows :, :] = jnp.where(even, last, first)
    outer[...] = jnp.where(even, first, last)
    copies[1].wait()
    copies[2].wait()
    branch[...] = (scale[...] * cotan[...].reshape(branch.shape)).astype(NARROW)
    copies[8].wait()
    lanes = pl.ds(pl.multiple_of(lax.rem(me, 4) * quarter, quarter), quarter)
    bias_part[...] = in_bias[:, lanes]
    for copy in copies[3:6]:
        copy.wait()


def join_body(mine, other, *targets):
    group = lax.axis_index("grp")
    for side in range(2):
        full, sent = targets[2 * side : 2 * side + 2]
        own_rows = mine.shape[2]
        for which in range(2):
            full[which, 0] = mine[side, which]
            full[which, 1] = other[pl.ds((2 * side + which) * own_rows, own_rows), :]
        sent[...] = full[group]


def acts_body(mine, got, *refs):
    acts, full = refs[-2:]
    pixels = acts.shape[1] // 2
    for which in range(2):
        rows = slice(which * pixels, (which + 1) * pixels)
        acts[which, :pixels] = mine[rows, :]
        acts[which, pixels:] = got[rows, :]
        own = full.shape[2]
        for core in range(2):
            start = 2 * pixels + (2 * which + core) * own
            full[which, core] = got[start : start + own, :]


def stack_body(*refs):
    for place_in, ref in enumerate(refs[:-1]):
        refs[-1][place_in] = ref[...]


def fill(padded, block, inner, outer):
    rows, cols, channels = block.shape
    _, c, _ = place()
    padded[:, :EDGE, :] = jnp.zeros_like(padded[:, :EDGE, :])
    padded[:, EDGE + cols :, :] = jnp.zeros_like(padded[:, EDGE + cols :, :])
    middle = slice(EDGE, EDGE + cols)
    inner = inner.astype(WIDE).reshape(RIM, cols, channels)
    outer = outer.astype(WIDE).reshape(RIM, cols, channels)
    padded[:RIM, middle, :] = jnp.where(c == 0, outer, inner)
    padded[RIM : RIM + rows, middle, :] = block
    padded[RIM + rows :, middle, :] = jnp.where(c == 0, inner, outer)


def taps_sum(padded, kernel, lanes, rows, cols, mirrored, start):
    total = list(start)
    for tap_col in range(TAPS):
        for row in range(rows + TAPS - 1):
            line = padded[row, pl.ds(EDGE - RIM + tap_col, cols), lanes]
            for out in range(rows):
                tap_row = row - out
                if 0 <= tap_row < TAPS:
                    if mirrored:
                        tap = kernel[TAPS - 1 - tap_row, pl.ds(TAPS - 1 - tap_col, 1), lanes]
                    else:
                        tap = kernel[tap_row, pl.ds(tap_col, 1), lanes]
                    total[out] = total[out] + line * tap
    return total


def conv_body(
    feats, core_got, outer, kernel, gain, bias, branch, full, normed, inv, acts, padded, result
):
    rows, cols, channels = feats.shape
    start = core_got.shape[0] - RIM * cols
    fill(padded, feats[...], core_got[start:, :], outer[...])

    @pl.loop(0, channels // LANES)
    def _(step):
        lanes = pl.ds(pl.multiple_of(step * LANES, LANES), LANES)
        zero = [jnp.zeros((cols, LANES), WIDE)] * rows
        total = taps_sum(padded, kernel, lanes, rows, cols, False, zero)
        for row in range(rows):
            result[pl.ds(row * cols, cols), lanes] = total[row]

    value = result[...]
    centred = value - jnp.mean(value, axis=1, keepdims=True)
    spread = lax.rsqrt(jnp.mean(centred * centred, axis=1, keepdims=True) + 1e-06)
    value = centred * spread
    normed[...] = value
    inv[...] = jnp.broadcast_to(spread, inv.shape)
    pixels = rows * cols
    acts[:pixels, :] = (value * gain[...] + bias[...]).astype(NARROW)
    acts[pixels : 2 * pixels, :] = branch[...]
    own = full.shape[2]
    for which in range(2):
        for core in range(2):
            start = 2 * pixels + (2 * which + core) * own
            acts[start : start + own, :] = full[which, core]


def hidden_body(copied, *refs):
    patterns = lax.axis_size("row") // 4
    me, _, _ = place()
    acts, in_bias = refs[:2], refs[2]
    scale = refs[3]
    pieces = refs[4:-7]
    keep, send, active, hidden, scale_part, bias_part, weights = refs[-7:]
    half = acts[0].shape[1]
    if copied:
        own = pieces[0].shape[2]
        group = lax.axis_index("grp")
        for side in range(2):
            full, near, here, there = pieces[4 * side : 4 * side + 4]
            for pattern in range(patterns):
                for c in range(2):
                    device = jnp.bitwise_xor(me, 4 * pattern + 2 * side + c)
                    rows = pl.ds(pl.multiple_of(device * own, own), own)
                    if pattern < 2:
                        source = near if pattern else full
                        weights[0, rows, :] = source[0, c]
                        weights[1, rows, :] = source[1, c]
                    else:
                        weights[group, rows, :] = here[pattern - 2, c]
                        weights[1 - group, rows, :] = there[pattern - 2, c]
    else:
        weights[...] = pieces[0][...]
    in_narrow = weights.at[0]
    out_narrow = weights.at[1]
    bias_row = in_bias[...]
    total = jnp.zeros_like(bias_row)
    scale_total = jnp.zeros_like(scale_part)
    for side in (1, 0):
        preact = dot(acts[side][0], in_narrow[...], ((1,), (0,))) + bias_row
        act_grad = dot(acts[side][1], out_narrow[...], ((1,), (0,)))
        cdf = 0.5 * (1.0 + lax.erf(preact * 0.7071067811865476))
        rows = pl.ds(side * half, half)
        activated = (preact * cdf).astype(NARROW)
        active[rows, :] = activated
        slope = cdf + preact * jnp.exp(-0.5 * preact * preact) * 0.3989422804014327
        grad = act_grad * slope
        total = total + jnp.sum(grad, axis=0, keepdims=True)
        narrow = grad.astype(NARROW)
        hidden[rows, :] = narrow
        out_grad = dot(narrow, in_narrow[...], ((1,), (1,)))
        mixed = dot(activated, out_narrow[...], ((1,), (1,)))
        scale_total = scale_total + jnp.sum(
            mixed * acts[side][1].astype(WIDE), axis=0, keepdims=True
        )
        if side:
            send[0] = out_grad.astype(NARROW)
            send[1] = mixed.astype(NARROW)
        else:
            keep[0] = out_grad
            keep[1] = mixed
    bias_part[...] = total
    scale_part[...] = scale_total / scale[...]


def weight_body(norm_scale, *refs):
    acts, (active, hidden, holder) = refs[:2], refs[2:]
    half = acts[0].shape[1]
    first, second = pl.ds(0, half), pl.ds(half, half)
    for which, right in enumerate((hidden, active)):
        grad = dot(acts[0][which], right[first, :], ((0,), (0,)))
        grad = grad + dot(acts[1][which], right[second, :], ((0,), (0,)))
        holder[which] = norm_scale * grad


def owners_body(turns, holder, after, *targets):
    me, _, _ = place()
    own = holder.shape[1] // lax.axis_size("row")
    for pattern, target in zip(turns, targets):
        for c in range(2):
            device = jnp.bitwise_xor(me, 2 * pattern + c)
            rows = pl.ds(pl.multiple_of(device * own, own), own)
            for which in range(2):
                start = (2 * c + which) * own
                target[start : start + own, :] = holder[which, rows, :].astype(target.dtype)
        if target.shape[0] > 4 * own:
            target[4 * own : 4 * own + SMALL_ROWS, :] = after[...].astype(target.dtype)
            rest = target.shape[0] - 4 * own - SMALL_ROWS
            target[4 * own + SMALL_ROWS :, :] = jnp.zeros((rest, target.shape[1]), target.dtype)


def fold_body(kept, got, stay, leave, mixed_stay, mixed_leave):
    size = stay.shape[0]
    for which, (near, away) in enumerate(((stay, leave), (mixed_stay, mixed_leave))):
        near[...] = kept[which, :size] + got[which, :size].astype(WIDE)
        away[...] = (kept[which, size:] + got[which, size:].astype(WIDE)).astype(NARROW)


def conv_grad_body(norm_scale, *refs):
    kept, got, normed, inv, gain, feats, core_got, outer, scale, in_bias = refs[:10]
    grad, inner_out, rim_out, stay, leave, padded, small = refs[10:]
    rows, cols, channels = feats.shape
    me, c, _ = place()
    out_grad = kept[...] + got[...].astype(WIDE)
    value = normed[...]
    normed_grad = out_grad * gain[...]
    mean = jnp.mean(normed_grad, axis=1, keepdims=True)
    along = jnp.mean(normed_grad * value, axis=1, keepdims=True)
    result = inv[:, :1] * (normed_grad - mean - value * along)
    grad[...] = result
    pixels = rows * cols
    rim = RIM * cols
    rim_out[...] = jnp.where(c == 0, result[:rim], result[pixels - rim :]).astype(NARROW)
    inner_out[...] = jnp.where(c == 0, result[pixels - rim :], result[:rim]).astype(NARROW)
    fill(padded, feats[...], core_got[core_got.shape[0] - rim :, :], outer[...])

    def put(row, lanes, total):
        small[row // SMALL_ROWS, pl.ds(row % SMALL_ROWS, 1), lanes] = norm_scale * total

    @pl.loop(0, channels // LANES)
    def _(step):
        lanes = pl.ds(pl.multiple_of(step * LANES, LANES), LANES)
        own = [grad[pl.ds(row * cols, cols), lanes] for row in range(rows)]
        for tap_col in range(TAPS):
            totals = [jnp.zeros((8, LANES), WIDE)] * TAPS
            for row in range(rows + TAPS - 1):
                line = padded[row, pl.ds(EDGE - RIM + tap_col, cols), lanes]
                for out in range(rows):
                    tap_row = row - out
                    if 0 <= tap_row < TAPS:
                        product = line * own[out]
                        for part in range(cols // 8):
                            totals[tap_row] = totals[tap_row] + product[8 * part : 8 * part + 8]
            for tap_row in range(TAPS):
                total = jnp.sum(totals[tap_row], axis=0, keepdims=True)
                put(TAPS * tap_row + tap_col, lanes, total)

    everything = slice(None)
    row = TAPS * TAPS
    put(row, everything, jnp.sum(out_grad * value, axis=0, keepdims=True))
    put(row + 1, everything, jnp.sum(out_grad, axis=0, keepdims=True))
    put(row + 2, everything, scale[...])
    for part in range(4):
        own_part = jnp.where(lax.rem(me, 4) == part, 1.0, 0.0)
        put(row + 3 + part, everything, own_part * in_bias[...])
    stay[...] = small[c]
    leave[...] = small[1 - c]


def input_grad_body(grad, inner, outer, kernel, cotan, result, padded):
    rows, cols, channels = cotan.shape
    fill(padded, grad[...].reshape(cotan.shape), inner[...], outer[...])

    @pl.loop(0, channels // LANES)
    def _(step):
        lanes = pl.ds(pl.multiple_of(step * LANES, LANES), LANES)
        start = [cotan[row, :, lanes] for row in range(rows)]
        total = taps_sum(padded, kernel, lanes, rows, cols, True, start)
        for row in range(rows):
            result[row, :, lanes] = total[row]


def output_body(feats, scale, kept, got, result):
    mixed = kept[...] + got[...].astype(WIDE)
    result[...] = feats[...] + (scale[...] * mixed).reshape(feats.shape)


def total_body(turns, *refs):
    parts, sums = refs[: len(turns)], refs[len(turns) : -3]
    stay, leave, half = refs[-3:]
    own = stay.shape[2]
    for side in range(2):
        total = jnp.zeros(parts[0].shape, WIDE)
        for part, turn in zip(parts, turns):
            if turn % 2 == side:
                total = total + part[...].astype(WIDE)
        for which in range(2):
            stay[side, which] = total[which * own : (which + 1) * own]
        leave[2 * side * own : 2 * (side + 1) * own, :] = total[2 * own :]
    total = sums[0][...]
    for one in sums[1:]:
        total = total + one[...].astype(WIDE)
    half[...] = total
    leave[4 * own :, :] = total


def final_body(stay, got, half, *refs):
    in_grad, out_grad, kernel_grad, gain, bias, scale, in_bias, held = refs
    _, c, x = place()
    quarter = stay.shape[-1]
    own = stay.shape[2]
    for side in range(2):
        part = 2 * jnp.bitwise_xor(x, side)
        near = pl.ds(pl.multiple_of((part + c) * quarter, quarter), quarter)
        far = pl.ds(pl.multiple_of((part + 1 - c) * quarter, quarter), quarter)
        for which, target in enumerate((in_grad, out_grad)):
            start = (2 * side + which) * own
            target[:, near] = stay[side, which]
            target[:, far] = got[start : start + own, :]
    held[c] = half[...]
    held[1 - c] = got[4 * own :, :]

    def take(row):
        return held[row // SMALL_ROWS, pl.ds(row % SMALL_ROWS, 1), :]

    for tap_row in range(TAPS):
        for tap_col in range(TAPS):
            kernel_grad[tap_row, pl.ds(tap_col, 1), :] = take(TAPS * tap_row + tap_col)
    row = TAPS * TAPS
    gain[...] = take(row)
    bias[...] = take(row + 1)
    scale[...] = take(row + 2)
    for part in range(4):
        in_bias[:, pl.ds(part * quarter, quarter)] = take(row + 3 + part)


def flipped(blocks, axis, bit_set):
    return jnp.where(bit_set == 1, jnp.flip(blocks, axis), blocks)


def canonical(blocks, me, bit_count):
    tail = blocks.shape[1:]
    blocks = blocks.reshape((2,) * bit_count + tail)
    for spot in range(bit_count):
        blocks = flipped(blocks, bit_count - 1 - spot, (me >> spot) & 1)
    return blocks.reshape((2**bit_count,) + tail)


def per_device(
    features, cotangent, kernel, norm_gain, norm_bias, in_weight, in_bias, out_weight, layer_scale
):
    row_count, col_count, channels = features.shape
    own_rows, hidden_count = in_weight.shape
    pixels = row_count * col_count
    count = lax.axis_size("row")
    bit_count = count.bit_length() - 1
    me = lax.axis_index("row")
    group_index = lax.axis_index("grp")
    quarter = hidden_count // 4
    norm_scale = 1.0 / math.sqrt(pixels * count)
    patterns = count // 4
    copied = own_rows % 16 == 0
    gain_row = norm_gain.reshape(1, channels)
    bias_row = norm_bias.reshape(1, channels)
    scale_row = layer_scale.reshape(1, channels)
    rim = RIM * col_count
    padded = pltpu.VMEM((row_count + 2 * RIM, col_count + 2 * EDGE, channels), WIDE)

    piece = (2, own_rows, quarter)
    once = (features, cotangent, scale_row, kernel, gain_row, bias_row)
    own, core, outer, branch, in_bias_own, feats, cotan, scale, taps, gain, bias = run(
        split_body,
        (
            shaped((2,) + piece, NARROW),
            shaped((4 * own_rows + rim, channels), NARROW),
            shaped((rim, channels), NARROW),
            shaped((pixels, channels), NARROW),
            shaped((1, quarter)),
        )
        + tuple(shaped(x.shape) for x in once),
        in_weight,
        out_weight,
        in_bias.reshape(1, hidden_count),
        *once,
        scratch=(
            pltpu.VMEM(in_weight.shape, WIDE),
            pltpu.VMEM(out_weight.shape, WIDE),
            pltpu.VMEM((1, hidden_count), WIDE),
            pltpu.SemaphoreType.DMA((9,)),
        ),
        apart=True,
    )
    core_got = swap(core, 1)
    outer_got = swap_rim(outer)
    full_shape = shaped((2, 2, own_rows, quarter), NARROW)
    joined = run(
        join_body,
        (full_shape, shaped(piece, NARROW)) * 2,
        own,
        core_got,
    )
    pieces = []
    for side in range(2):
        full, sent = joined[2 * side : 2 * side + 2]
        here = [swap(sent, 4 * p + 2 * side) for p in range(2, patterns)]
        here = run(stack_body, (shaped((patterns - 2,) + piece, NARROW),), *here, order=8)[0]
        near = swap(full, 4 + 2 * side)
        pieces += [full, near, here, swap_group(here)]

    normed, inv, sent = run(
        conv_body,
        (
            shaped((pixels, channels)),
            shaped((pixels, LANES)),
            shaped((2 * pixels + 4 * own_rows, channels), NARROW),
        ),
        feats,
        core_got,
        outer_got,
        taps,
        gain,
        bias,
        branch,
        joined[2],
        scratch=(padded, pltpu.VMEM((pixels, channels), WIDE)),
    )
    first_blocks = [pieces[k] for k in (1, 3, 5, 7)]
    acts, pieces[4] = run(
        acts_body,
        (shaped((2, 2 * pixels, channels), NARROW), full_shape),
        sent,
        swap(sent, 2),
        *first_blocks,
    )
    acts_got = swap(acts, 1)

    if not copied:
        lines = []
        for pattern in range(patterns):
            for side in range(2):
                full, near, here, there = pieces[4 * side : 4 * side + 4]
                if pattern < 2:
                    lines.append(near if pattern else full)
                else:
                    pair = jnp.stack([here[pattern - 2], there[pattern - 2]])
                    lines.append(flipped(pair, 0, group_index))
        lines = jnp.moveaxis(jnp.stack(lines), 1, 2).reshape(count, 2, own_rows, quarter)
        lines = jnp.moveaxis(canonical(lines, me, bit_count), 1, 0)
        pieces = [lines.reshape(2, channels, quarter)]
    group = 4 * pixels
    both = (2, 2 * pixels, channels)
    keep, send, active, hidden, scale_part, in_bias_part = run(
        functools.partial(hidden_body, copied),
        (
            shaped(both),
            shaped(both, NARROW),
            shaped((group, quarter), NARROW),
            shaped((group, quarter), NARROW),
            shaped((1, channels)),
            shaped((1, quarter)),
        ),
        acts,
        acts_got,
        in_bias_own,
        scale,
        *pieces,
        scratch=(pltpu.VMEM((2, channels, quarter), NARROW),),
        mib=24,
    )
    half = (shaped((pixels, channels)), shaped((pixels, channels), NARROW))
    out_stay, out_leave, mixed_stay, mixed_leave = run(fold_body, half * 2, keep, swap(send, 1))
    out_got = swap(out_leave, 2)

    holder = run(
        functools.partial(weight_body, norm_scale),
        (shaped((2, channels, quarter)),),
        acts,
        acts_got,
        active,
        hidden,
        mib=24,
    )[0]
    conv_grad, inner_out, rim_out, stay, leave = run(
        functools.partial(conv_grad_body, norm_scale),
        (
            shaped((pixels, channels)),
            shaped((rim, channels), NARROW),
            shaped((rim, channels), NARROW),
            shaped((SMALL_ROWS, channels)),
            shaped((SMALL_ROWS, channels)),
        ),
        out_stay,
        out_got,
        normed,
        inv,
        gain,
        feats,
        core_got,
        outer_got,
        scale_part,
        in_bias_part,
        scratch=(padded, pltpu.VMEM((2, SMALL_ROWS, channels), WIDE)),
    )
    rim_got = swap_rim(rim_out)
    inner_got = swap(inner_out, 1)
    sums = stay + swap(leave, 1)

    far_turns = (*range(2 * patterns - 1, 4, -2), 3)
    near_turns = (*range(4, 2 * patterns, 2), 2, 1, 0)
    owned = 4 * own_rows
    if copied:
        parts = run(
            functools.partial(owners_body, far_turns),
            (shaped((owned, quarter), NARROW),) * len(far_turns),
            holder,
            out_leave,
        )
    else:
        flat = holder.reshape(2, count, own_rows, quarter)
        flat = canonical(jnp.moveaxis(flat, 1, 0), me, bit_count)
        flat = flat.reshape(2 * patterns, owned, quarter)
        parts = [flat[p].astype(NARROW) for p in far_turns]
    far_parts = [swap(part, 2 * p) for p, part in zip(far_turns, parts)]
    sums, far_parts = lax.optimization_barrier((sums, far_parts))
    sums = sums + swap(sums, 2)
    sums, mixed_leave = lax.optimization_barrier((sums, mixed_leave))
    if copied:
        joint = shaped((owned + 32, quarter), NARROW)
        *parts, side_part, near_own = run(
            functools.partial(owners_body, near_turns),
            (joint,) * (len(near_turns) - 2)
            + (shaped((owned, quarter), NARROW), shaped((owned, quarter))),
            holder,
            sums,
        )
        parts = [swap(part, 2 * p) for p, part in zip(near_turns, parts)]
        sums_parts = [part[owned : owned + SMALL_ROWS] for part in parts]
        near_parts = [part[:owned] for part in parts] + [swap(side_part, 2), near_own]
    else:
        near_parts = [swap(flat[p].astype(NARROW), 2 * p) for p in near_turns[:-1]] + [flat[0]]
        sums_parts = [swap(sums.astype(NARROW), 2 * p) for p in near_turns[:-2]]

    input_grad = run(
        input_grad_body,
        (shaped(features.shape),),
        conv_grad,
        inner_got,
        rim_got,
        taps,
        cotan,
        scratch=(padded,),
    )[0]
    output = run(
        output_body,
        (shaped(features.shape),),
        feats,
        scale,
        mixed_stay,
        swap(mixed_leave, 2),
    )[0]
    parts = list(far_parts) + near_parts
    parts, input_grad, output = lax.optimization_barrier((parts, input_grad, output))

    stay, leave, half_sums = run(
        functools.partial(total_body, far_turns + near_turns),
        (
            shaped((2, 2, own_rows, quarter)),
            shaped((owned + SMALL_ROWS, quarter)),
            shaped((SMALL_ROWS, channels)),
        ),
        *parts,
        sums,
        *sums_parts,
    )
    (
        in_weight_grad,
        out_weight_grad,
        kernel_grad,
        gain_grad,
        bias_grad,
        scale_grad,
        in_bias_grad,
    ) = run(
        final_body,
        (
            shaped((own_rows, hidden_count)),
            shaped((own_rows, hidden_count)),
            shaped(kernel.shape),
            shaped((1, channels)),
            shaped((1, channels)),
            shaped((1, channels)),
            shaped((1, hidden_count)),
        ),
        stay,
        swap(leave, 1),
        half_sums,
        scratch=(pltpu.VMEM((2, SMALL_ROWS, channels), WIDE),),
    )
    return (
        output,
        input_grad,
        in_weight_grad,
        out_weight_grad,
        kernel_grad,
        gain_grad.reshape(channels),
        bias_grad.reshape(channels),
        in_bias_grad.reshape(hidden_count),
        scale_grad.reshape(channels),
    )


def solution(mesh):
    return jax.shard_map(
        per_device,
        mesh=mesh,
        in_specs=(
            P(("grp", "row"), None, None),
            P(("grp", "row"), None, None),
            P(),
            P(),
            P(),
            P("row", None),
            P(),
            P("row", None),
            P(),
        ),
        out_specs=(
            P(("grp", "row"), None, None),
            P(("grp", "row"), None, None),
            P(("grp", "row"), None),
            P(("grp", "row"), None),
            P("grp", None, None),
            P("grp"),
            P("grp"),
            P("grp"),
            P("grp"),
        ),
        check_vma=False,
    )
```

```python
import functools
import math

import jax
import jax.numpy as jnp
from jax import lax
from jax.experimental import pallas as pl
from jax.experimental.pallas import tpu as pltpu
from jax.sharding import PartitionSpec as P

NARROW = jnp.bfloat16
WIDE = jnp.float32
TAPS = 7
RIM = 3
EDGE = 8
LANES = 128
SMALL_ROWS = 28


def swap(value, bit):
    count = lax.axis_size("row")
    return lax.ppermute(value, "row", [(i, i ^ bit) for i in range(count)])


def swap_rim(value):
    count = lax.axis_size("row")
    pairs = [(i, i + 1) for i in range(1, count - 1, 2)]
    return lax.ppermute(value, "row", pairs + [(j, i) for i, j in pairs])


def shaped(shape, dtype=WIDE):
    return jax.ShapeDtypeStruct(shape, dtype)


def swap_far(value, pair, side):
    count = lax.axis_size("row")
    pairs = []
    for group in range(2):
        bits = 4 * (2 * pair + group) + 2 * side
        pairs += [(group * count + i, group * count + (i ^ bits)) for i in range(count)]
    return lax.ppermute(value, ("grp", "row"), pairs)


def swap_group(value):
    return lax.ppermute(value, "grp", [(0, 1), (1, 0)])


def run(body, outs, *operands, scratch=(), mib=16, order=0, apart=False):
    extra = {}
    if apart:
        extra = {"in_specs": [pl.BlockSpec(memory_space=pltpu.HBM)] * len(operands)}
        operands = [pltpu.with_memory_space_constraint(x, pltpu.HBM) for x in operands]
    return pl.pallas_call(
        body,
        out_shape=outs,
        **extra,
        scratch_shapes=scratch,
        compiler_params=pltpu.CompilerParams(vmem_limit_bytes=mib * 2**20),
        cost_estimate=pl.CostEstimate(flops=order * 10**9, bytes_accessed=0, transcendentals=0),
    )(*operands)


def place():
    me = lax.axis_index("row")
    return me, lax.rem(me, 2), lax.rem(lax.div(me, 2), 2)


def dot(left, right, dims):
    return lax.dot_general(left, right, (dims, ((), ())), preferred_element_type=WIDE)


def split_body(*refs):
    inw_hbm, outw_hbm, in_bias_hbm = refs[:3]
    own, core, outer, branch, bias_part = refs[9:14]
    inw, outw, in_bias, sems = refs[20:]
    feats, cotan, scale = refs[14:17]
    pairs = list(zip(refs[3:9], refs[14:20]))
    pairs += [(inw_hbm, inw), (outw_hbm, outw), (in_bias_hbm, in_bias)]
    copies = [pltpu.make_async_copy(a, b, sems.at[k]) for k, (a, b) in enumerate(pairs)]
    for copy in copies[6:] + copies[:6]:
        copy.start()
    me, c, x = place()
    even = c == 0
    quarter = own.shape[-1]
    rows, cols, channels = feats.shape
    own_rows = inw.shape[0]
    copies[6].wait()
    copies[7].wait()
    for side in range(2):
        for part, near in ((2 * jnp.bitwise_xor(x, side) + c, True), (2 * jnp.bitwise_xor(x, side) + 1 - c, False)):
            lanes = pl.ds(pl.multiple_of(part * quarter, quarter), quarter)
            for which, source in enumerate((inw, outw)):
                value = source[:, lanes].astype(NARROW)
                if near:
                    own[side, which] = value
                else:
                    core[pl.ds((2 * side + which) * own_rows, own_rows), :] = value
    copies[0].wait()
    first = feats[:RIM].astype(NARROW).reshape(RIM * cols, channels)
    last = feats[rows - RIM :].astype(NARROW).reshape(RIM * cols, channels)
    core[4 * own_rows :, :] = jnp.where(even, last, first)
    outer[...] = jnp.where(even, first, last)
    copies[1].wait()
    copies[2].wait()
    branch[...] = (scale[...] * cotan[...].reshape(branch.shape)).astype(NARROW)
    copies[8].wait()
    lanes = pl.ds(pl.multiple_of(lax.rem(me, 4) * quarter, quarter), quarter)
    bias_part[...] = in_bias[:, lanes]
    for copy in copies[3:6]:
        copy.wait()


def join_body(mine, other, branch, *targets):
    own = mine.shape[2]
    sent = targets[2]
    pixels = branch.shape[0]
    sent[:pixels, :] = branch[...]
    for side, full in enumerate(targets[:2]):
        for which in range(2):
            rows = pl.ds((2 * side + which) * own, own)
            full[which, 0] = mine[side, which]
            full[which, 1] = other[rows, :]
            if side:
                start = pixels + 2 * which * own
                sent[start : start + own, :] = mine[side, which]
                sent[start + own : start + 2 * own, :] = other[rows, :]


def acts_body(normed, branch, normed_got, sent_got, *refs):
    acts, full = refs[-2:]
    pixels = branch.shape[0]
    acts[0, :pixels] = normed[...]
    acts[0, pixels:] = normed_got[...]
    acts[1, :pixels] = branch[...]
    acts[1, pixels:] = sent_got[:pixels, :]
    own = full.shape[2]
    for which in range(2):
        for core in range(2):
            start = pixels + (2 * which + core) * own
            full[which, core] = sent_got[start : start + own, :]


def fill(padded, block, inner, outer):
    rows, cols, channels = block.shape
    _, c, _ = place()
    padded[:, :EDGE, :] = jnp.zeros_like(padded[:, :EDGE, :])
    padded[:, EDGE + cols :, :] = jnp.zeros_like(padded[:, EDGE + cols :, :])
    middle = slice(EDGE, EDGE + cols)
    inner = inner.astype(WIDE).reshape(RIM, cols, channels)
    outer = outer.astype(WIDE).reshape(RIM, cols, channels)
    padded[:RIM, middle, :] = jnp.where(c == 0, outer, inner)
    padded[RIM : RIM + rows, middle, :] = block
    padded[RIM + rows :, middle, :] = jnp.where(c == 0, inner, outer)


def taps_sum(padded, kernel, lanes, rows, cols, mirrored, start):
    total = list(start)
    for tap_col in range(TAPS):
        for row in range(rows + TAPS - 1):
            line = padded[row, pl.ds(EDGE - RIM + tap_col, cols), lanes]
            for out in range(rows):
                tap_row = row - out
                if 0 <= tap_row < TAPS:
                    if mirrored:
                        tap = kernel[TAPS - 1 - tap_row, pl.ds(TAPS - 1 - tap_col, 1), lanes]
                    else:
                        tap = kernel[tap_row, pl.ds(tap_col, 1), lanes]
                    total[out] = total[out] + line * tap
    return total


def conv_body(
    feats, core_got, outer, kernel, gain, bias, normed, inv, narrow, padded, result
):
    rows, cols, channels = feats.shape
    start = core_got.shape[0] - RIM * cols
    fill(padded, feats[...], core_got[start:, :], outer[...])

    @pl.loop(0, channels // LANES)
    def _(step):
        lanes = pl.ds(pl.multiple_of(step * LANES, LANES), LANES)
        zero = [jnp.zeros((cols, LANES), WIDE)] * rows
        total = taps_sum(padded, kernel, lanes, rows, cols, False, zero)
        for row in range(rows):
            result[pl.ds(row * cols, cols), lanes] = total[row]

    value = result[...]
    centred = value - jnp.mean(value, axis=1, keepdims=True)
    spread = lax.rsqrt(jnp.mean(centred * centred, axis=1, keepdims=True) + 1e-06)
    value = centred * spread
    normed[...] = value
    inv[...] = jnp.broadcast_to(spread, inv.shape)
    narrow[...] = (value * gain[...] + bias[...]).astype(NARROW)


def hidden_body(copied, *refs):
    patterns = lax.axis_size("row") // 4
    me, _, _ = place()
    acts, in_bias = refs[:2], refs[2]
    scale = refs[3]
    pieces = refs[4:-7]
    keep, send, active, hidden, scale_part, bias_part, weights = refs[-7:]
    half = acts[0].shape[1]
    if copied:
        own = pieces[0].shape[2]
        group = lax.axis_index("grp")
        each = len(pieces) // 2
        for side in range(2):
            blocks = pieces[side * each : (side + 1) * each]
            for spot, block in enumerate(blocks):
                other = jnp.bitwise_xor(group, spot % 2)
                pattern = spot if spot < 2 else 2 * (spot // 2) + other
                for c in range(2):
                    device = jnp.bitwise_xor(me, 4 * pattern + 2 * side + c)
                    rows = pl.ds(pl.multiple_of(device * own, own), own)
                    for which in range(2):
                        weights[which, rows, :] = block[which, c]
    else:
        weights[...] = pieces[0][...]
    in_narrow = weights.at[0]
    out_narrow = weights.at[1]
    bias_row = in_bias[...]
    total = jnp.zeros_like(bias_row)
    scale_total = jnp.zeros_like(scale_part)
    for side in (1, 0):
        preact = dot(acts[side][0], in_narrow[...], ((1,), (0,))) + bias_row
        act_grad = dot(acts[side][1], out_narrow[...], ((1,), (0,)))
        cdf = 0.5 * (1.0 + lax.erf(preact * 0.7071067811865476))
        rows = pl.ds(side * half, half)
        activated = (preact * cdf).astype(NARROW)
        active[rows, :] = activated
        slope = cdf + preact * jnp.exp(-0.5 * preact * preact) * 0.3989422804014327
        grad = act_grad * slope
        total = total + jnp.sum(grad, axis=0, keepdims=True)
        narrow = grad.astype(NARROW)
        hidden[rows, :] = narrow
        out_grad = dot(narrow, in_narrow[...], ((1,), (1,)))
        mixed = dot(activated, out_narrow[...], ((1,), (1,)))
        scale_total = scale_total + jnp.sum(
            mixed * acts[side][1].astype(WIDE), axis=0, keepdims=True
        )
        if side:
            send[0] = out_grad.astype(NARROW)
            send[1] = mixed.astype(NARROW)
        else:
            keep[0] = out_grad
            keep[1] = mixed
    bias_part[...] = total
    scale_part[...] = scale_total / scale[...]


def weight_body(norm_scale, *refs):
    acts, (active, hidden, holder) = refs[:2], refs[2:]
    half = acts[0].shape[1]
    first, second = pl.ds(0, half), pl.ds(half, half)
    for which, right in enumerate((hidden, active)):
        grad = dot(acts[0][which], right[first, :], ((0,), (0,)))
        grad = grad + dot(acts[1][which], right[second, :], ((0,), (0,)))
        holder[which] = norm_scale * grad


def owners_body(turns, holder, after, *targets):
    me, _, _ = place()
    own = holder.shape[1] // lax.axis_size("row")
    for pattern, target in zip(turns, targets):
        for c in range(2):
            device = jnp.bitwise_xor(me, 2 * pattern + c)
            rows = pl.ds(pl.multiple_of(device * own, own), own)
            for which in range(2):
                start = (2 * c + which) * own
                target[start : start + own, :] = holder[which, rows, :].astype(target.dtype)
        if target.shape[0] > 4 * own:
            target[4 * own : 4 * own + SMALL_ROWS, :] = after[...].astype(target.dtype)
            rest = target.shape[0] - 4 * own - SMALL_ROWS
            target[4 * own + SMALL_ROWS :, :] = jnp.zeros((rest, target.shape[1]), target.dtype)


def fold_body(kept, got, stay, leave, mixed_stay, mixed_leave):
    size = stay.shape[0]
    for which, (near, away) in enumerate(((stay, leave), (mixed_stay, mixed_leave))):
        near[...] = kept[which, :size] + got[which, :size].astype(WIDE)
        away[...] = (kept[which, size:] + got[which, size:].astype(WIDE)).astype(NARROW)


def conv_grad_body(norm_scale, *refs):
    kept, got, normed, inv, gain, feats, core_got, outer, scale, in_bias = refs[:10]
    grad, inner_out, rim_out, stay, leave, padded, small = refs[10:]
    rows, cols, channels = feats.shape
    me, c, _ = place()
    out_grad = kept[...] + got[...].astype(WIDE)
    value = normed[...]
    normed_grad = out_grad * gain[...]
    mean = jnp.mean(normed_grad, axis=1, keepdims=True)
    along = jnp.mean(normed_grad * value, axis=1, keepdims=True)
    result = inv[:, :1] * (normed_grad - mean - value * along)
    grad[...] = result
    pixels = rows * cols
    rim = RIM * cols
    rim_out[...] = jnp.where(c == 0, result[:rim], result[pixels - rim :]).astype(NARROW)
    inner_out[...] = jnp.where(c == 0, result[pixels - rim :], result[:rim]).astype(NARROW)
    fill(padded, feats[...], core_got[core_got.shape[0] - rim :, :], outer[...])

    def put(row, lanes, total):
        small[row // SMALL_ROWS, pl.ds(row % SMALL_ROWS, 1), lanes] = norm_scale * total

    @pl.loop(0, channels // LANES)
    def _(step):
        lanes = pl.ds(pl.multiple_of(step * LANES, LANES), LANES)
        own = [grad[pl.ds(row * cols, cols), lanes] for row in range(rows)]
        for tap_col in range(TAPS):
            totals = [jnp.zeros((8, LANES), WIDE)] * TAPS
            for row in range(rows + TAPS - 1):
                line = padded[row, pl.ds(EDGE - RIM + tap_col, cols), lanes]
                for out in range(rows):
                    tap_row = row - out
                    if 0 <= tap_row < TAPS:
                        product = line * own[out]
                        for part in range(cols // 8):
                            totals[tap_row] = totals[tap_row] + product[8 * part : 8 * part + 8]
            for tap_row in range(TAPS):
                total = jnp.sum(totals[tap_row], axis=0, keepdims=True)
                put(TAPS * tap_row + tap_col, lanes, total)

    everything = slice(None)
    row = TAPS * TAPS
    put(row, everything, jnp.sum(out_grad * value, axis=0, keepdims=True))
    put(row + 1, everything, jnp.sum(out_grad, axis=0, keepdims=True))
    put(row + 2, everything, scale[...])
    for part in range(4):
        own_part = jnp.where(lax.rem(me, 4) == part, 1.0, 0.0)
        put(row + 3 + part, everything, own_part * in_bias[...])
    stay[...] = small[c]
    leave[...] = small[1 - c]


def input_grad_body(grad, inner, outer, kernel, cotan, result, padded):
    rows, cols, channels = cotan.shape
    fill(padded, grad[...].reshape(cotan.shape), inner[...], outer[...])

    @pl.loop(0, channels // LANES)
    def _(step):
        lanes = pl.ds(pl.multiple_of(step * LANES, LANES), LANES)
        start = [cotan[row, :, lanes] for row in range(rows)]
        total = taps_sum(padded, kernel, lanes, rows, cols, True, start)
        for row in range(rows):
            result[row, :, lanes] = total[row]


def output_body(feats, scale, kept, got, result):
    mixed = kept[...] + got[...].astype(WIDE)
    result[...] = feats[...] + (scale[...] * mixed).reshape(feats.shape)


def total_body(turns, *refs):
    parts, sums = refs[: len(turns)], refs[len(turns) : -3]
    stay, leave, half = refs[-3:]
    own = stay.shape[2]
    for side in range(2):
        total = jnp.zeros(parts[0].shape, WIDE)
        for part, turn in zip(parts, turns):
            if turn % 2 == side:
                total = total + part[...].astype(WIDE)
        for which in range(2):
            stay[side, which] = total[which * own : (which + 1) * own]
        leave[2 * side * own : 2 * (side + 1) * own, :] = total[2 * own :]
    total = sums[0][...]
    for one in sums[1:]:
        total = total + one[...].astype(WIDE)
    half[...] = total
    leave[4 * own :, :] = total


def final_body(stay, got, half, *refs):
    in_grad, out_grad, kernel_grad, gain, bias, scale, in_bias, held = refs
    _, c, x = place()
    quarter = stay.shape[-1]
    own = stay.shape[2]
    for side in range(2):
        part = 2 * jnp.bitwise_xor(x, side)
        near = pl.ds(pl.multiple_of((part + c) * quarter, quarter), quarter)
        far = pl.ds(pl.multiple_of((part + 1 - c) * quarter, quarter), quarter)
        for which, target in enumerate((in_grad, out_grad)):
            start = (2 * side + which) * own
            target[:, near] = stay[side, which]
            target[:, far] = got[start : start + own, :]
    held[c] = half[...]
    held[1 - c] = got[4 * own :, :]

    def take(row):
        return held[row // SMALL_ROWS, pl.ds(row % SMALL_ROWS, 1), :]

    for tap_row in range(TAPS):
        for tap_col in range(TAPS):
            kernel_grad[tap_row, pl.ds(tap_col, 1), :] = take(TAPS * tap_row + tap_col)
    row = TAPS * TAPS
    gain[...] = take(row)
    bias[...] = take(row + 1)
    scale[...] = take(row + 2)
    for part in range(4):
        in_bias[:, pl.ds(part * quarter, quarter)] = take(row + 3 + part)


def flipped(blocks, axis, bit_set):
    return jnp.where(bit_set == 1, jnp.flip(blocks, axis), blocks)


def canonical(blocks, me, bit_count):
    tail = blocks.shape[1:]
    blocks = blocks.reshape((2,) * bit_count + tail)
    for spot in range(bit_count):
        blocks = flipped(blocks, bit_count - 1 - spot, (me >> spot) & 1)
    return blocks.reshape((2**bit_count,) + tail)


def per_device(
    features, cotangent, kernel, norm_gain, norm_bias, in_weight, in_bias, out_weight, layer_scale
):
    row_count, col_count, channels = features.shape
    own_rows, hidden_count = in_weight.shape
    pixels = row_count * col_count
    count = lax.axis_size("row")
    bit_count = count.bit_length() - 1
    me = lax.axis_index("row")
    group_index = lax.axis_index("grp")
    quarter = hidden_count // 4
    norm_scale = 1.0 / math.sqrt(pixels * count)
    patterns = count // 4
    copied = own_rows % 16 == 0
    gain_row = norm_gain.reshape(1, channels)
    bias_row = norm_bias.reshape(1, channels)
    scale_row = layer_scale.reshape(1, channels)
    rim = RIM * col_count
    padded = pltpu.VMEM((row_count + 2 * RIM, col_count + 2 * EDGE, channels), WIDE)

    piece = (2, own_rows, quarter)
    once = (features, cotangent, scale_row, kernel, gain_row, bias_row)
    own, core, outer, branch, in_bias_own, feats, cotan, scale, taps, gain, bias = run(
        split_body,
        (
            shaped((2,) + piece, NARROW),
            shaped((4 * own_rows + rim, channels), NARROW),
            shaped((rim, channels), NARROW),
            shaped((pixels, channels), NARROW),
            shaped((1, quarter)),
        )
        + tuple(shaped(x.shape) for x in once),
        in_weight,
        out_weight,
        in_bias.reshape(1, hidden_count),
        *once,
        scratch=(
            pltpu.VMEM(in_weight.shape, WIDE),
            pltpu.VMEM(out_weight.shape, WIDE),
            pltpu.VMEM((1, hidden_count), WIDE),
            pltpu.SemaphoreType.DMA((9,)),
        ),
        apart=True,
    )
    core_got = swap(core, 1)
    outer_got = swap_rim(outer)
    full_shape = shaped((2, 2, own_rows, quarter), NARROW)
    joined = run(
        join_body,
        (full_shape, full_shape, shaped((pixels + 4 * own_rows, channels), NARROW)),
        own,
        core_got,
        branch,
    )
    sent_got = swap(joined[2], 2)
    pieces = []
    for side, full in enumerate(joined[:2]):
        pieces += [full, swap(full, 4 + 2 * side)]
        for pair in range(1, patterns // 2):
            here = swap_far(full, pair, side)
            pieces += [here, swap_group(here)]
    each = len(pieces) // 2

    normed, inv, normed_out = run(
        conv_body,
        (
            shaped((pixels, channels)),
            shaped((pixels, LANES)),
            shaped((pixels, channels), NARROW),
        ),
        feats,
        core_got,
        outer_got,
        taps,
        gain,
        bias,
        scratch=(padded, pltpu.VMEM((pixels, channels), WIDE)),
    )
    first_blocks = [block for k, block in enumerate(pieces) if k % each and k != each - 1]
    acts, pieces[each] = run(
        acts_body,
        (shaped((2, 2 * pixels, channels), NARROW), full_shape),
        normed_out,
        branch,
        swap(normed_out, 2),
        sent_got,
        *first_blocks,
    )
    acts_got = swap(acts, 1)

    if not copied:
        lines = []
        for pattern in range(patterns):
            for side in range(2):
                blocks = pieces[side * each : (side + 1) * each]
                if pattern < 2:
                    lines.append(blocks[pattern])
                else:
                    pair = jnp.stack(blocks[pattern - pattern % 2 : pattern - pattern % 2 + 2])
                    lines.append(flipped(pair, 0, group_index)[pattern % 2])
        lines = jnp.moveaxis(jnp.stack(lines), 1, 2).reshape(count, 2, own_rows, quarter)
        lines = jnp.moveaxis(canonical(lines, me, bit_count), 1, 0)
        pieces = [lines.reshape(2, channels, quarter)]
    group = 4 * pixels
    both = (2, 2 * pixels, channels)
    keep, send, active, hidden, scale_part, in_bias_part = run(
        functools.partial(hidden_body, copied),
        (
            shaped(both),
            shaped(both, NARROW),
            shaped((group, quarter), NARROW),
            shaped((group, quarter), NARROW),
            shaped((1, channels)),
            shaped((1, quarter)),
        ),
        acts,
        acts_got,
        in_bias_own,
        scale,
        *pieces,
        scratch=(pltpu.VMEM((2, channels, quarter), NARROW),),
        mib=24,
    )
    half = (shaped((pixels, channels)), shaped((pixels, channels), NARROW))
    out_stay, out_leave, mixed_stay, mixed_leave = run(fold_body, half * 2, keep, swap(send, 1))
    out_got = swap(out_leave, 2)

    holder = run(
        functools.partial(weight_body, norm_scale),
        (shaped((2, channels, quarter)),),
        acts,
        acts_got,
        active,
        hidden,
        mib=24,
    )[0]
    conv_grad, inner_out, rim_out, stay, leave = run(
        functools.partial(conv_grad_body, norm_scale),
        (
            shaped((pixels, channels)),
            shaped((rim, channels), NARROW),
            shaped((rim, channels), NARROW),
            shaped((SMALL_ROWS, channels)),
            shaped((SMALL_ROWS, channels)),
        ),
        out_stay,
        out_got,
        normed,
        inv,
        gain,
        feats,
        core_got,
        outer_got,
        scale_part,
        in_bias_part,
        scratch=(padded, pltpu.VMEM((2, SMALL_ROWS, channels), WIDE)),
    )
    rim_got = swap_rim(rim_out)
    inner_got = swap(inner_out, 1)
    sums = stay + swap(leave, 1)

    far_turns = (*range(2 * patterns - 1, 4, -2), 3)
    near_turns = (*range(4, 2 * patterns, 2), 2, 1, 0)
    owned = 4 * own_rows
    if copied:
        parts = run(
            functools.partial(owners_body, far_turns),
            (shaped((owned, quarter), NARROW),) * len(far_turns),
            holder,
            out_leave,
        )
    else:
        flat = holder.reshape(2, count, own_rows, quarter)
        flat = canonical(jnp.moveaxis(flat, 1, 0), me, bit_count)
        flat = flat.reshape(2 * patterns, owned, quarter)
        parts = [flat[p].astype(NARROW) for p in far_turns]
    far_parts = [swap(part, 2 * p) for p, part in zip(far_turns, parts)]
    sums, far_parts = lax.optimization_barrier((sums, far_parts))
    sums = sums + swap(sums, 2)
    sums, mixed_leave = lax.optimization_barrier((sums, mixed_leave))
    if copied:
        joint = shaped((owned + 32, quarter), NARROW)
        *parts, side_part, near_own = run(
            functools.partial(owners_body, near_turns),
            (joint,) * (len(near_turns) - 2)
            + (shaped((owned, quarter), NARROW), shaped((owned, quarter))),
            holder,
            sums,
        )
        parts = [swap(part, 2 * p) for p, part in zip(near_turns, parts)]
        sums_parts = [part[owned : owned + SMALL_ROWS] for part in parts]
        near_parts = [part[:owned] for part in parts] + [swap(side_part, 2), near_own]
    else:
        near_parts = [swap(flat[p].astype(NARROW), 2 * p) for p in near_turns[:-1]] + [flat[0]]
        sums_parts = [swap(sums.astype(NARROW), 2 * p) for p in near_turns[:-2]]

    input_grad = run(
        input_grad_body,
        (shaped(features.shape),),
        conv_grad,
        inner_got,
        rim_got,
        taps,
        cotan,
        scratch=(padded,),
    )[0]
    output = run(
        output_body,
        (shaped(features.shape),),
        feats,
        scale,
        mixed_stay,
        swap(mixed_leave, 2),
    )[0]
    parts = list(far_parts) + near_parts
    parts, input_grad, output = lax.optimization_barrier((parts, input_grad, output))

    stay, leave, half_sums = run(
        functools.partial(total_body, far_turns + near_turns),
        (
            shaped((2, 2, own_rows, quarter)),
            shaped((owned + SMALL_ROWS, quarter)),
            shaped((SMALL_ROWS, channels)),
        ),
        *parts,
        sums,
        *sums_parts,
    )
    (
        in_weight_grad,
        out_weight_grad,
        kernel_grad,
        gain_grad,
        bias_grad,
        scale_grad,
        in_bias_grad,
    ) = run(
        final_body,
        (
            shaped((own_rows, hidden_count)),
            shaped((own_rows, hidden_count)),
            shaped(kernel.shape),
            shaped((1, channels)),
            shaped((1, channels)),
            shaped((1, channels)),
            shaped((1, hidden_count)),
        ),
        stay,
        swap(leave, 1),
        half_sums,
        scratch=(pltpu.VMEM((2, SMALL_ROWS, channels), WIDE),),
    )
    return (
        output,
        input_grad,
        in_weight_grad,
        out_weight_grad,
        kernel_grad,
        gain_grad.reshape(channels),
        bias_grad.reshape(channels),
        in_bias_grad.reshape(hidden_count),
        scale_grad.reshape(channels),
    )


def solution(mesh):
    return jax.shard_map(
        per_device,
        mesh=mesh,
        in_specs=(
            P(("grp", "row"), None, None),
            P(("grp", "row"), None, None),
            P(),
            P(),
            P(),
            P("row", None),
            P(),
            P("row", None),
            P(),
        ),
        out_specs=(
            P(("grp", "row"), None, None),
            P(("grp", "row"), None, None),
            P(("grp", "row"), None),
            P(("grp", "row"), None),
            P("grp", None, None),
            P("grp"),
            P("grp"),
            P("grp"),
            P("grp"),
        ),
        check_vma=False,
    )
```

```python
import functools
import math

import jax
import jax.numpy as jnp
from jax import lax
from jax.experimental import pallas as pl
from jax.experimental.pallas import tpu as pltpu
from jax.sharding import PartitionSpec as P

NARROW = jnp.bfloat16
WIDE = jnp.float32
TAPS = 7
RIM = 3
EDGE = 8
LANES = 128
SMALL_ROWS = 28


def swap(value, bit):
    count = lax.axis_size("row")
    return lax.ppermute(value, "row", [(i, i ^ bit) for i in range(count)])


def swap_rim(value):
    count = lax.axis_size("row")
    pairs = [(i, i + 1) for i in range(1, count - 1, 2)]
    return lax.ppermute(value, "row", pairs + [(j, i) for i, j in pairs])


def shaped(shape, dtype=WIDE):
    return jax.ShapeDtypeStruct(shape, dtype)


def swap_far(value, pair, side):
    count = lax.axis_size("row")
    pairs = []
    for group in range(2):
        bits = 4 * (2 * pair + group) + 2 * side
        pairs += [(group * count + i, group * count + (i ^ bits)) for i in range(count)]
    return lax.ppermute(value, ("grp", "row"), pairs)


def swap_group(value):
    return lax.ppermute(value, "grp", [(0, 1), (1, 0)])


def run(body, outs, *operands, scratch=(), mib=16, order=0, apart=False):
    extra = {}
    if apart:
        extra = {"in_specs": [pl.BlockSpec(memory_space=pltpu.HBM)] * len(operands)}
        operands = [pltpu.with_memory_space_constraint(x, pltpu.HBM) for x in operands]
    return pl.pallas_call(
        body,
        out_shape=outs,
        **extra,
        scratch_shapes=scratch,
        compiler_params=pltpu.CompilerParams(vmem_limit_bytes=mib * 2**20),
        cost_estimate=pl.CostEstimate(flops=order * 10**9, bytes_accessed=0, transcendentals=0),
    )(*operands)


def place():
    me = lax.axis_index("row")
    return me, lax.rem(me, 2), lax.rem(lax.div(me, 2), 2)


def dot(left, right, dims):
    return lax.dot_general(left, right, (dims, ((), ())), preferred_element_type=WIDE)


def split_body(*refs):
    inw_hbm, outw_hbm, in_bias_hbm = refs[:3]
    own, core, outer, branch, bias_part = refs[9:14]
    inw, outw, in_bias, sems = refs[20:]
    feats, cotan, scale = refs[14:17]
    pairs = list(zip(refs[3:9], refs[14:20]))
    pairs += [(inw_hbm, inw), (outw_hbm, outw), (in_bias_hbm, in_bias)]
    copies = [pltpu.make_async_copy(a, b, sems.at[k]) for k, (a, b) in enumerate(pairs)]
    for copy in copies[6:] + copies[:6]:
        copy.start()
    me, c, x = place()
    even = c == 0
    quarter = own.shape[-1]
    rows, cols, channels = feats.shape
    own_rows = inw.shape[0]
    copies[6].wait()
    copies[7].wait()
    for side in range(2):
        for part, near in ((2 * jnp.bitwise_xor(x, side) + c, True), (2 * jnp.bitwise_xor(x, side) + 1 - c, False)):
            lanes = pl.ds(pl.multiple_of(part * quarter, quarter), quarter)
            for which, source in enumerate((inw, outw)):
                value = source[:, lanes].astype(NARROW)
                if near:
                    own[side, which] = value
                else:
                    core[pl.ds((2 * side + which) * own_rows, own_rows), :] = value
    copies[0].wait()
    first = feats[:RIM].astype(NARROW).reshape(RIM * cols, channels)
    last = feats[rows - RIM :].astype(NARROW).reshape(RIM * cols, channels)
    core[4 * own_rows :, :] = jnp.where(even, last, first)
    outer[...] = jnp.where(even, first, last)
    copies[1].wait()
    copies[2].wait()
    branch[...] = (scale[...] * cotan[...].reshape(branch.shape)).astype(NARROW)
    copies[8].wait()
    lanes = pl.ds(pl.multiple_of(lax.rem(me, 4) * quarter, quarter), quarter)
    bias_part[...] = in_bias[:, lanes]
    for copy in copies[3:6]:
        copy.wait()


def join_body(mine, other, branch, after, *targets):
    del after
    own = mine.shape[2]
    sent = targets[2]
    pixels = branch.shape[0]
    sent[:pixels, :] = branch[...]
    for side, full in enumerate(targets[:2]):
        for which in range(2):
            rows = pl.ds((2 * side + which) * own, own)
            full[which, 0] = mine[side, which]
            full[which, 1] = other[rows, :]
            if side:
                start = pixels + 2 * which * own
                sent[start : start + own, :] = mine[side, which]
                sent[start + own : start + 2 * own, :] = other[rows, :]


def acts_body(normed, branch, normed_got, sent_got, *refs):
    acts, full = refs[-2:]
    pixels = branch.shape[0]
    acts[0, :pixels] = normed[...]
    acts[0, pixels:] = normed_got[...]
    acts[1, :pixels] = branch[...]
    acts[1, pixels:] = sent_got[:pixels, :]
    own = full.shape[2]
    for which in range(2):
        for core in range(2):
            start = pixels + (2 * which + core) * own
            full[which, core] = sent_got[start : start + own, :]


def fill(padded, block, inner, outer):
    rows, cols, channels = block.shape
    _, c, _ = place()
    padded[:, :EDGE, :] = jnp.zeros_like(padded[:, :EDGE, :])
    padded[:, EDGE + cols :, :] = jnp.zeros_like(padded[:, EDGE + cols :, :])
    middle = slice(EDGE, EDGE + cols)
    inner = inner.astype(WIDE).reshape(RIM, cols, channels)
    outer = outer.astype(WIDE).reshape(RIM, cols, channels)
    padded[:RIM, middle, :] = jnp.where(c == 0, outer, inner)
    padded[RIM : RIM + rows, middle, :] = block
    padded[RIM + rows :, middle, :] = jnp.where(c == 0, inner, outer)


def taps_sum(padded, kernel, lanes, rows, cols, mirrored, start):
    total = list(start)
    for tap_col in range(TAPS):
        for row in range(rows + TAPS - 1):
            line = padded[row, pl.ds(EDGE - RIM + tap_col, cols), lanes]
            for out in range(rows):
                tap_row = row - out
                if 0 <= tap_row < TAPS:
                    if mirrored:
                        tap = kernel[TAPS - 1 - tap_row, pl.ds(TAPS - 1 - tap_col, 1), lanes]
                    else:
                        tap = kernel[tap_row, pl.ds(tap_col, 1), lanes]
                    total[out] = total[out] + line * tap
    return total


def conv_body(
    feats, core_got, outer, kernel, gain, bias, normed, inv, narrow, padded, result
):
    rows, cols, channels = feats.shape
    start = core_got.shape[0] - RIM * cols
    fill(padded, feats[...], core_got[start:, :], outer[...])

    @pl.loop(0, channels // LANES)
    def _(step):
        lanes = pl.ds(pl.multiple_of(step * LANES, LANES), LANES)
        zero = [jnp.zeros((cols, LANES), WIDE)] * rows
        total = taps_sum(padded, kernel, lanes, rows, cols, False, zero)
        for row in range(rows):
            result[pl.ds(row * cols, cols), lanes] = total[row]

    value = result[...]
    centred = value - jnp.mean(value, axis=1, keepdims=True)
    spread = lax.rsqrt(jnp.mean(centred * centred, axis=1, keepdims=True) + 1e-06)
    value = centred * spread
    normed[...] = value
    inv[...] = jnp.broadcast_to(spread, inv.shape)
    narrow[...] = (value * gain[...] + bias[...]).astype(NARROW)


def hidden_body(copied, *refs):
    patterns = lax.axis_size("row") // 4
    me, _, _ = place()
    acts, in_bias = refs[:2], refs[2]
    pieces = refs[3:-7]
    keep, send, active, hidden, out_copy, bias_part, weights = refs[-7:]
    half = acts[0].shape[1]
    if copied:
        own = pieces[0].shape[2]
        group = lax.axis_index("grp")
        each = len(pieces) // 2
        for side in range(2):
            blocks = pieces[side * each : (side + 1) * each]
            for spot, block in enumerate(blocks):
                other = jnp.bitwise_xor(group, spot % 2)
                pattern = spot if spot < 2 else 2 * (spot // 2) + other
                for c in range(2):
                    device = jnp.bitwise_xor(me, 4 * pattern + 2 * side + c)
                    rows = pl.ds(pl.multiple_of(device * own, own), own)
                    for which in range(2):
                        weights[which, rows, :] = block[which, c]
    else:
        weights[...] = pieces[0][...]
    in_narrow = weights.at[0]
    out_narrow = weights.at[1]
    out_copy[...] = weights[1]
    bias_row = in_bias[...]
    total = jnp.zeros_like(bias_row)
    for side in (1, 0):
        preact = dot(acts[side][0], in_narrow[...], ((1,), (0,))) + bias_row
        act_grad = dot(acts[side][1], out_narrow[...], ((1,), (0,)))
        cdf = 0.5 * (1.0 + lax.erf(preact * 0.7071067811865476))
        rows = pl.ds(side * half, half)
        activated = (preact * cdf).astype(NARROW)
        active[rows, :] = activated
        slope = cdf + preact * jnp.exp(-0.5 * preact * preact) * 0.3989422804014327
        grad = act_grad * slope
        total = total + jnp.sum(grad, axis=0, keepdims=True)
        narrow = grad.astype(NARROW)
        hidden[rows, :] = narrow
        out_grad = dot(narrow, in_narrow[...], ((1,), (1,)))
        if side:
            send[...] = out_grad.astype(NARROW)
        else:
            keep[...] = out_grad
    bias_part[...] = total


def weight_body(norm_scale, *refs):
    acts, (active, hidden, out_narrow, scale) = refs[:2], refs[2:6]
    holder, keep, send, scale_part = refs[6:]
    half = acts[0].shape[1]
    first, second = pl.ds(0, half), pl.ds(half, half)
    for which, right in enumerate((hidden, active)):
        grad = dot(acts[0][which], right[first, :], ((0,), (0,)))
        grad = grad + dot(acts[1][which], right[second, :], ((0,), (0,)))
        holder[which] = norm_scale * grad
    total = jnp.zeros_like(scale_part)
    for side, rows in enumerate((first, second)):
        mixed = dot(active[rows, :], out_narrow[...], ((1,), (1,)))
        total = total + jnp.sum(mixed * acts[side][1].astype(WIDE), axis=0, keepdims=True)
        if side:
            send[...] = mixed.astype(NARROW)
        else:
            keep[...] = mixed
    scale_part[...] = total / scale[...]


def owners_body(turns, holder, after, *targets):
    me, _, _ = place()
    own = holder.shape[1] // lax.axis_size("row")
    for pattern, target in zip(turns, targets):
        for c in range(2):
            device = jnp.bitwise_xor(me, 2 * pattern + c)
            rows = pl.ds(pl.multiple_of(device * own, own), own)
            for which in range(2):
                start = (2 * c + which) * own
                target[start : start + own, :] = holder[which, rows, :].astype(target.dtype)
        if target.shape[0] > 4 * own:
            target[4 * own : 4 * own + SMALL_ROWS, :] = after[...].astype(target.dtype)
            rest = target.shape[0] - 4 * own - SMALL_ROWS
            target[4 * own + SMALL_ROWS :, :] = jnp.zeros((rest, target.shape[1]), target.dtype)


def fold_body(kept, got, stay, leave):
    size = stay.shape[0]
    stay[...] = kept[:size] + got[:size].astype(WIDE)
    leave[...] = (kept[size:] + got[size:].astype(WIDE)).astype(NARROW)


def conv_grad_body(norm_scale, *refs):
    kept, got, normed, inv, gain, feats, core_got, outer, scale, in_bias = refs[:10]
    grad, inner_out, rim_out, stay, leave, padded, small = refs[10:]
    rows, cols, channels = feats.shape
    me, c, _ = place()
    out_grad = kept[...] + got[...].astype(WIDE)
    value = normed[...]
    normed_grad = out_grad * gain[...]
    mean = jnp.mean(normed_grad, axis=1, keepdims=True)
    along = jnp.mean(normed_grad * value, axis=1, keepdims=True)
    result = inv[:, :1] * (normed_grad - mean - value * along)
    grad[...] = result
    pixels = rows * cols
    rim = RIM * cols
    rim_out[...] = jnp.where(c == 0, result[:rim], result[pixels - rim :]).astype(NARROW)
    inner_out[...] = jnp.where(c == 0, result[pixels - rim :], result[:rim]).astype(NARROW)
    fill(padded, feats[...], core_got[core_got.shape[0] - rim :, :], outer[...])

    def put(row, lanes, total):
        small[row // SMALL_ROWS, pl.ds(row % SMALL_ROWS, 1), lanes] = norm_scale * total

    @pl.loop(0, channels // LANES)
    def _(step):
        lanes = pl.ds(pl.multiple_of(step * LANES, LANES), LANES)
        own = [grad[pl.ds(row * cols, cols), lanes] for row in range(rows)]
        for tap_col in range(TAPS):
            totals = [jnp.zeros((8, LANES), WIDE)] * TAPS
            for row in range(rows + TAPS - 1):
                line = padded[row, pl.ds(EDGE - RIM + tap_col, cols), lanes]
                for out in range(rows):
                    tap_row = row - out
                    if 0 <= tap_row < TAPS:
                        product = line * own[out]
                        for part in range(cols // 8):
                            totals[tap_row] = totals[tap_row] + product[8 * part : 8 * part + 8]
            for tap_row in range(TAPS):
                total = jnp.sum(totals[tap_row], axis=0, keepdims=True)
                put(TAPS * tap_row + tap_col, lanes, total)

    everything = slice(None)
    row = TAPS * TAPS
    put(row, everything, jnp.sum(out_grad * value, axis=0, keepdims=True))
    put(row + 1, everything, jnp.sum(out_grad, axis=0, keepdims=True))
    put(row + 2, everything, scale[...])
    for part in range(4):
        own_part = jnp.where(lax.rem(me, 4) == part, 1.0, 0.0)
        put(row + 3 + part, everything, own_part * in_bias[...])
    stay[...] = small[c]
    leave[...] = small[1 - c]


def input_grad_body(grad, inner, outer, kernel, cotan, result, padded):
    rows, cols, channels = cotan.shape
    fill(padded, grad[...].reshape(cotan.shape), inner[...], outer[...])

    @pl.loop(0, channels // LANES)
    def _(step):
        lanes = pl.ds(pl.multiple_of(step * LANES, LANES), LANES)
        start = [cotan[row, :, lanes] for row in range(rows)]
        total = taps_sum(padded, kernel, lanes, rows, cols, True, start)
        for row in range(rows):
            result[row, :, lanes] = total[row]


def output_body(feats, scale, kept, got, result):
    mixed = kept[...] + got[...].astype(WIDE)
    result[...] = feats[...] + (scale[...] * mixed).reshape(feats.shape)


def total_body(turns, *refs):
    parts, sums = refs[: len(turns)], refs[len(turns) : -3]
    stay, leave, half = refs[-3:]
    own = stay.shape[2]
    for side in range(2):
        total = jnp.zeros(parts[0].shape, WIDE)
        for part, turn in zip(parts, turns):
            if turn % 2 == side:
                total = total + part[...].astype(WIDE)
        for which in range(2):
            stay[side, which] = total[which * own : (which + 1) * own]
        leave[2 * side * own : 2 * (side + 1) * own, :] = total[2 * own :]
    total = sums[0][...]
    for one in sums[1:]:
        total = total + one[...].astype(WIDE)
    half[...] = total
    leave[4 * own :, :] = total


def final_body(stay, got, half, *refs):
    in_grad, out_grad, kernel_grad, gain, bias, scale, in_bias, held = refs
    _, c, x = place()
    quarter = stay.shape[-1]
    own = stay.shape[2]
    for side in range(2):
        part = 2 * jnp.bitwise_xor(x, side)
        near = pl.ds(pl.multiple_of((part + c) * quarter, quarter), quarter)
        far = pl.ds(pl.multiple_of((part + 1 - c) * quarter, quarter), quarter)
        for which, target in enumerate((in_grad, out_grad)):
            start = (2 * side + which) * own
            target[:, near] = stay[side, which]
            target[:, far] = got[start : start + own, :]
    held[c] = half[...]
    held[1 - c] = got[4 * own :, :]

    def take(row):
        return held[row // SMALL_ROWS, pl.ds(row % SMALL_ROWS, 1), :]

    for tap_row in range(TAPS):
        for tap_col in range(TAPS):
            kernel_grad[tap_row, pl.ds(tap_col, 1), :] = take(TAPS * tap_row + tap_col)
    row = TAPS * TAPS
    gain[...] = take(row)
    bias[...] = take(row + 1)
    scale[...] = take(row + 2)
    for part in range(4):
        in_bias[:, pl.ds(part * quarter, quarter)] = take(row + 3 + part)


def flipped(blocks, axis, bit_set):
    return jnp.where(bit_set == 1, jnp.flip(blocks, axis), blocks)


def canonical(blocks, me, bit_count):
    tail = blocks.shape[1:]
    blocks = blocks.reshape((2,) * bit_count + tail)
    for spot in range(bit_count):
        blocks = flipped(blocks, bit_count - 1 - spot, (me >> spot) & 1)
    return blocks.reshape((2**bit_count,) + tail)


def per_device(
    features, cotangent, kernel, norm_gain, norm_bias, in_weight, in_bias, out_weight, layer_scale
):
    row_count, col_count, channels = features.shape
    own_rows, hidden_count = in_weight.shape
    pixels = row_count * col_count
    count = lax.axis_size("row")
    bit_count = count.bit_length() - 1
    me = lax.axis_index("row")
    group_index = lax.axis_index("grp")
    quarter = hidden_count // 4
    norm_scale = 1.0 / math.sqrt(pixels * count)
    patterns = count // 4
    copied = own_rows % 16 == 0
    gain_row = norm_gain.reshape(1, channels)
    bias_row = norm_bias.reshape(1, channels)
    scale_row = layer_scale.reshape(1, channels)
    rim = RIM * col_count
    padded = pltpu.VMEM((row_count + 2 * RIM, col_count + 2 * EDGE, channels), WIDE)

    piece = (2, own_rows, quarter)
    once = (features, cotangent, scale_row, kernel, gain_row, bias_row)
    own, core, outer, branch, in_bias_own, feats, cotan, scale, taps, gain, bias = run(
        split_body,
        (
            shaped((2,) + piece, NARROW),
            shaped((4 * own_rows + rim, channels), NARROW),
            shaped((rim, channels), NARROW),
            shaped((pixels, channels), NARROW),
            shaped((1, quarter)),
        )
        + tuple(shaped(x.shape) for x in once),
        in_weight,
        out_weight,
        in_bias.reshape(1, hidden_count),
        *once,
        scratch=(
            pltpu.VMEM(in_weight.shape, WIDE),
            pltpu.VMEM(out_weight.shape, WIDE),
            pltpu.VMEM((1, hidden_count), WIDE),
            pltpu.SemaphoreType.DMA((9,)),
        ),
        apart=True,
    )
    core_got = swap(core, 1)
    outer_got = swap_rim(outer)
    full_shape = shaped((2, 2, own_rows, quarter), NARROW)
    joined = run(
        join_body,
        (full_shape, full_shape, shaped((pixels + 4 * own_rows, channels), NARROW)),
        own,
        core_got,
        branch,
        outer_got,
    )
    sent_got = swap(joined[2], 2)
    pieces = []
    for side, full in enumerate(joined[:2]):
        pieces += [full, swap(full, 4 + 2 * side)]
        for pair in range(1, patterns // 2):
            here = swap_far(full, pair, side)
            pieces += [here, swap_group(here)]
    each = len(pieces) // 2

    normed, inv, normed_out = run(
        conv_body,
        (
            shaped((pixels, channels)),
            shaped((pixels, LANES)),
            shaped((pixels, channels), NARROW),
        ),
        feats,
        core_got,
        outer_got,
        taps,
        gain,
        bias,
        scratch=(padded, pltpu.VMEM((pixels, channels), WIDE)),
    )
    first_blocks = [block for k, block in enumerate(pieces) if k % each and k != each - 1]
    acts, pieces[each] = run(
        acts_body,
        (shaped((2, 2 * pixels, channels), NARROW), full_shape),
        normed_out,
        branch,
        swap(normed_out, 2),
        sent_got,
        *first_blocks,
    )
    acts_got = swap(acts, 1)

    if not copied:
        lines = []
        for pattern in range(patterns):
            for side in range(2):
                blocks = pieces[side * each : (side + 1) * each]
                if pattern < 2:
                    lines.append(blocks[pattern])
                else:
                    pair = jnp.stack(blocks[pattern - pattern % 2 : pattern - pattern % 2 + 2])
                    lines.append(flipped(pair, 0, group_index)[pattern % 2])
        lines = jnp.moveaxis(jnp.stack(lines), 1, 2).reshape(count, 2, own_rows, quarter)
        lines = jnp.moveaxis(canonical(lines, me, bit_count), 1, 0)
        pieces = [lines.reshape(2, channels, quarter)]
    group = 4 * pixels
    keep, send, active, hidden, out_narrow, in_bias_part = run(
        functools.partial(hidden_body, copied),
        (
            shaped((2 * pixels, channels)),
            shaped((2 * pixels, channels), NARROW),
            shaped((group, quarter), NARROW),
            shaped((group, quarter), NARROW),
            shaped((channels, quarter), NARROW),
            shaped((1, quarter)),
        ),
        acts,
        acts_got,
        in_bias_own,
        *pieces,
        scratch=(pltpu.VMEM((2, channels, quarter), NARROW),),
        mib=24,
    )
    half = (shaped((pixels, channels)), shaped((pixels, channels), NARROW))
    out_stay, out_leave = run(fold_body, half, keep, swap(send, 1))
    out_got = swap(out_leave, 2)

    holder, mixed_keep, mixed_send, scale_part = run(
        functools.partial(weight_body, norm_scale),
        (
            shaped((2, channels, quarter)),
            shaped((2 * pixels, channels)),
            shaped((2 * pixels, channels), NARROW),
            shaped((1, channels)),
        ),
        acts,
        acts_got,
        active,
        hidden,
        out_narrow,
        scale,
        mib=24,
    )
    conv_grad, inner_out, rim_out, stay, leave = run(
        functools.partial(conv_grad_body, norm_scale),
        (
            shaped((pixels, channels)),
            shaped((rim, channels), NARROW),
            shaped((rim, channels), NARROW),
            shaped((SMALL_ROWS, channels)),
            shaped((SMALL_ROWS, channels)),
        ),
        out_stay,
        out_got,
        normed,
        inv,
        gain,
        feats,
        core_got,
        outer_got,
        scale_part,
        in_bias_part,
        scratch=(padded, pltpu.VMEM((2, SMALL_ROWS, channels), WIDE)),
    )
    sums = stay + swap(leave, 1)

    far_turns = (*range(2 * patterns - 1, 4, -2), 3)
    near_turns = (*range(4, 2 * patterns, 2), 2, 1, 0)
    owned = 4 * own_rows
    if copied:
        parts = run(
            functools.partial(owners_body, far_turns),
            (shaped((owned, quarter), NARROW),) * len(far_turns),
            holder,
            out_leave,
        )
    else:
        flat = holder.reshape(2, count, own_rows, quarter)
        flat = canonical(jnp.moveaxis(flat, 1, 0), me, bit_count)
        flat = flat.reshape(2 * patterns, owned, quarter)
        parts = [flat[p].astype(NARROW) for p in far_turns]
    far_parts = [swap(part, 2 * p) for p, part in zip(far_turns, parts)]
    sums, far_parts[0] = lax.optimization_barrier((sums, far_parts[0]))
    sums = sums + swap(sums, 2)
    rim_got = swap_rim(rim_out)
    inner_got = swap(inner_out, 1)
    sums, far_parts, rim_got, inner_got = lax.optimization_barrier(
        (sums, far_parts, rim_got, inner_got)
    )
    if copied:
        joint = shaped((owned + 32, quarter), NARROW)
        *parts, side_part, near_own = run(
            functools.partial(owners_body, near_turns),
            (joint,) * (len(near_turns) - 2)
            + (shaped((owned, quarter), NARROW), shaped((owned, quarter))),
            holder,
            sums,
        )
        parts, mixed_send = lax.optimization_barrier((parts, mixed_send))
        parts = [swap(part, 2 * p) for p, part in zip(near_turns, parts)]
        sums_parts = [part[owned : owned + SMALL_ROWS] for part in parts]
        near_parts = [part[:owned] for part in parts] + [swap(side_part, 2), near_own]
    else:
        near_parts = [swap(flat[p].astype(NARROW), 2 * p) for p in near_turns[:-1]] + [flat[0]]
        sums_parts = [swap(sums.astype(NARROW), 2 * p) for p in near_turns[:-2]]

    mixed_stay, mixed_leave = run(fold_body, half, mixed_keep, swap(mixed_send, 1))
    input_grad = run(
        input_grad_body,
        (shaped(features.shape),),
        conv_grad,
        inner_got,
        rim_got,
        taps,
        cotan,
        scratch=(padded,),
    )[0]
    output = run(
        output_body,
        (shaped(features.shape),),
        feats,
        scale,
        mixed_stay,
        swap(mixed_leave, 2),
    )[0]
    parts = list(far_parts) + near_parts
    parts, input_grad, output = lax.optimization_barrier((parts, input_grad, output))

    stay, leave, half_sums = run(
        functools.partial(total_body, far_turns + near_turns),
        (
            shaped((2, 2, own_rows, quarter)),
            shaped((owned + SMALL_ROWS, quarter)),
            shaped((SMALL_ROWS, channels)),
        ),
        *parts,
        sums,
        *sums_parts,
    )
    (
        in_weight_grad,
        out_weight_grad,
        kernel_grad,
        gain_grad,
        bias_grad,
        scale_grad,
        in_bias_grad,
    ) = run(
        final_body,
        (
            shaped((own_rows, hidden_count)),
            shaped((own_rows, hidden_count)),
            shaped(kernel.shape),
            shaped((1, channels)),
            shaped((1, channels)),
            shaped((1, channels)),
            shaped((1, hidden_count)),
        ),
        stay,
        swap(leave, 1),
        half_sums,
        scratch=(pltpu.VMEM((2, SMALL_ROWS, channels), WIDE),),
    )
    return (
        output,
        input_grad,
        in_weight_grad,
        out_weight_grad,
        kernel_grad,
        gain_grad.reshape(channels),
        bias_grad.reshape(channels),
        in_bias_grad.reshape(hidden_count),
        scale_grad.reshape(channels),
    )


def solution(mesh):
    return jax.shard_map(
        per_device,
        mesh=mesh,
        in_specs=(
            P(("grp", "row"), None, None),
            P(("grp", "row"), None, None),
            P(),
            P(),
            P(),
            P("row", None),
            P(),
            P("row", None),
            P(),
        ),
        out_specs=(
            P(("grp", "row"), None, None),
            P(("grp", "row"), None, None),
            P(("grp", "row"), None),
            P(("grp", "row"), None),
            P("grp", None, None),
            P("grp"),
            P("grp"),
            P("grp"),
            P("grp"),
        ),
        check_vma=False,
    )
```

```python
import functools
import math

import jax
import jax.numpy as jnp
from jax import lax
from jax.experimental import pallas as pl
from jax.experimental.pallas import tpu as pltpu
from jax.sharding import PartitionSpec as P

NARROW = jnp.bfloat16
WIDE = jnp.float32
TAPS = 7
RIM = 3
EDGE = 8
LANES = 128
SMALL_ROWS = 28


def swap(value, bit):
    count = lax.axis_size("row")
    return lax.ppermute(value, "row", [(i, i ^ bit) for i in range(count)])


def swap_rim(value):
    count = lax.axis_size("row")
    pairs = [(i, i + 1) for i in range(1, count - 1, 2)]
    return lax.ppermute(value, "row", pairs + [(j, i) for i, j in pairs])


def shaped(shape, dtype=WIDE):
    return jax.ShapeDtypeStruct(shape, dtype)


def swap_far(value, pair, side):
    count = lax.axis_size("row")
    pairs = []
    for group in range(2):
        bits = 4 * (2 * pair + group) + 2 * side
        pairs += [(group * count + i, group * count + (i ^ bits)) for i in range(count)]
    return lax.ppermute(value, ("grp", "row"), pairs)


def swap_group(value):
    return lax.ppermute(value, "grp", [(0, 1), (1, 0)])


def run(body, outs, *operands, scratch=(), mib=16, order=0, apart=False):
    extra = {}
    if apart:
        extra = {"in_specs": [pl.BlockSpec(memory_space=pltpu.HBM)] * len(operands)}
        operands = [pltpu.with_memory_space_constraint(x, pltpu.HBM) for x in operands]
    return pl.pallas_call(
        body,
        out_shape=outs,
        **extra,
        scratch_shapes=scratch,
        compiler_params=pltpu.CompilerParams(vmem_limit_bytes=mib * 2**20),
        cost_estimate=pl.CostEstimate(flops=order * 10**9, bytes_accessed=0, transcendentals=0),
    )(*operands)


def place():
    me = lax.axis_index("row")
    return me, lax.rem(me, 2), lax.rem(lax.div(me, 2), 2)


def dot(left, right, dims):
    return lax.dot_general(left, right, (dims, ((), ())), preferred_element_type=WIDE)


def split_body(*refs):
    inw_hbm, outw_hbm, in_bias_hbm = refs[:3]
    own, core, outer, branch, bias_part = refs[9:14]
    inw, outw, in_bias, sems = refs[20:]
    feats, cotan, scale = refs[14:17]
    pairs = list(zip(refs[3:9], refs[14:20]))
    pairs += [(inw_hbm, inw), (outw_hbm, outw), (in_bias_hbm, in_bias)]
    copies = [pltpu.make_async_copy(a, b, sems.at[k]) for k, (a, b) in enumerate(pairs)]
    for copy in copies[6:] + copies[:6]:
        copy.start()
    me, c, x = place()
    even = c == 0
    quarter = own.shape[-1]
    rows, cols, channels = feats.shape
    own_rows = inw.shape[0]
    copies[6].wait()
    copies[7].wait()
    for side in range(2):
        for part, near in ((2 * jnp.bitwise_xor(x, side) + c, True), (2 * jnp.bitwise_xor(x, side) + 1 - c, False)):
            lanes = pl.ds(pl.multiple_of(part * quarter, quarter), quarter)
            for which, source in enumerate((inw, outw)):
                value = source[:, lanes].astype(NARROW)
                if near:
                    own[side, which] = value
                else:
                    core[pl.ds((2 * side + which) * own_rows, own_rows), :] = value
    copies[0].wait()
    first = feats[:RIM].reshape(RIM * cols, channels)
    last = feats[rows - RIM :].reshape(RIM * cols, channels)
    core[4 * own_rows :, :] = jnp.where(even, last, first).astype(NARROW)
    outer[...] = jnp.where(even, first, last)
    copies[1].wait()
    copies[2].wait()
    branch[...] = (scale[...] * cotan[...].reshape(branch.shape)).astype(NARROW)
    copies[8].wait()
    lanes = pl.ds(pl.multiple_of(lax.rem(me, 4) * quarter, quarter), quarter)
    bias_part[...] = in_bias[:, lanes]
    for copy in copies[3:6]:
        copy.wait()


def join_body(mine, other, branch, *targets):
    own = mine.shape[2]
    sent = targets[2]
    pixels = branch.shape[0]
    sent[:pixels, :] = branch[...]
    for side, full in enumerate(targets[:2]):
        for which in range(2):
            rows = pl.ds((2 * side + which) * own, own)
            full[which, 0] = mine[side, which]
            full[which, 1] = other[rows, :]
            if side:
                start = pixels + 2 * which * own
                sent[start : start + own, :] = mine[side, which]
                sent[start + own : start + 2 * own, :] = other[rows, :]


def acts_body(normed, branch, normed_got, sent_got, *refs):
    acts, full = refs[-2:]
    pixels = branch.shape[0]
    acts[0, :pixels] = normed[...]
    acts[0, pixels:] = normed_got[...]
    acts[1, :pixels] = branch[...]
    acts[1, pixels:] = sent_got[:pixels, :]
    own = full.shape[2]
    for which in range(2):
        for core in range(2):
            start = pixels + (2 * which + core) * own
            full[which, core] = sent_got[start : start + own, :]


def fill(padded, block, inner, outer):
    rows, cols, channels = block.shape
    _, c, _ = place()
    padded[:, :EDGE, :] = jnp.zeros_like(padded[:, :EDGE, :])
    padded[:, EDGE + cols :, :] = jnp.zeros_like(padded[:, EDGE + cols :, :])
    middle = slice(EDGE, EDGE + cols)
    inner = inner.astype(WIDE).reshape(RIM, cols, channels)
    outer = outer.astype(WIDE).reshape(RIM, cols, channels)
    padded[:RIM, middle, :] = jnp.where(c == 0, outer, inner)
    padded[RIM : RIM + rows, middle, :] = block
    padded[RIM + rows :, middle, :] = jnp.where(c == 0, inner, outer)


def taps_sum(padded, kernel, lanes, rows, cols, mirrored, start):
    total = list(start)
    for tap_col in range(TAPS):
        for row in range(rows + TAPS - 1):
            line = padded[row, pl.ds(EDGE - RIM + tap_col, cols), lanes]
            for out in range(rows):
                tap_row = row - out
                if 0 <= tap_row < TAPS:
                    if mirrored:
                        tap = kernel[TAPS - 1 - tap_row, pl.ds(TAPS - 1 - tap_col, 1), lanes]
                    else:
                        tap = kernel[tap_row, pl.ds(tap_col, 1), lanes]
                    total[out] = total[out] + line * tap
    return total


def conv_body(
    feats, core_got, outer, kernel, gain, bias, normed, inv, narrow, padded, result
):
    rows, cols, channels = feats.shape
    start = core_got.shape[0] - RIM * cols
    fill(padded, feats[...], core_got[start:, :], outer[...])

    @pl.loop(0, channels // LANES)
    def _(step):
        lanes = pl.ds(pl.multiple_of(step * LANES, LANES), LANES)
        zero = [jnp.zeros((cols, LANES), WIDE)] * rows
        total = taps_sum(padded, kernel, lanes, rows, cols, False, zero)
        for row in range(rows):
            result[pl.ds(row * cols, cols), lanes] = total[row]

    value = result[...]
    centred = value - jnp.mean(value, axis=1, keepdims=True)
    spread = lax.rsqrt(jnp.mean(centred * centred, axis=1, keepdims=True) + 1e-06)
    value = centred * spread
    normed[...] = value
    inv[...] = jnp.broadcast_to(spread, inv.shape)
    narrow[...] = (value * gain[...] + bias[...]).astype(NARROW)


def hidden_body(copied, *refs):
    patterns = lax.axis_size("row") // 4
    me, _, _ = place()
    acts, in_bias = refs[:2], refs[2]
    pieces = refs[3:-7]
    keep, send, active, hidden, out_copy, bias_part, weights = refs[-7:]
    half = acts[0].shape[1]
    if copied:
        own = pieces[0].shape[2]
        group = lax.axis_index("grp")
        each = len(pieces) // 2
        for side in range(2):
            blocks = pieces[side * each : (side + 1) * each]
            for spot, block in enumerate(blocks):
                other = jnp.bitwise_xor(group, spot % 2)
                pattern = spot if spot < 2 else 2 * (spot // 2) + other
                for c in range(2):
                    device = jnp.bitwise_xor(me, 4 * pattern + 2 * side + c)
                    rows = pl.ds(pl.multiple_of(device * own, own), own)
                    for which in range(2):
                        weights[which, rows, :] = block[which, c]
    else:
        weights[...] = pieces[0][...]
    in_narrow = weights.at[0]
    out_narrow = weights.at[1]
    out_copy[...] = weights[1]
    bias_row = in_bias[...]
    total = jnp.zeros_like(bias_row)
    for side in (1, 0):
        preact = dot(acts[side][0], in_narrow[...], ((1,), (0,))) + bias_row
        act_grad = dot(acts[side][1], out_narrow[...], ((1,), (0,)))
        cdf = 0.5 * (1.0 + lax.erf(preact * 0.7071067811865476))
        rows = pl.ds(side * half, half)
        activated = (preact * cdf).astype(NARROW)
        active[rows, :] = activated
        slope = cdf + preact * jnp.exp(-0.5 * preact * preact) * 0.3989422804014327
        grad = act_grad * slope
        total = total + jnp.sum(grad, axis=0, keepdims=True)
        narrow = grad.astype(NARROW)
        hidden[rows, :] = narrow
        out_grad = dot(narrow, in_narrow[...], ((1,), (1,)))
        if side:
            send[...] = out_grad.astype(NARROW)
        else:
            keep[...] = out_grad
    bias_part[...] = total


def weight_body(norm_scale, *refs):
    acts, (active, hidden, out_narrow, scale) = refs[:2], refs[2:6]
    holder, keep, send, scale_part = refs[6:]
    half = acts[0].shape[1]
    first, second = pl.ds(0, half), pl.ds(half, half)
    for which, right in enumerate((hidden, active)):
        grad = dot(acts[0][which], right[first, :], ((0,), (0,)))
        grad = grad + dot(acts[1][which], right[second, :], ((0,), (0,)))
        holder[which] = norm_scale * grad
    total = jnp.zeros_like(scale_part)
    for side, rows in enumerate((first, second)):
        mixed = dot(active[rows, :], out_narrow[...], ((1,), (1,)))
        total = total + jnp.sum(mixed * acts[side][1].astype(WIDE), axis=0, keepdims=True)
        if side:
            send[...] = mixed.astype(NARROW)
        else:
            keep[...] = mixed
    scale_part[...] = total / scale[...]


def owners_body(turns, holder, after, *targets):
    me, _, _ = place()
    own = holder.shape[1] // lax.axis_size("row")
    for pattern, target in zip(turns, targets):
        for c in range(2):
            device = jnp.bitwise_xor(me, 2 * pattern + c)
            rows = pl.ds(pl.multiple_of(device * own, own), own)
            for which in range(2):
                start = (2 * c + which) * own
                target[start : start + own, :] = holder[which, rows, :].astype(target.dtype)
        if target.shape[0] > 4 * own:
            target[4 * own : 4 * own + SMALL_ROWS, :] = after[...].astype(target.dtype)
            rest = target.shape[0] - 4 * own - SMALL_ROWS
            target[4 * own + SMALL_ROWS :, :] = jnp.zeros((rest, target.shape[1]), target.dtype)


def fold_body(kept, got, stay, leave):
    size = stay.shape[0]
    stay[...] = kept[:size] + got[:size].astype(WIDE)
    leave[...] = (kept[size:] + got[size:].astype(WIDE)).astype(NARROW)


def conv_grad_body(norm_scale, *refs):
    kept, got, normed, inv, gain, feats, core_got, outer, scale, in_bias = refs[:10]
    grad, inner_out, rim_out, stay, leave, padded, small = refs[10:]
    rows, cols, channels = feats.shape
    me, c, _ = place()
    out_grad = kept[...] + got[...].astype(WIDE)
    value = normed[...]
    normed_grad = out_grad * gain[...]
    mean = jnp.mean(normed_grad, axis=1, keepdims=True)
    along = jnp.mean(normed_grad * value, axis=1, keepdims=True)
    result = inv[:, :1] * (normed_grad - mean - value * along)
    grad[...] = result
    pixels = rows * cols
    rim = RIM * cols
    rim_out[...] = jnp.where(c == 0, result[:rim], result[pixels - rim :]).astype(NARROW)
    inner_out[...] = jnp.where(c == 0, result[pixels - rim :], result[:rim]).astype(NARROW)
    fill(padded, feats[...], core_got[core_got.shape[0] - rim :, :], outer[...])

    def put(row, lanes, total):
        small[row // SMALL_ROWS, pl.ds(row % SMALL_ROWS, 1), lanes] = norm_scale * total

    @pl.loop(0, channels // LANES)
    def _(step):
        lanes = pl.ds(pl.multiple_of(step * LANES, LANES), LANES)
        own = [grad[pl.ds(row * cols, cols), lanes] for row in range(rows)]
        for tap_col in range(TAPS):
            totals = [jnp.zeros((8, LANES), WIDE)] * TAPS
            for row in range(rows + TAPS - 1):
                line = padded[row, pl.ds(EDGE - RIM + tap_col, cols), lanes]
                for out in range(rows):
                    tap_row = row - out
                    if 0 <= tap_row < TAPS:
                        product = line * own[out]
                        for part in range(cols // 8):
                            totals[tap_row] = totals[tap_row] + product[8 * part : 8 * part + 8]
            for tap_row in range(TAPS):
                total = jnp.sum(totals[tap_row], axis=0, keepdims=True)
                put(TAPS * tap_row + tap_col, lanes, total)

    everything = slice(None)
    row = TAPS * TAPS
    put(row, everything, jnp.sum(out_grad * value, axis=0, keepdims=True))
    put(row + 1, everything, jnp.sum(out_grad, axis=0, keepdims=True))
    put(row + 2, everything, scale[...])
    for part in range(4):
        own_part = jnp.where(lax.rem(me, 4) == part, 1.0, 0.0)
        put(row + 3 + part, everything, own_part * in_bias[...])
    stay[...] = small[c]
    leave[...] = small[1 - c]


def input_grad_body(grad, inner, outer, kernel, cotan, result, padded):
    rows, cols, channels = cotan.shape
    fill(padded, grad[...].reshape(cotan.shape), inner[...], outer[...])

    @pl.loop(0, channels // LANES)
    def _(step):
        lanes = pl.ds(pl.multiple_of(step * LANES, LANES), LANES)
        start = [cotan[row, :, lanes] for row in range(rows)]
        total = taps_sum(padded, kernel, lanes, rows, cols, True, start)
        for row in range(rows):
            result[row, :, lanes] = total[row]


def output_body(feats, scale, kept, got, result):
    mixed = kept[...] + got[...].astype(WIDE)
    result[...] = feats[...] + (scale[...] * mixed).reshape(feats.shape)


def total_body(turns, *refs):
    parts, sums = refs[: len(turns)], refs[len(turns) : -3]
    stay, leave, half = refs[-3:]
    own = stay.shape[2]
    for side in range(2):
        total = jnp.zeros(parts[0].shape, WIDE)
        for part, turn in zip(parts, turns):
            if turn % 2 == side:
                total = total + part[...].astype(WIDE)
        for which in range(2):
            stay[side, which] = total[which * own : (which + 1) * own]
        leave[2 * side * own : 2 * (side + 1) * own, :] = total[2 * own :]
    total = sums[0][...]
    for one in sums[1:]:
        total = total + one[...].astype(WIDE)
    half[...] = total
    leave[4 * own :, :] = total


def final_body(stay, got, half, *refs):
    in_grad, out_grad, kernel_grad, gain, bias, scale, in_bias, held = refs
    _, c, x = place()
    quarter = stay.shape[-1]
    own = stay.shape[2]
    for side in range(2):
        part = 2 * jnp.bitwise_xor(x, side)
        near = pl.ds(pl.multiple_of((part + c) * quarter, quarter), quarter)
        far = pl.ds(pl.multiple_of((part + 1 - c) * quarter, quarter), quarter)
        for which, target in enumerate((in_grad, out_grad)):
            start = (2 * side + which) * own
            target[:, near] = stay[side, which]
            target[:, far] = got[start : start + own, :]
    held[c] = half[...]
    held[1 - c] = got[4 * own :, :]

    def take(row):
        return held[row // SMALL_ROWS, pl.ds(row % SMALL_ROWS, 1), :]

    for tap_row in range(TAPS):
        for tap_col in range(TAPS):
            kernel_grad[tap_row, pl.ds(tap_col, 1), :] = take(TAPS * tap_row + tap_col)
    row = TAPS * TAPS
    gain[...] = take(row)
    bias[...] = take(row + 1)
    scale[...] = take(row + 2)
    for part in range(4):
        in_bias[:, pl.ds(part * quarter, quarter)] = take(row + 3 + part)


def flipped(blocks, axis, bit_set):
    return jnp.where(bit_set == 1, jnp.flip(blocks, axis), blocks)


def canonical(blocks, me, bit_count):
    tail = blocks.shape[1:]
    blocks = blocks.reshape((2,) * bit_count + tail)
    for spot in range(bit_count):
        blocks = flipped(blocks, bit_count - 1 - spot, (me >> spot) & 1)
    return blocks.reshape((2**bit_count,) + tail)


def per_device(
    features, cotangent, kernel, norm_gain, norm_bias, in_weight, in_bias, out_weight, layer_scale
):
    row_count, col_count, channels = features.shape
    own_rows, hidden_count = in_weight.shape
    pixels = row_count * col_count
    count = lax.axis_size("row")
    bit_count = count.bit_length() - 1
    me = lax.axis_index("row")
    group_index = lax.axis_index("grp")
    quarter = hidden_count // 4
    norm_scale = 1.0 / math.sqrt(pixels * count)
    patterns = count // 4
    copied = own_rows % 16 == 0
    gain_row = norm_gain.reshape(1, channels)
    bias_row = norm_bias.reshape(1, channels)
    scale_row = layer_scale.reshape(1, channels)
    rim = RIM * col_count
    padded = pltpu.VMEM((row_count + 2 * RIM, col_count + 2 * EDGE, channels), WIDE)

    piece = (2, own_rows, quarter)
    once = (features, cotangent, scale_row, kernel, gain_row, bias_row)
    own, core, outer, branch, in_bias_own, feats, cotan, scale, taps, gain, bias = run(
        split_body,
        (
            shaped((2,) + piece, NARROW),
            shaped((4 * own_rows + rim, channels), NARROW),
            shaped((rim, channels)),
            shaped((pixels, channels), NARROW),
            shaped((1, quarter)),
        )
        + tuple(shaped(x.shape) for x in once),
        in_weight,
        out_weight,
        in_bias.reshape(1, hidden_count),
        *once,
        scratch=(
            pltpu.VMEM(in_weight.shape, WIDE),
            pltpu.VMEM(out_weight.shape, WIDE),
            pltpu.VMEM((1, hidden_count), WIDE),
            pltpu.SemaphoreType.DMA((9,)),
        ),
        apart=True,
    )
    core_got = swap(core, 1)
    outer_got = swap_rim(outer)
    full_shape = shaped((2, 2, own_rows, quarter), NARROW)
    joined = run(
        join_body,
        (full_shape, full_shape, shaped((pixels + 4 * own_rows, channels), NARROW)),
        own,
        core_got,
        branch,
    )
    sent_got = swap(joined[2], 2)
    pieces = []
    for side, full in enumerate(joined[:2]):
        pieces += [full, swap(full, 4 + 2 * side)]
        for pair in range(1, patterns // 2):
            here = swap_far(full, pair, side)
            pieces += [here, swap_group(here)]
    each = len(pieces) // 2

    normed, inv, normed_out = run(
        conv_body,
        (
            shaped((pixels, channels)),
            shaped((pixels, LANES)),
            shaped((pixels, channels), NARROW),
        ),
        feats,
        core_got,
        outer_got,
        taps,
        gain,
        bias,
        scratch=(padded, pltpu.VMEM((pixels, channels), WIDE)),
    )
    first_blocks = [block for k, block in enumerate(pieces) if k % each]
    acts, pieces[each] = run(
        acts_body,
        (shaped((2, 2 * pixels, channels), NARROW), full_shape),
        normed_out,
        branch,
        swap(normed_out, 2),
        sent_got,
        *first_blocks,
    )
    acts_got = swap(acts, 1)

    if not copied:
        lines = []
        for pattern in range(patterns):
            for side in range(2):
                blocks = pieces[side * each : (side + 1) * each]
                if pattern < 2:
                    lines.append(blocks[pattern])
                else:
                    pair = jnp.stack(blocks[pattern - pattern % 2 : pattern - pattern % 2 + 2])
                    lines.append(flipped(pair, 0, group_index)[pattern % 2])
        lines = jnp.moveaxis(jnp.stack(lines), 1, 2).reshape(count, 2, own_rows, quarter)
        lines = jnp.moveaxis(canonical(lines, me, bit_count), 1, 0)
        pieces = [lines.reshape(2, channels, quarter)]
    group = 4 * pixels
    keep, send, active, hidden, out_narrow, in_bias_part = run(
        functools.partial(hidden_body, copied),
        (
            shaped((2 * pixels, channels)),
            shaped((2 * pixels, channels), NARROW),
            shaped((group, quarter), NARROW),
            shaped((group, quarter), NARROW),
            shaped((channels, quarter), NARROW),
            shaped((1, quarter)),
        ),
        acts,
        acts_got,
        in_bias_own,
        *pieces,
        scratch=(pltpu.VMEM((2, channels, quarter), NARROW),),
        mib=24,
    )
    half = (shaped((pixels, channels)), shaped((pixels, channels), NARROW))
    out_stay, out_leave = run(fold_body, half, keep, swap(send, 1))
    out_got = swap(out_leave, 2)

    holder, mixed_keep, mixed_send, scale_part = run(
        functools.partial(weight_body, norm_scale),
        (
            shaped((2, channels, quarter)),
            shaped((2 * pixels, channels)),
            shaped((2 * pixels, channels), NARROW),
            shaped((1, channels)),
        ),
        acts,
        acts_got,
        active,
        hidden,
        out_narrow,
        scale,
        mib=24,
    )
    conv_grad, inner_out, rim_out, stay, leave = run(
        functools.partial(conv_grad_body, norm_scale),
        (
            shaped((pixels, channels)),
            shaped((rim, channels), NARROW),
            shaped((rim, channels), NARROW),
            shaped((SMALL_ROWS, channels)),
            shaped((SMALL_ROWS, channels)),
        ),
        out_stay,
        out_got,
        normed,
        inv,
        gain,
        feats,
        core_got,
        outer_got,
        scale_part,
        in_bias_part,
        scratch=(padded, pltpu.VMEM((2, SMALL_ROWS, channels), WIDE)),
    )
    sums = stay + swap(leave, 1)

    far_turns = tuple(range(2 * patterns - 1, 4, -2))
    near_turns = (*range(4, 2 * patterns, 2), 2, 3, 1, 0)
    owned = 4 * own_rows
    if copied:
        parts = run(
            functools.partial(owners_body, far_turns),
            (shaped((owned, quarter), NARROW),) * len(far_turns),
            holder,
            out_leave,
        )
    else:
        flat = holder.reshape(2, count, own_rows, quarter)
        flat = canonical(jnp.moveaxis(flat, 1, 0), me, bit_count)
        flat = flat.reshape(2 * patterns, owned, quarter)
        parts = [flat[p].astype(NARROW) for p in far_turns]
    far_parts = [swap(part, 2 * p) for p, part in zip(far_turns, parts)]
    sums, far_parts[0] = lax.optimization_barrier((sums, far_parts[0]))
    sums = sums + swap(sums, 2)
    sums, far_parts = lax.optimization_barrier((sums, far_parts))
    joint = shaped((owned + 32, quarter), NARROW)
    plain = shaped((owned, quarter), NARROW)
    if copied:
        first_joint = run(
            functools.partial(owners_body, near_turns[:-4]),
            (joint,) * (len(near_turns) - 4),
            holder,
            sums,
        )
    rim_got = swap_rim(rim_out)
    inner_got = swap(inner_out, 1)
    mixed_stay, mixed_leave = run(fold_body, half, mixed_keep, swap(mixed_send, 1))
    mixed_got = swap(mixed_leave, 2)
    sums, rim_got, inner_got, mixed_got = lax.optimization_barrier(
        (sums, rim_got, inner_got, mixed_got)
    )
    if copied:
        next_joint, *plains, near_own = run(
            functools.partial(owners_body, near_turns[-4:]),
            (joint, plain, plain, shaped((owned, quarter))),
            holder,
            sums,
        )
        parts = [swap(part, 2 * p) for p, part in zip(near_turns, (*first_joint, next_joint))]
        sums_parts = [part[owned : owned + SMALL_ROWS] for part in parts]
        near_parts = [part[:owned] for part in parts]
        near_parts += [swap(plains[0], 6), swap(plains[1], 2), near_own]
    else:
        near_parts = [swap(flat[p].astype(NARROW), 2 * p) for p in near_turns[:-1]] + [flat[0]]
        sums_parts = [swap(sums.astype(NARROW), 2 * p) for p in near_turns[:-3]]
    input_grad = run(
        input_grad_body,
        (shaped(features.shape),),
        conv_grad,
        inner_got,
        rim_got,
        taps,
        cotan,
        scratch=(padded,),
    )[0]
    output = run(
        output_body,
        (shaped(features.shape),),
        feats,
        scale,
        mixed_stay,
        mixed_got,
    )[0]
    parts = list(far_parts) + near_parts
    parts, input_grad, output = lax.optimization_barrier((parts, input_grad, output))

    stay, leave, half_sums = run(
        functools.partial(total_body, far_turns + near_turns),
        (
            shaped((2, 2, own_rows, quarter)),
            shaped((owned + SMALL_ROWS, quarter)),
            shaped((SMALL_ROWS, channels)),
        ),
        *parts,
        sums,
        *sums_parts,
    )
    (
        in_weight_grad,
        out_weight_grad,
        kernel_grad,
        gain_grad,
        bias_grad,
        scale_grad,
        in_bias_grad,
    ) = run(
        final_body,
        (
            shaped((own_rows, hidden_count)),
            shaped((own_rows, hidden_count)),
            shaped(kernel.shape),
            shaped((1, channels)),
            shaped((1, channels)),
            shaped((1, channels)),
            shaped((1, hidden_count)),
        ),
        stay,
        swap(leave, 1),
        half_sums,
        scratch=(pltpu.VMEM((2, SMALL_ROWS, channels), WIDE),),
    )
    return (
        output,
        input_grad,
        in_weight_grad,
        out_weight_grad,
        kernel_grad,
        gain_grad.reshape(channels),
        bias_grad.reshape(channels),
        in_bias_grad.reshape(hidden_count),
        scale_grad.reshape(channels),
    )


def solution(mesh):
    return jax.shard_map(
        per_device,
        mesh=mesh,
        in_specs=(
            P(("grp", "row"), None, None),
            P(("grp", "row"), None, None),
            P(),
            P(),
            P(),
            P("row", None),
            P(),
            P("row", None),
            P(),
        ),
        out_specs=(
            P(("grp", "row"), None, None),
            P(("grp", "row"), None, None),
            P(("grp", "row"), None),
            P(("grp", "row"), None),
            P("grp", None, None),
            P("grp"),
            P("grp"),
            P("grp"),
            P("grp"),
        ),
        check_vma=False,
    )
```

```python
import functools
import math

import jax
import jax.numpy as jnp
from jax import lax
from jax.experimental import pallas as pl
from jax.experimental.pallas import tpu as pltpu
from jax.sharding import PartitionSpec as P

NARROW = jnp.bfloat16
WIDE = jnp.float32
TAPS = 7
RIM = 3
EDGE = 8
LANES = 128
SMALL_ROWS = 28


def swap(value, bit):
    count = lax.axis_size("row")
    return lax.ppermute(value, "row", [(i, i ^ bit) for i in range(count)])


def swap_rim(value):
    count = lax.axis_size("row")
    pairs = [(i, i + 1) for i in range(1, count - 1, 2)]
    return lax.ppermute(value, "row", pairs + [(j, i) for i, j in pairs])


def shaped(shape, dtype=WIDE):
    return jax.ShapeDtypeStruct(shape, dtype)


def swap_group(value):
    return lax.ppermute(value, "grp", [(0, 1), (1, 0)])


def run(body, outs, *operands, scratch=(), mib=16, order=0, apart=False):
    extra = {}
    if apart:
        extra = {"in_specs": [pl.BlockSpec(memory_space=pltpu.HBM)] * len(operands)}
        operands = [pltpu.with_memory_space_constraint(x, pltpu.HBM) for x in operands]
    return pl.pallas_call(
        body,
        out_shape=outs,
        **extra,
        scratch_shapes=scratch,
        compiler_params=pltpu.CompilerParams(vmem_limit_bytes=mib * 2**20),
        cost_estimate=pl.CostEstimate(flops=order * 10**9, bytes_accessed=0, transcendentals=0),
    )(*operands)


def place():
    me = lax.axis_index("row")
    return me, lax.rem(me, 2), lax.rem(lax.div(me, 2), 2)


def dot(left, right, dims):
    return lax.dot_general(left, right, (dims, ((), ())), preferred_element_type=WIDE)


def split_body(*refs):
    inw_hbm, outw_hbm, in_bias_hbm = refs[:3]
    own, core, outer, branch, bias_part = refs[9:14]
    inw, outw, in_bias, sems = refs[20:]
    feats, cotan, scale = refs[14:17]
    pairs = list(zip(refs[3:9], refs[14:20]))
    pairs += [(inw_hbm, inw), (outw_hbm, outw), (in_bias_hbm, in_bias)]
    copies = [pltpu.make_async_copy(a, b, sems.at[k]) for k, (a, b) in enumerate(pairs)]
    for copy in copies[6:] + copies[:6]:
        copy.start()
    me, c, x = place()
    even = c == 0
    quarter = own.shape[-1]
    rows, cols, channels = feats.shape
    own_rows = inw.shape[0]
    copies[6].wait()
    copies[7].wait()
    for side in range(2):
        for part, near in ((2 * jnp.bitwise_xor(x, side) + c, True), (2 * jnp.bitwise_xor(x, side) + 1 - c, False)):
            lanes = pl.ds(pl.multiple_of(part * quarter, quarter), quarter)
            for which, source in enumerate((inw, outw)):
                value = source[:, lanes].astype(NARROW)
                if near:
                    own[side, which] = value
                else:
                    core[pl.ds((2 * side + which) * own_rows, own_rows), :] = value
    copies[0].wait()
    first = feats[:RIM].astype(NARROW).reshape(RIM * cols, channels)
    last = feats[rows - RIM :].astype(NARROW).reshape(RIM * cols, channels)
    core[4 * own_rows :, :] = jnp.where(even, last, first)
    outer[...] = jnp.where(even, first, last)
    copies[1].wait()
    copies[2].wait()
    branch[...] = (scale[...] * cotan[...].reshape(branch.shape)).astype(NARROW)
    copies[8].wait()
    lanes = pl.ds(pl.multiple_of(lax.rem(me, 4) * quarter, quarter), quarter)
    bias_part[...] = in_bias[:, lanes]
    for copy in copies[3:6]:
        copy.wait()


def join_body(mine, other, *targets):
    group = lax.axis_index("grp")
    for side in range(2):
        full, sent = targets[2 * side : 2 * side + 2]
        own_rows = mine.shape[2]
        for which in range(2):
            full[which, 0] = mine[side, which]
            full[which, 1] = other[pl.ds((2 * side + which) * own_rows, own_rows), :]
        sent[...] = full[group]


def acts_body(mine, got, *refs):
    acts, full = refs[-2:]
    pixels = acts.shape[1] // 2
    for which in range(2):
        rows = slice(which * pixels, (which + 1) * pixels)
        acts[which, :pixels] = mine[rows, :]
        acts[which, pixels:] = got[rows, :]
        own = full.shape[2]
        for core in range(2):
            start = 2 * pixels + (2 * which + core) * own
            full[which, core] = got[start : start + own, :]


def stack_body(*refs):
    for place_in, ref in enumerate(refs[:-1]):
        refs[-1][place_in] = ref[...]


def fill(padded, block, inner, outer):
    rows, cols, channels = block.shape
    _, c, _ = place()
    padded[:, :EDGE, :] = jnp.zeros_like(padded[:, :EDGE, :])
    padded[:, EDGE + cols :, :] = jnp.zeros_like(padded[:, EDGE + cols :, :])
    middle = slice(EDGE, EDGE + cols)
    inner = inner.astype(WIDE).reshape(RIM, cols, channels)
    outer = outer.astype(WIDE).reshape(RIM, cols, channels)
    padded[:RIM, middle, :] = jnp.where(c == 0, outer, inner)
    padded[RIM : RIM + rows, middle, :] = block
    padded[RIM + rows :, middle, :] = jnp.where(c == 0, inner, outer)


def taps_sum(padded, kernel, lanes, rows, cols, mirrored, start):
    total = list(start)
    for tap_col in range(TAPS):
        for row in range(rows + TAPS - 1):
            line = padded[row, pl.ds(EDGE - RIM + tap_col, cols), lanes]
            for out in range(rows):
                tap_row = row - out
                if 0 <= tap_row < TAPS:
                    if mirrored:
                        tap = kernel[TAPS - 1 - tap_row, pl.ds(TAPS - 1 - tap_col, 1), lanes]
                    else:
                        tap = kernel[tap_row, pl.ds(tap_col, 1), lanes]
                    total[out] = total[out] + line * tap
    return total


def conv_body(
    feats, core_got, outer, kernel, gain, bias, branch, full, normed, inv, acts, padded, result
):
    rows, cols, channels = feats.shape
    start = core_got.shape[0] - RIM * cols
    fill(padded, feats[...], core_got[start:, :], outer[...])

    @pl.loop(0, channels // LANES)
    def _(step):
        lanes = pl.ds(pl.multiple_of(step * LANES, LANES), LANES)
        zero = [jnp.zeros((cols, LANES), WIDE)] * rows
        total = taps_sum(padded, kernel, lanes, rows, cols, False, zero)
        for row in range(rows):
            result[pl.ds(row * cols, cols), lanes] = total[row]

    value = result[...]
    centred = value - jnp.mean(value, axis=1, keepdims=True)
    spread = lax.rsqrt(jnp.mean(centred * centred, axis=1, keepdims=True) + 1e-06)
    value = centred * spread
    normed[...] = value
    inv[...] = jnp.broadcast_to(spread, inv.shape)
    pixels = rows * cols
    acts[:pixels, :] = (value * gain[...] + bias[...]).astype(NARROW)
    acts[pixels : 2 * pixels, :] = branch[...]
    own = full.shape[2]
    for which in range(2):
        for core in range(2):
            start = 2 * pixels + (2 * which + core) * own
            acts[start : start + own, :] = full[which, core]


def hidden_body(copied, *refs):
    patterns = lax.axis_size("row") // 4
    me, _, _ = place()
    acts, in_bias = refs[:2], refs[2]
    pieces = refs[3:-7]
    keep, send, active, hidden, out_copy, bias_part, weights = refs[-7:]
    half = acts[0].shape[1]
    if copied:
        own = pieces[0].shape[2]
        group = lax.axis_index("grp")
        for side in range(2):
            full, near, here, there = pieces[4 * side : 4 * side + 4]
            for pattern in range(patterns):
                for c in range(2):
                    device = jnp.bitwise_xor(me, 4 * pattern + 2 * side + c)
                    rows = pl.ds(pl.multiple_of(device * own, own), own)
                    if pattern < 2:
                        source = near if pattern else full
                        weights[0, rows, :] = source[0, c]
                        weights[1, rows, :] = source[1, c]
                    else:
                        weights[group, rows, :] = here[pattern - 2, c]
                        weights[1 - group, rows, :] = there[pattern - 2, c]
    else:
        weights[...] = pieces[0][...]
    in_narrow = weights.at[0]
    out_narrow = weights.at[1]
    out_copy[...] = weights[1]
    bias_row = in_bias[...]
    total = jnp.zeros_like(bias_row)
    for side in (1, 0):
        preact = dot(acts[side][0], in_narrow[...], ((1,), (0,))) + bias_row
        act_grad = dot(acts[side][1], out_narrow[...], ((1,), (0,)))
        cdf = 0.5 * (1.0 + lax.erf(preact * 0.7071067811865476))
        rows = pl.ds(side * half, half)
        activated = (preact * cdf).astype(NARROW)
        active[rows, :] = activated
        slope = cdf + preact * jnp.exp(-0.5 * preact * preact) * 0.3989422804014327
        grad = act_grad * slope
        total = total + jnp.sum(grad, axis=0, keepdims=True)
        narrow = grad.astype(NARROW)
        hidden[rows, :] = narrow
        out_grad = dot(narrow, in_narrow[...], ((1,), (1,)))
        if side:
            send[...] = out_grad.astype(NARROW)
        else:
            keep[...] = out_grad
    bias_part[...] = total


def weight_body(norm_scale, *refs):
    acts, (active, hidden, out_narrow, scale) = refs[:2], refs[2:6]
    holder, keep, send, scale_part = refs[6:]
    half = acts[0].shape[1]
    first, second = pl.ds(0, half), pl.ds(half, half)
    for which, right in enumerate((hidden, active)):
        grad = dot(acts[0][which], right[first, :], ((0,), (0,)))
        grad = grad + dot(acts[1][which], right[second, :], ((0,), (0,)))
        holder[which] = norm_scale * grad
    total = jnp.zeros_like(scale_part)
    for side, rows in enumerate((first, second)):
        mixed = dot(active[rows, :], out_narrow[...], ((1,), (1,)))
        total = total + jnp.sum(mixed * acts[side][1].astype(WIDE), axis=0, keepdims=True)
        if side:
            send[...] = mixed.astype(NARROW)
        else:
            keep[...] = mixed
    scale_part[...] = total / scale[...]


def owners_body(turns, holder, after, *targets):
    me, _, _ = place()
    own = holder.shape[1] // lax.axis_size("row")
    for pattern, target in zip(turns, targets):
        for c in range(2):
            device = jnp.bitwise_xor(me, 2 * pattern + c)
            rows = pl.ds(pl.multiple_of(device * own, own), own)
            for which in range(2):
                start = (2 * c + which) * own
                target[start : start + own, :] = holder[which, rows, :].astype(target.dtype)
        if target.shape[0] > 4 * own:
            target[4 * own : 4 * own + SMALL_ROWS, :] = after[...].astype(target.dtype)
            rest = target.shape[0] - 4 * own - SMALL_ROWS
            target[4 * own + SMALL_ROWS :, :] = jnp.zeros((rest, target.shape[1]), target.dtype)


def fold_body(kept, got, stay, leave):
    size = stay.shape[0]
    stay[...] = kept[:size] + got[:size].astype(WIDE)
    leave[...] = (kept[size:] + got[size:].astype(WIDE)).astype(NARROW)


def conv_grad_body(norm_scale, *refs):
    kept, got, normed, inv, gain, feats, core_got, outer, scale, in_bias = refs[:10]
    grad, inner_out, rim_out, stay, leave, padded, small = refs[10:]
    rows, cols, channels = feats.shape
    me, c, _ = place()
    out_grad = kept[...] + got[...].astype(WIDE)
    value = normed[...]
    normed_grad = out_grad * gain[...]
    mean = jnp.mean(normed_grad, axis=1, keepdims=True)
    along = jnp.mean(normed_grad * value, axis=1, keepdims=True)
    result = inv[:, :1] * (normed_grad - mean - value * along)
    grad[...] = result
    pixels = rows * cols
    rim = RIM * cols
    rim_out[...] = jnp.where(c == 0, result[:rim], result[pixels - rim :]).astype(NARROW)
    inner_out[...] = jnp.where(c == 0, result[pixels - rim :], result[:rim]).astype(NARROW)
    fill(padded, feats[...], core_got[core_got.shape[0] - rim :, :], outer[...])

    def put(row, lanes, total):
        small[row // SMALL_ROWS, pl.ds(row % SMALL_ROWS, 1), lanes] = norm_scale * total

    @pl.loop(0, channels // LANES)
    def _(step):
        lanes = pl.ds(pl.multiple_of(step * LANES, LANES), LANES)
        own = [grad[pl.ds(row * cols, cols), lanes] for row in range(rows)]
        for tap_col in range(TAPS):
            totals = [jnp.zeros((8, LANES), WIDE)] * TAPS
            for row in range(rows + TAPS - 1):
                line = padded[row, pl.ds(EDGE - RIM + tap_col, cols), lanes]
                for out in range(rows):
                    tap_row = row - out
                    if 0 <= tap_row < TAPS:
                        product = line * own[out]
                        for part in range(cols // 8):
                            totals[tap_row] = totals[tap_row] + product[8 * part : 8 * part + 8]
            for tap_row in range(TAPS):
                total = jnp.sum(totals[tap_row], axis=0, keepdims=True)
                put(TAPS * tap_row + tap_col, lanes, total)

    everything = slice(None)
    row = TAPS * TAPS
    put(row, everything, jnp.sum(out_grad * value, axis=0, keepdims=True))
    put(row + 1, everything, jnp.sum(out_grad, axis=0, keepdims=True))
    put(row + 2, everything, scale[...])
    for part in range(4):
        own_part = jnp.where(lax.rem(me, 4) == part, 1.0, 0.0)
        put(row + 3 + part, everything, own_part * in_bias[...])
    stay[...] = small[c]
    leave[...] = small[1 - c]


def input_grad_body(grad, inner, outer, kernel, cotan, result, padded):
    rows, cols, channels = cotan.shape
    fill(padded, grad[...].reshape(cotan.shape), inner[...], outer[...])

    @pl.loop(0, channels // LANES)
    def _(step):
        lanes = pl.ds(pl.multiple_of(step * LANES, LANES), LANES)
        start = [cotan[row, :, lanes] for row in range(rows)]
        total = taps_sum(padded, kernel, lanes, rows, cols, True, start)
        for row in range(rows):
            result[row, :, lanes] = total[row]


def output_body(feats, scale, kept, got, result):
    mixed = kept[...] + got[...].astype(WIDE)
    result[...] = feats[...] + (scale[...] * mixed).reshape(feats.shape)


def total_body(turns, *refs):
    parts, sums = refs[: len(turns)], refs[len(turns) : -3]
    stay, leave, half = refs[-3:]
    own = stay.shape[2]
    for side in range(2):
        total = jnp.zeros(parts[0].shape, WIDE)
        for part, turn in zip(parts, turns):
            if turn % 2 == side:
                total = total + part[...].astype(WIDE)
        for which in range(2):
            stay[side, which] = total[which * own : (which + 1) * own]
        leave[2 * side * own : 2 * (side + 1) * own, :] = total[2 * own :]
    total = sums[0][...]
    for one in sums[1:]:
        total = total + one[...].astype(WIDE)
    half[...] = total
    leave[4 * own :, :] = total


def final_body(stay, got, half, *refs):
    in_grad, out_grad, kernel_grad, gain, bias, scale, in_bias, held = refs
    _, c, x = place()
    quarter = stay.shape[-1]
    own = stay.shape[2]
    for side in range(2):
        part = 2 * jnp.bitwise_xor(x, side)
        near = pl.ds(pl.multiple_of((part + c) * quarter, quarter), quarter)
        far = pl.ds(pl.multiple_of((part + 1 - c) * quarter, quarter), quarter)
        for which, target in enumerate((in_grad, out_grad)):
            start = (2 * side + which) * own
            target[:, near] = stay[side, which]
            target[:, far] = got[start : start + own, :]
    held[c] = half[...]
    held[1 - c] = got[4 * own :, :]

    def take(row):
        return held[row // SMALL_ROWS, pl.ds(row % SMALL_ROWS, 1), :]

    for tap_row in range(TAPS):
        for tap_col in range(TAPS):
            kernel_grad[tap_row, pl.ds(tap_col, 1), :] = take(TAPS * tap_row + tap_col)
    row = TAPS * TAPS
    gain[...] = take(row)
    bias[...] = take(row + 1)
    scale[...] = take(row + 2)
    for part in range(4):
        in_bias[:, pl.ds(part * quarter, quarter)] = take(row + 3 + part)


def flipped(blocks, axis, bit_set):
    return jnp.where(bit_set == 1, jnp.flip(blocks, axis), blocks)


def canonical(blocks, me, bit_count):
    tail = blocks.shape[1:]
    blocks = blocks.reshape((2,) * bit_count + tail)
    for spot in range(bit_count):
        blocks = flipped(blocks, bit_count - 1 - spot, (me >> spot) & 1)
    return blocks.reshape((2**bit_count,) + tail)


def per_device(
    features, cotangent, kernel, norm_gain, norm_bias, in_weight, in_bias, out_weight, layer_scale
):
    row_count, col_count, channels = features.shape
    own_rows, hidden_count = in_weight.shape
    pixels = row_count * col_count
    count = lax.axis_size("row")
    bit_count = count.bit_length() - 1
    me = lax.axis_index("row")
    group_index = lax.axis_index("grp")
    quarter = hidden_count // 4
    norm_scale = 1.0 / math.sqrt(pixels * count)
    patterns = count // 4
    copied = own_rows % 16 == 0
    gain_row = norm_gain.reshape(1, channels)
    bias_row = norm_bias.reshape(1, channels)
    scale_row = layer_scale.reshape(1, channels)
    rim = RIM * col_count
    padded = pltpu.VMEM((row_count + 2 * RIM, col_count + 2 * EDGE, channels), WIDE)

    piece = (2, own_rows, quarter)
    once = (features, cotangent, scale_row, kernel, gain_row, bias_row)
    own, core, outer, branch, in_bias_own, feats, cotan, scale, taps, gain, bias = run(
        split_body,
        (
            shaped((2,) + piece, NARROW),
            shaped((4 * own_rows + rim, channels), NARROW),
            shaped((rim, channels), NARROW),
            shaped((pixels, channels), NARROW),
            shaped((1, quarter)),
        )
        + tuple(shaped(x.shape) for x in once),
        in_weight,
        out_weight,
        in_bias.reshape(1, hidden_count),
        *once,
        scratch=(
            pltpu.VMEM(in_weight.shape, WIDE),
            pltpu.VMEM(out_weight.shape, WIDE),
            pltpu.VMEM((1, hidden_count), WIDE),
            pltpu.SemaphoreType.DMA((9,)),
        ),
        apart=True,
    )
    core_got = swap(core, 1)
    outer_got = swap_rim(outer)
    full_shape = shaped((2, 2, own_rows, quarter), NARROW)
    joined = run(
        join_body,
        (full_shape, shaped(piece, NARROW)) * 2,
        own,
        core_got,
    )
    pieces = []
    for side in range(2):
        full, sent = joined[2 * side : 2 * side + 2]
        here = [swap(sent, 4 * p + 2 * side) for p in range(2, patterns)]
        here = run(stack_body, (shaped((patterns - 2,) + piece, NARROW),), *here, order=8)[0]
        near = swap(full, 4 + 2 * side)
        pieces += [full, near, here, swap_group(here)]

    normed, inv, sent = run(
        conv_body,
        (
            shaped((pixels, channels)),
            shaped((pixels, LANES)),
            shaped((2 * pixels + 4 * own_rows, channels), NARROW),
        ),
        feats,
        core_got,
        outer_got,
        taps,
        gain,
        bias,
        branch,
        joined[2],
        scratch=(padded, pltpu.VMEM((pixels, channels), WIDE)),
    )
    first_blocks = [pieces[k] for k in (1, 3, 5, 7)]
    acts, pieces[4] = run(
        acts_body,
        (shaped((2, 2 * pixels, channels), NARROW), full_shape),
        sent,
        swap(sent, 2),
        *first_blocks,
    )
    acts_got = swap(acts, 1)

    if not copied:
        lines = []
        for pattern in range(patterns):
            for side in range(2):
                full, near, here, there = pieces[4 * side : 4 * side + 4]
                if pattern < 2:
                    lines.append(near if pattern else full)
                else:
                    pair = jnp.stack([here[pattern - 2], there[pattern - 2]])
                    lines.append(flipped(pair, 0, group_index))
        lines = jnp.moveaxis(jnp.stack(lines), 1, 2).reshape(count, 2, own_rows, quarter)
        lines = jnp.moveaxis(canonical(lines, me, bit_count), 1, 0)
        pieces = [lines.reshape(2, channels, quarter)]
    group = 4 * pixels
    keep, send, active, hidden, out_narrow, in_bias_part = run(
        functools.partial(hidden_body, copied),
        (
            shaped((2 * pixels, channels)),
            shaped((2 * pixels, channels), NARROW),
            shaped((group, quarter), NARROW),
            shaped((group, quarter), NARROW),
            shaped((channels, quarter), NARROW),
            shaped((1, quarter)),
        ),
        acts,
        acts_got,
        in_bias_own,
        *pieces,
        scratch=(pltpu.VMEM((2, channels, quarter), NARROW),),
        mib=24,
    )
    half = (shaped((pixels, channels)), shaped((pixels, channels), NARROW))
    out_stay, out_leave = run(fold_body, half, keep, swap(send, 1))
    out_got = swap(out_leave, 2)

    holder, mixed_keep, mixed_send, scale_part = run(
        functools.partial(weight_body, norm_scale),
        (
            shaped((2, channels, quarter)),
            shaped((2 * pixels, channels)),
            shaped((2 * pixels, channels), NARROW),
            shaped((1, channels)),
        ),
        acts,
        acts_got,
        active,
        hidden,
        out_narrow,
        scale,
        mib=24,
    )
    conv_grad, inner_out, rim_out, stay, leave = run(
        functools.partial(conv_grad_body, norm_scale),
        (
            shaped((pixels, channels)),
            shaped((rim, channels), NARROW),
            shaped((rim, channels), NARROW),
            shaped((SMALL_ROWS, channels)),
            shaped((SMALL_ROWS, channels)),
        ),
        out_stay,
        out_got,
        normed,
        inv,
        gain,
        feats,
        core_got,
        outer_got,
        scale_part,
        in_bias_part,
        scratch=(padded, pltpu.VMEM((2, SMALL_ROWS, channels), WIDE)),
    )
    rim_got = swap_rim(rim_out)
    inner_got = swap(inner_out, 1)
    sums = stay + swap(leave, 1)

    first_turns = (*range(2 * patterns - 2, 3, -2), 2)
    next_turns = (*range(2 * patterns - 1, 4, -2), 3, 1, 0)
    owned = 4 * own_rows
    if copied:
        parts = run(
            functools.partial(owners_body, first_turns),
            (shaped((owned, quarter), NARROW),) * len(first_turns),
            holder,
            out_leave,
        )
    else:
        flat = holder.reshape(2, count, own_rows, quarter)
        flat = canonical(jnp.moveaxis(flat, 1, 0), me, bit_count)
        flat = flat.reshape(2 * patterns, owned, quarter)
        parts = [flat[p].astype(NARROW) for p in first_turns]
    first_parts = [swap(part, 2 * p) for p, part in zip(first_turns, parts)]
    sums, first_parts = lax.optimization_barrier((sums, first_parts))
    sums = sums + swap(sums, 2)
    sums, mixed_send, rim_got, inner_got = lax.optimization_barrier(
        (sums, mixed_send, rim_got, inner_got)
    )
    mixed_stay, mixed_leave = run(fold_body, half, mixed_keep, swap(mixed_send, 1))
    if copied:
        joint = shaped((owned + 32, quarter), NARROW)
        *parts, side_part, near_own = run(
            functools.partial(owners_body, next_turns),
            (joint,) * (len(next_turns) - 2)
            + (shaped((owned, quarter), NARROW), shaped((owned, quarter))),
            holder,
            sums,
        )
        parts = [swap(part, 2 * p) for p, part in zip(next_turns, parts)]
        sums_parts = [part[owned : owned + SMALL_ROWS] for part in parts]
        next_parts = [part[:owned] for part in parts] + [swap(side_part, 2), near_own]
    else:
        next_parts = [swap(flat[p].astype(NARROW), 2 * p) for p in next_turns[:-1]] + [flat[0]]
        sums_parts = [swap(sums.astype(NARROW), 2 * p) for p in next_turns[:-2]]

    input_grad = run(
        input_grad_body,
        (shaped(features.shape),),
        conv_grad,
        inner_got,
        rim_got,
        taps,
        cotan,
        scratch=(padded,),
    )[0]
    output = run(
        output_body,
        (shaped(features.shape),),
        feats,
        scale,
        mixed_stay,
        swap(mixed_leave, 2),
    )[0]
    parts = list(first_parts) + next_parts
    parts, input_grad, output = lax.optimization_barrier((parts, input_grad, output))

    stay, leave, half_sums = run(
        functools.partial(total_body, first_turns + next_turns),
        (
            shaped((2, 2, own_rows, quarter)),
            shaped((owned + SMALL_ROWS, quarter)),
            shaped((SMALL_ROWS, channels)),
        ),
        *parts,
        sums,
        *sums_parts,
    )
    (
        in_weight_grad,
        out_weight_grad,
        kernel_grad,
        gain_grad,
        bias_grad,
        scale_grad,
        in_bias_grad,
    ) = run(
        final_body,
        (
            shaped((own_rows, hidden_count)),
            shaped((own_rows, hidden_count)),
            shaped(kernel.shape),
            shaped((1, channels)),
            shaped((1, channels)),
            shaped((1, channels)),
            shaped((1, hidden_count)),
        ),
        stay,
        swap(leave, 1),
        half_sums,
        scratch=(pltpu.VMEM((2, SMALL_ROWS, channels), WIDE),),
    )
    return (
        output,
        input_grad,
        in_weight_grad,
        out_weight_grad,
        kernel_grad,
        gain_grad.reshape(channels),
        bias_grad.reshape(channels),
        in_bias_grad.reshape(hidden_count),
        scale_grad.reshape(channels),
    )


def solution(mesh):
    return jax.shard_map(
        per_device,
        mesh=mesh,
        in_specs=(
            P(("grp", "row"), None, None),
            P(("grp", "row"), None, None),
            P(),
            P(),
            P(),
            P("row", None),
            P(),
            P("row", None),
            P(),
        ),
        out_specs=(
            P(("grp", "row"), None, None),
            P(("grp", "row"), None, None),
            P(("grp", "row"), None),
            P(("grp", "row"), None),
            P("grp", None, None),
            P("grp"),
            P("grp"),
            P("grp"),
            P("grp"),
        ),
        check_vma=False,
    )
```

```python
import functools
import math

import jax
import jax.numpy as jnp
from jax import lax
from jax.experimental import pallas as pl
from jax.experimental.pallas import tpu as pltpu
from jax.sharding import PartitionSpec as P

NARROW = jnp.bfloat16
WIDE = jnp.float32
TAPS = 7
RIM = 3
EDGE = 8
LANES = 128
SMALL_ROWS = 28


def swap(value, bit):
    count = lax.axis_size("row")
    return lax.ppermute(value, "row", [(i, i ^ bit) for i in range(count)])


def swap_rim(value):
    count = lax.axis_size("row")
    pairs = [(i, i + 1) for i in range(1, count - 1, 2)]
    return lax.ppermute(value, "row", pairs + [(j, i) for i, j in pairs])


def shaped(shape, dtype=WIDE):
    return jax.ShapeDtypeStruct(shape, dtype)


def swap_group(value):
    return lax.ppermute(value, "grp", [(0, 1), (1, 0)])


def run(body, outs, *operands, scratch=(), mib=16, order=0, apart=False):
    extra = {}
    if apart:
        extra = {"in_specs": [pl.BlockSpec(memory_space=pltpu.HBM)] * len(operands)}
        operands = [pltpu.with_memory_space_constraint(x, pltpu.HBM) for x in operands]
    return pl.pallas_call(
        body,
        out_shape=outs,
        **extra,
        scratch_shapes=scratch,
        compiler_params=pltpu.CompilerParams(vmem_limit_bytes=mib * 2**20),
        cost_estimate=pl.CostEstimate(flops=order * 10**9, bytes_accessed=0, transcendentals=0),
    )(*operands)


def place():
    me = lax.axis_index("row")
    return me, lax.rem(me, 2), lax.rem(lax.div(me, 2), 2)


def dot(left, right, dims):
    return lax.dot_general(left, right, (dims, ((), ())), preferred_element_type=WIDE)


def split_body(*refs):
    inw_hbm, outw_hbm, in_bias_hbm = refs[:3]
    own, core, outer, branch, bias_part = refs[9:14]
    inw, outw, in_bias, sems = refs[20:]
    feats, cotan, scale = refs[14:17]
    pairs = list(zip(refs[3:9], refs[14:20]))
    pairs += [(inw_hbm, inw), (outw_hbm, outw), (in_bias_hbm, in_bias)]
    copies = [pltpu.make_async_copy(a, b, sems.at[k]) for k, (a, b) in enumerate(pairs)]
    for copy in copies[6:] + copies[:6]:
        copy.start()
    me, c, x = place()
    even = c == 0
    quarter = own.shape[-1]
    rows, cols, channels = feats.shape
    own_rows = inw.shape[0]
    copies[6].wait()
    copies[7].wait()
    for side in range(2):
        for part, near in ((2 * jnp.bitwise_xor(x, side) + c, True), (2 * jnp.bitwise_xor(x, side) + 1 - c, False)):
            lanes = pl.ds(pl.multiple_of(part * quarter, quarter), quarter)
            for which, source in enumerate((inw, outw)):
                value = source[:, lanes].astype(NARROW)
                if near:
                    own[side, which] = value
                else:
                    core[pl.ds((2 * side + which) * own_rows, own_rows), :] = value
    copies[0].wait()
    first = feats[:RIM].astype(NARROW).reshape(RIM * cols, channels)
    last = feats[rows - RIM :].astype(NARROW).reshape(RIM * cols, channels)
    core[4 * own_rows :, :] = jnp.where(even, last, first)
    outer[...] = jnp.where(even, first, last)
    copies[1].wait()
    copies[2].wait()
    branch[...] = (scale[...] * cotan[...].reshape(branch.shape)).astype(NARROW)
    copies[8].wait()
    lanes = pl.ds(pl.multiple_of(lax.rem(me, 4) * quarter, quarter), quarter)
    bias_part[...] = in_bias[:, lanes]
    for copy in copies[3:6]:
        copy.wait()


def join_body(mine, other, *targets):
    group = lax.axis_index("grp")
    for side in range(2):
        full, sent = targets[2 * side : 2 * side + 2]
        own_rows = mine.shape[2]
        for which in range(2):
            full[which, 0] = mine[side, which]
            full[which, 1] = other[pl.ds((2 * side + which) * own_rows, own_rows), :]
        sent[...] = full[group]


def acts_body(mine, got, *refs):
    acts, full = refs[-2:]
    pixels = acts.shape[1] // 2
    for which in range(2):
        rows = slice(which * pixels, (which + 1) * pixels)
        acts[which, :pixels] = mine[rows, :]
        acts[which, pixels:] = got[rows, :]
        own = full.shape[2]
        for core in range(2):
            start = 2 * pixels + (2 * which + core) * own
            full[which, core] = got[start : start + own, :]


def stack_body(*refs):
    for place_in, ref in enumerate(refs[:-1]):
        refs[-1][place_in] = ref[...]


def fill(padded, block, inner, outer):
    rows, cols, channels = block.shape
    _, c, _ = place()
    padded[:, :EDGE, :] = jnp.zeros_like(padded[:, :EDGE, :])
    padded[:, EDGE + cols :, :] = jnp.zeros_like(padded[:, EDGE + cols :, :])
    middle = slice(EDGE, EDGE + cols)
    inner = inner.astype(WIDE).reshape(RIM, cols, channels)
    outer = outer.astype(WIDE).reshape(RIM, cols, channels)
    padded[:RIM, middle, :] = jnp.where(c == 0, outer, inner)
    padded[RIM : RIM + rows, middle, :] = block
    padded[RIM + rows :, middle, :] = jnp.where(c == 0, inner, outer)


def taps_sum(padded, kernel, lanes, rows, cols, mirrored, start):
    total = list(start)
    for tap_col in range(TAPS):
        for row in range(rows + TAPS - 1):
            line = padded[row, pl.ds(EDGE - RIM + tap_col, cols), lanes]
            for out in range(rows):
                tap_row = row - out
                if 0 <= tap_row < TAPS:
                    if mirrored:
                        tap = kernel[TAPS - 1 - tap_row, pl.ds(TAPS - 1 - tap_col, 1), lanes]
                    else:
                        tap = kernel[tap_row, pl.ds(tap_col, 1), lanes]
                    total[out] = total[out] + line * tap
    return total


def conv_body(
    feats, core_got, outer, kernel, gain, bias, branch, full, normed, inv, acts, padded, result
):
    rows, cols, channels = feats.shape
    start = core_got.shape[0] - RIM * cols
    fill(padded, feats[...], core_got[start:, :], outer[...])

    @pl.loop(0, channels // LANES)
    def _(step):
        lanes = pl.ds(pl.multiple_of(step * LANES, LANES), LANES)
        zero = [jnp.zeros((cols, LANES), WIDE)] * rows
        total = taps_sum(padded, kernel, lanes, rows, cols, False, zero)
        for row in range(rows):
            result[pl.ds(row * cols, cols), lanes] = total[row]

    value = result[...]
    centred = value - jnp.mean(value, axis=1, keepdims=True)
    spread = lax.rsqrt(jnp.mean(centred * centred, axis=1, keepdims=True) + 1e-06)
    value = centred * spread
    normed[...] = value
    inv[...] = jnp.broadcast_to(spread, inv.shape)
    pixels = rows * cols
    acts[:pixels, :] = (value * gain[...] + bias[...]).astype(NARROW)
    acts[pixels : 2 * pixels, :] = branch[...]
    own = full.shape[2]
    for which in range(2):
        for core in range(2):
            start = 2 * pixels + (2 * which + core) * own
            acts[start : start + own, :] = full[which, core]


def hidden_body(copied, *refs):
    patterns = lax.axis_size("row") // 4
    me, _, _ = place()
    acts, in_bias = refs[:2], refs[2]
    pieces = refs[3:-7]
    keep, send, active, hidden, out_copy, bias_part, weights = refs[-7:]
    half = acts[0].shape[1]
    if copied:
        own = pieces[0].shape[2]
        group = lax.axis_index("grp")
        for side in range(2):
            full, near, here, there = pieces[4 * side : 4 * side + 4]
            for pattern in range(patterns):
                for c in range(2):
                    device = jnp.bitwise_xor(me, 4 * pattern + 2 * side + c)
                    rows = pl.ds(pl.multiple_of(device * own, own), own)
                    if pattern < 2:
                        source = near if pattern else full
                        weights[0, rows, :] = source[0, c]
                        weights[1, rows, :] = source[1, c]
                    else:
                        weights[group, rows, :] = here[pattern - 2, c]
                        weights[1 - group, rows, :] = there[pattern - 2, c]
    else:
        weights[...] = pieces[0][...]
    in_narrow = weights.at[0]
    out_narrow = weights.at[1]
    out_copy[...] = weights[1]
    bias_row = in_bias[...]
    total = jnp.zeros_like(bias_row)
    for side in (1, 0):
        preact = dot(acts[side][0], in_narrow[...], ((1,), (0,))) + bias_row
        act_grad = dot(acts[side][1], out_narrow[...], ((1,), (0,)))
        cdf = 0.5 * (1.0 + lax.erf(preact * 0.7071067811865476))
        rows = pl.ds(side * half, half)
        activated = (preact * cdf).astype(NARROW)
        active[rows, :] = activated
        slope = cdf + preact * jnp.exp(-0.5 * preact * preact) * 0.3989422804014327
        grad = act_grad * slope
        total = total + jnp.sum(grad, axis=0, keepdims=True)
        narrow = grad.astype(NARROW)
        hidden[rows, :] = narrow
        out_grad = dot(narrow, in_narrow[...], ((1,), (1,)))
        if side:
            send[...] = out_grad.astype(NARROW)
        else:
            keep[...] = out_grad
    bias_part[...] = total


def weight_body(norm_scale, *refs):
    acts, (active, hidden, out_narrow, scale) = refs[:2], refs[2:6]
    holder, keep, send, scale_part = refs[6:]
    half = acts[0].shape[1]
    first, second = pl.ds(0, half), pl.ds(half, half)
    for which, right in enumerate((hidden, active)):
        grad = dot(acts[0][which], right[first, :], ((0,), (0,)))
        grad = grad + dot(acts[1][which], right[second, :], ((0,), (0,)))
        holder[which] = norm_scale * grad
    total = jnp.zeros_like(scale_part)
    for side, rows in enumerate((first, second)):
        mixed = dot(active[rows, :], out_narrow[...], ((1,), (1,)))
        total = total + jnp.sum(mixed * acts[side][1].astype(WIDE), axis=0, keepdims=True)
        if side:
            send[...] = mixed.astype(NARROW)
        else:
            keep[...] = mixed
    scale_part[...] = total / scale[...]


def owners_body(turns, holder, after, *targets):
    me, _, _ = place()
    own = holder.shape[1] // lax.axis_size("row")
    for pattern, target in zip(turns, targets):
        for c in range(2):
            device = jnp.bitwise_xor(me, 2 * pattern + c)
            rows = pl.ds(pl.multiple_of(device * own, own), own)
            for which in range(2):
                start = (2 * c + which) * own
                target[start : start + own, :] = holder[which, rows, :].astype(target.dtype)
        if target.shape[0] > 4 * own:
            target[4 * own : 4 * own + SMALL_ROWS, :] = after[...].astype(target.dtype)
            rest = target.shape[0] - 4 * own - SMALL_ROWS
            target[4 * own + SMALL_ROWS :, :] = jnp.zeros((rest, target.shape[1]), target.dtype)


def fold_body(kept, got, stay, leave):
    size = stay.shape[0]
    stay[...] = kept[:size] + got[:size].astype(WIDE)
    leave[...] = (kept[size:] + got[size:].astype(WIDE)).astype(NARROW)


def conv_grad_body(norm_scale, *refs):
    kept, got, normed, inv, gain, feats, core_got, outer, scale, in_bias = refs[:10]
    grad, inner_out, rim_out, stay, leave, padded, small = refs[10:]
    rows, cols, channels = feats.shape
    me, c, _ = place()
    out_grad = kept[...] + got[...].astype(WIDE)
    value = normed[...]
    normed_grad = out_grad * gain[...]
    mean = jnp.mean(normed_grad, axis=1, keepdims=True)
    along = jnp.mean(normed_grad * value, axis=1, keepdims=True)
    result = inv[:, :1] * (normed_grad - mean - value * along)
    grad[...] = result
    pixels = rows * cols
    rim = RIM * cols
    rim_out[...] = jnp.where(c == 0, result[:rim], result[pixels - rim :]).astype(NARROW)
    inner_out[...] = jnp.where(c == 0, result[pixels - rim :], result[:rim]).astype(NARROW)
    fill(padded, feats[...], core_got[core_got.shape[0] - rim :, :], outer[...])

    def put(row, lanes, total):
        small[row // SMALL_ROWS, pl.ds(row % SMALL_ROWS, 1), lanes] = norm_scale * total

    @pl.loop(0, channels // LANES)
    def _(step):
        lanes = pl.ds(pl.multiple_of(step * LANES, LANES), LANES)
        own = [grad[pl.ds(row * cols, cols), lanes] for row in range(rows)]
        for tap_col in range(TAPS):
            totals = [jnp.zeros((8, LANES), WIDE)] * TAPS
            for row in range(rows + TAPS - 1):
                line = padded[row, pl.ds(EDGE - RIM + tap_col, cols), lanes]
                for out in range(rows):
                    tap_row = row - out
                    if 0 <= tap_row < TAPS:
                        product = line * own[out]
                        for part in range(cols // 8):
                            totals[tap_row] = totals[tap_row] + product[8 * part : 8 * part + 8]
            for tap_row in range(TAPS):
                total = jnp.sum(totals[tap_row], axis=0, keepdims=True)
                put(TAPS * tap_row + tap_col, lanes, total)

    everything = slice(None)
    row = TAPS * TAPS
    put(row, everything, jnp.sum(out_grad * value, axis=0, keepdims=True))
    put(row + 1, everything, jnp.sum(out_grad, axis=0, keepdims=True))
    put(row + 2, everything, scale[...])
    for part in range(4):
        own_part = jnp.where(lax.rem(me, 4) == part, 1.0, 0.0)
        put(row + 3 + part, everything, own_part * in_bias[...])
    stay[...] = small[c]
    leave[...] = small[1 - c]


def input_grad_body(grad, inner, outer, kernel, cotan, result, padded):
    rows, cols, channels = cotan.shape
    fill(padded, grad[...].reshape(cotan.shape), inner[...], outer[...])

    @pl.loop(0, channels // LANES)
    def _(step):
        lanes = pl.ds(pl.multiple_of(step * LANES, LANES), LANES)
        start = [cotan[row, :, lanes] for row in range(rows)]
        total = taps_sum(padded, kernel, lanes, rows, cols, True, start)
        for row in range(rows):
            result[row, :, lanes] = total[row]


def output_body(feats, scale, kept, got, result):
    mixed = kept[...] + got[...].astype(WIDE)
    result[...] = feats[...] + (scale[...] * mixed).reshape(feats.shape)


def total_body(turns, *refs):
    parts, sums = refs[: len(turns)], refs[len(turns) : -3]
    stay, leave, half = refs[-3:]
    own = stay.shape[2]
    for side in range(2):
        total = jnp.zeros(parts[0].shape, WIDE)
        for part, turn in zip(parts, turns):
            if turn % 2 == side:
                total = total + part[...].astype(WIDE)
        for which in range(2):
            stay[side, which] = total[which * own : (which + 1) * own]
        leave[2 * side * own : 2 * (side + 1) * own, :] = total[2 * own :]
    total = sums[0][...]
    for one in sums[1:]:
        total = total + one[...].astype(WIDE)
    half[...] = total
    leave[4 * own :, :] = total


def final_body(stay, got, half, *refs):
    in_grad, out_grad, kernel_grad, gain, bias, scale, in_bias, held = refs
    _, c, x = place()
    quarter = stay.shape[-1]
    own = stay.shape[2]
    for side in range(2):
        part = 2 * jnp.bitwise_xor(x, side)
        near = pl.ds(pl.multiple_of((part + c) * quarter, quarter), quarter)
        far = pl.ds(pl.multiple_of((part + 1 - c) * quarter, quarter), quarter)
        for which, target in enumerate((in_grad, out_grad)):
            start = (2 * side + which) * own
            target[:, near] = stay[side, which]
            target[:, far] = got[start : start + own, :]
    held[c] = half[...]
    held[1 - c] = got[4 * own :, :]

    def take(row):
        return held[row // SMALL_ROWS, pl.ds(row % SMALL_ROWS, 1), :]

    for tap_row in range(TAPS):
        for tap_col in range(TAPS):
            kernel_grad[tap_row, pl.ds(tap_col, 1), :] = take(TAPS * tap_row + tap_col)
    row = TAPS * TAPS
    gain[...] = take(row)
    bias[...] = take(row + 1)
    scale[...] = take(row + 2)
    for part in range(4):
        in_bias[:, pl.ds(part * quarter, quarter)] = take(row + 3 + part)


def flipped(blocks, axis, bit_set):
    return jnp.where(bit_set == 1, jnp.flip(blocks, axis), blocks)


def canonical(blocks, me, bit_count):
    tail = blocks.shape[1:]
    blocks = blocks.reshape((2,) * bit_count + tail)
    for spot in range(bit_count):
        blocks = flipped(blocks, bit_count - 1 - spot, (me >> spot) & 1)
    return blocks.reshape((2**bit_count,) + tail)


def per_device(
    features, cotangent, kernel, norm_gain, norm_bias, in_weight, in_bias, out_weight, layer_scale
):
    row_count, col_count, channels = features.shape
    own_rows, hidden_count = in_weight.shape
    pixels = row_count * col_count
    count = lax.axis_size("row")
    bit_count = count.bit_length() - 1
    me = lax.axis_index("row")
    group_index = lax.axis_index("grp")
    quarter = hidden_count // 4
    norm_scale = 1.0 / math.sqrt(pixels * count)
    patterns = count // 4
    copied = own_rows % 16 == 0
    gain_row = norm_gain.reshape(1, channels)
    bias_row = norm_bias.reshape(1, channels)
    scale_row = layer_scale.reshape(1, channels)
    rim = RIM * col_count
    padded = pltpu.VMEM((row_count + 2 * RIM, col_count + 2 * EDGE, channels), WIDE)

    piece = (2, own_rows, quarter)
    once = (features, cotangent, scale_row, kernel, gain_row, bias_row)
    own, core, outer, branch, in_bias_own, feats, cotan, scale, taps, gain, bias = run(
        split_body,
        (
            shaped((2,) + piece, NARROW),
            shaped((4 * own_rows + rim, channels), NARROW),
            shaped((rim, channels), NARROW),
            shaped((pixels, channels), NARROW),
            shaped((1, quarter)),
        )
        + tuple(shaped(x.shape) for x in once),
        in_weight,
        out_weight,
        in_bias.reshape(1, hidden_count),
        *once,
        scratch=(
            pltpu.VMEM(in_weight.shape, WIDE),
            pltpu.VMEM(out_weight.shape, WIDE),
            pltpu.VMEM((1, hidden_count), WIDE),
            pltpu.SemaphoreType.DMA((9,)),
        ),
        apart=True,
    )
    core_got = swap(core, 1)
    outer_got = swap_rim(outer)
    full_shape = shaped((2, 2, own_rows, quarter), NARROW)
    joined = run(
        join_body,
        (full_shape, shaped(piece, NARROW)) * 2,
        own,
        core_got,
    )
    pieces = []
    for side in range(2):
        full, sent = joined[2 * side : 2 * side + 2]
        here = [swap(sent, 4 * p + 2 * side) for p in range(2, patterns)]
        here = run(stack_body, (shaped((patterns - 2,) + piece, NARROW),), *here, order=8)[0]
        near = swap(full, 4 + 2 * side)
        pieces += [full, near, here, swap_group(here)]

    normed, inv, sent = run(
        conv_body,
        (
            shaped((pixels, channels)),
            shaped((pixels, LANES)),
            shaped((2 * pixels + 4 * own_rows, channels), NARROW),
        ),
        feats,
        core_got,
        outer_got,
        taps,
        gain,
        bias,
        branch,
        joined[2],
        scratch=(padded, pltpu.VMEM((pixels, channels), WIDE)),
    )
    first_blocks = [pieces[k] for k in (1, 3, 5, 7)]
    acts, pieces[4] = run(
        acts_body,
        (shaped((2, 2 * pixels, channels), NARROW), full_shape),
        sent,
        swap(sent, 2),
        *first_blocks,
    )
    acts_got = swap(acts, 1)

    if not copied:
        lines = []
        for pattern in range(patterns):
            for side in range(2):
                full, near, here, there = pieces[4 * side : 4 * side + 4]
                if pattern < 2:
                    lines.append(near if pattern else full)
                else:
                    pair = jnp.stack([here[pattern - 2], there[pattern - 2]])
                    lines.append(flipped(pair, 0, group_index))
        lines = jnp.moveaxis(jnp.stack(lines), 1, 2).reshape(count, 2, own_rows, quarter)
        lines = jnp.moveaxis(canonical(lines, me, bit_count), 1, 0)
        pieces = [lines.reshape(2, channels, quarter)]
    group = 4 * pixels
    keep, send, active, hidden, out_narrow, in_bias_part = run(
        functools.partial(hidden_body, copied),
        (
            shaped((2 * pixels, channels)),
            shaped((2 * pixels, channels), NARROW),
            shaped((group, quarter), NARROW),
            shaped((group, quarter), NARROW),
            shaped((channels, quarter), NARROW),
            shaped((1, quarter)),
        ),
        acts,
        acts_got,
        in_bias_own,
        *pieces,
        scratch=(pltpu.VMEM((2, channels, quarter), NARROW),),
        mib=24,
    )
    half = (shaped((pixels, channels)), shaped((pixels, channels), NARROW))
    out_stay, out_leave = run(fold_body, half, keep, swap(send, 1))
    out_got = swap(out_leave, 2)

    holder, mixed_keep, mixed_send, scale_part = run(
        functools.partial(weight_body, norm_scale),
        (
            shaped((2, channels, quarter)),
            shaped((2 * pixels, channels)),
            shaped((2 * pixels, channels), NARROW),
            shaped((1, channels)),
        ),
        acts,
        acts_got,
        active,
        hidden,
        out_narrow,
        scale,
        mib=24,
    )
    mixed_stay, mixed_leave = run(fold_body, half, mixed_keep, swap(mixed_send, 1))
    conv_grad, inner_out, rim_out, stay, leave = run(
        functools.partial(conv_grad_body, norm_scale),
        (
            shaped((pixels, channels)),
            shaped((rim, channels), NARROW),
            shaped((rim, channels), NARROW),
            shaped((SMALL_ROWS, channels)),
            shaped((SMALL_ROWS, channels)),
        ),
        out_stay,
        out_got,
        normed,
        inv,
        gain,
        feats,
        core_got,
        outer_got,
        scale_part,
        in_bias_part,
        scratch=(padded, pltpu.VMEM((2, SMALL_ROWS, channels), WIDE)),
    )
    rim_got = swap_rim(rim_out)
    inner_got = swap(inner_out, 1)
    sums = stay + swap(leave, 1)

    first_turns = (*range(2 * patterns - 1, 4, -2), 3)
    next_turns = (*range(4, 2 * patterns, 2), 2, 1, 0)
    owned = 4 * own_rows
    if copied:
        parts = run(
            functools.partial(owners_body, first_turns),
            (shaped((owned, quarter), NARROW),) * len(first_turns),
            holder,
            out_leave,
        )
    else:
        flat = holder.reshape(2, count, own_rows, quarter)
        flat = canonical(jnp.moveaxis(flat, 1, 0), me, bit_count)
        flat = flat.reshape(2 * patterns, owned, quarter)
        parts = [flat[p].astype(NARROW) for p in first_turns]
    first_parts = [swap(part, 2 * p) for p, part in zip(first_turns, parts)]
    sums, first_parts = lax.optimization_barrier((sums, first_parts))
    sums = sums + swap(sums, 2)
    sums, mixed_leave = lax.optimization_barrier((sums, mixed_leave))
    if copied:
        joint = shaped((owned + 32, quarter), NARROW)
        *parts, side_part, near_own = run(
            functools.partial(owners_body, next_turns),
            (joint,) * (len(next_turns) - 2)
            + (shaped((owned, quarter), NARROW), shaped((owned, quarter))),
            holder,
            sums,
        )
        parts = [swap(part, 2 * p) for p, part in zip(next_turns, parts)]
        sums_parts = [part[owned : owned + SMALL_ROWS] for part in parts]
        next_parts = [part[:owned] for part in parts] + [swap(side_part, 2), near_own]
    else:
        next_parts = [swap(flat[p].astype(NARROW), 2 * p) for p in next_turns[:-1]] + [flat[0]]
        sums_parts = [swap(sums.astype(NARROW), 2 * p) for p in next_turns[:-2]]

    input_grad = run(
        input_grad_body,
        (shaped(features.shape),),
        conv_grad,
        inner_got,
        rim_got,
        taps,
        cotan,
        scratch=(padded,),
    )[0]
    output = run(
        output_body,
        (shaped(features.shape),),
        feats,
        scale,
        mixed_stay,
        swap(mixed_leave, 2),
    )[0]
    parts = list(first_parts) + next_parts
    parts, input_grad, output = lax.optimization_barrier((parts, input_grad, output))

    stay, leave, half_sums = run(
        functools.partial(total_body, first_turns + next_turns),
        (
            shaped((2, 2, own_rows, quarter)),
            shaped((owned + SMALL_ROWS, quarter)),
            shaped((SMALL_ROWS, channels)),
        ),
        *parts,
        sums,
        *sums_parts,
    )
    (
        in_weight_grad,
        out_weight_grad,
        kernel_grad,
        gain_grad,
        bias_grad,
        scale_grad,
        in_bias_grad,
    ) = run(
        final_body,
        (
            shaped((own_rows, hidden_count)),
            shaped((own_rows, hidden_count)),
            shaped(kernel.shape),
            shaped((1, channels)),
            shaped((1, channels)),
            shaped((1, channels)),
            shaped((1, hidden_count)),
        ),
        stay,
        swap(leave, 1),
        half_sums,
        scratch=(pltpu.VMEM((2, SMALL_ROWS, channels), WIDE),),
    )
    return (
        output,
        input_grad,
        in_weight_grad,
        out_weight_grad,
        kernel_grad,
        gain_grad.reshape(channels),
        bias_grad.reshape(channels),
        in_bias_grad.reshape(hidden_count),
        scale_grad.reshape(channels),
    )


def solution(mesh):
    return jax.shard_map(
        per_device,
        mesh=mesh,
        in_specs=(
            P(("grp", "row"), None, None),
            P(("grp", "row"), None, None),
            P(),
            P(),
            P(),
            P("row", None),
            P(),
            P("row", None),
            P(),
        ),
        out_specs=(
            P(("grp", "row"), None, None),
            P(("grp", "row"), None, None),
            P(("grp", "row"), None),
            P(("grp", "row"), None),
            P("grp", None, None),
            P("grp"),
            P("grp"),
            P("grp"),
            P("grp"),
        ),
        check_vma=False,
    )
```

```python
import functools
import math

import jax
import jax.numpy as jnp
from jax import lax
from jax.experimental import pallas as pl
from jax.experimental.pallas import tpu as pltpu
from jax.sharding import PartitionSpec as P

NARROW = jnp.bfloat16
WIDE = jnp.float32
TAPS = 7
RIM = 3
EDGE = 8
LANES = 128
SMALL_ROWS = 28


def swap(value, bit):
    count = lax.axis_size("row")
    return lax.ppermute(value, "row", [(i, i ^ bit) for i in range(count)])


def swap_rim(value):
    count = lax.axis_size("row")
    pairs = [(i, i + 1) for i in range(1, count - 1, 2)]
    return lax.ppermute(value, "row", pairs + [(j, i) for i, j in pairs])


def shaped(shape, dtype=WIDE):
    return jax.ShapeDtypeStruct(shape, dtype)


def swap_group(value):
    return lax.ppermute(value, "grp", [(0, 1), (1, 0)])


def run(body, outs, *operands, scratch=(), mib=16, order=0, apart=False):
    extra = {}
    if apart:
        extra = {"in_specs": [pl.BlockSpec(memory_space=pltpu.HBM)] * len(operands)}
        operands = [pltpu.with_memory_space_constraint(x, pltpu.HBM) for x in operands]
    return pl.pallas_call(
        body,
        out_shape=outs,
        **extra,
        scratch_shapes=scratch,
        compiler_params=pltpu.CompilerParams(vmem_limit_bytes=mib * 2**20),
        cost_estimate=pl.CostEstimate(flops=order * 10**9, bytes_accessed=0, transcendentals=0),
    )(*operands)


def place():
    me = lax.axis_index("row")
    return me, lax.rem(me, 2), lax.rem(lax.div(me, 2), 2)


def dot(left, right, dims):
    return lax.dot_general(left, right, (dims, ((), ())), preferred_element_type=WIDE)


def split_body(*refs):
    inw_hbm, outw_hbm, in_bias_hbm = refs[:3]
    own, core, outer, branch, bias_part = refs[9:14]
    inw, outw, in_bias, sems = refs[20:]
    feats, cotan, scale = refs[14:17]
    pairs = list(zip(refs[3:9], refs[14:20]))
    pairs += [(inw_hbm, inw), (outw_hbm, outw), (in_bias_hbm, in_bias)]
    copies = [pltpu.make_async_copy(a, b, sems.at[k]) for k, (a, b) in enumerate(pairs)]
    for copy in copies[6:] + copies[:6]:
        copy.start()
    me, c, x = place()
    even = c == 0
    quarter = own.shape[-1]
    rows, cols, channels = feats.shape
    own_rows = inw.shape[0]
    copies[6].wait()
    copies[7].wait()
    for side in range(2):
        for part, near in ((2 * jnp.bitwise_xor(x, side) + c, True), (2 * jnp.bitwise_xor(x, side) + 1 - c, False)):
            lanes = pl.ds(pl.multiple_of(part * quarter, quarter), quarter)
            for which, source in enumerate((inw, outw)):
                value = source[:, lanes].astype(NARROW)
                if near:
                    own[side, which] = value
                else:
                    core[pl.ds((2 * side + which) * own_rows, own_rows), :] = value
    copies[0].wait()
    first = feats[:RIM].astype(NARROW).reshape(RIM * cols, channels)
    last = feats[rows - RIM :].astype(NARROW).reshape(RIM * cols, channels)
    core[4 * own_rows :, :] = jnp.where(even, last, first)
    outer[...] = jnp.where(even, first, last)
    copies[1].wait()
    copies[2].wait()
    branch[...] = (scale[...] * cotan[...].reshape(branch.shape)).astype(NARROW)
    copies[8].wait()
    lanes = pl.ds(pl.multiple_of(lax.rem(me, 4) * quarter, quarter), quarter)
    bias_part[...] = in_bias[:, lanes]
    for copy in copies[3:6]:
        copy.wait()


def join_body(mine, other, *targets):
    group = lax.axis_index("grp")
    for side in range(2):
        full, sent = targets[2 * side : 2 * side + 2]
        own_rows = mine.shape[2]
        for which in range(2):
            full[which, 0] = mine[side, which]
            full[which, 1] = other[pl.ds((2 * side + which) * own_rows, own_rows), :]
        sent[...] = full[group]


def acts_body(mine, got, *refs):
    acts, full = refs[-2:]
    pixels = acts.shape[1] // 2
    for which in range(2):
        rows = slice(which * pixels, (which + 1) * pixels)
        acts[which, :pixels] = mine[rows, :]
        acts[which, pixels:] = got[rows, :]
        own = full.shape[2]
        for core in range(2):
            start = 2 * pixels + (2 * which + core) * own
            full[which, core] = got[start : start + own, :]


def stack_body(*refs):
    for place_in, ref in enumerate(refs[:-1]):
        refs[-1][place_in] = ref[...]


def fill(padded, block, inner, outer):
    rows, cols, channels = block.shape
    _, c, _ = place()
    padded[:, :EDGE, :] = jnp.zeros_like(padded[:, :EDGE, :])
    padded[:, EDGE + cols :, :] = jnp.zeros_like(padded[:, EDGE + cols :, :])
    middle = slice(EDGE, EDGE + cols)
    inner = inner.astype(WIDE).reshape(RIM, cols, channels)
    outer = outer.astype(WIDE).reshape(RIM, cols, channels)
    padded[:RIM, middle, :] = jnp.where(c == 0, outer, inner)
    padded[RIM : RIM + rows, middle, :] = block
    padded[RIM + rows :, middle, :] = jnp.where(c == 0, inner, outer)


def taps_sum(padded, kernel, lanes, rows, cols, mirrored, start):
    total = list(start)
    for tap_col in range(TAPS):
        for row in range(rows + TAPS - 1):
            line = padded[row, pl.ds(EDGE - RIM + tap_col, cols), lanes]
            for out in range(rows):
                tap_row = row - out
                if 0 <= tap_row < TAPS:
                    if mirrored:
                        tap = kernel[TAPS - 1 - tap_row, pl.ds(TAPS - 1 - tap_col, 1), lanes]
                    else:
                        tap = kernel[tap_row, pl.ds(tap_col, 1), lanes]
                    total[out] = total[out] + line * tap
    return total


def conv_body(
    feats, core_got, outer, kernel, gain, bias, branch, full, normed, inv, acts, padded, result
):
    rows, cols, channels = feats.shape
    start = core_got.shape[0] - RIM * cols
    fill(padded, feats[...], core_got[start:, :], outer[...])

    @pl.loop(0, channels // LANES)
    def _(step):
        lanes = pl.ds(pl.multiple_of(step * LANES, LANES), LANES)
        zero = [jnp.zeros((cols, LANES), WIDE)] * rows
        total = taps_sum(padded, kernel, lanes, rows, cols, False, zero)
        for row in range(rows):
            result[pl.ds(row * cols, cols), lanes] = total[row]

    value = result[...]
    centred = value - jnp.mean(value, axis=1, keepdims=True)
    spread = lax.rsqrt(jnp.mean(centred * centred, axis=1, keepdims=True) + 1e-06)
    value = centred * spread
    normed[...] = value
    inv[...] = jnp.broadcast_to(spread, inv.shape)
    pixels = rows * cols
    acts[:pixels, :] = (value * gain[...] + bias[...]).astype(NARROW)
    acts[pixels : 2 * pixels, :] = branch[...]
    own = full.shape[2]
    for which in range(2):
        for core in range(2):
            start = 2 * pixels + (2 * which + core) * own
            acts[start : start + own, :] = full[which, core]


def hidden_body(copied, *refs):
    patterns = lax.axis_size("row") // 4
    me, _, _ = place()
    acts, in_bias = refs[:2], refs[2]
    pieces = refs[3:-7]
    keep, send, active, hidden, out_copy, bias_part, weights = refs[-7:]
    half = acts[0].shape[1]
    if copied:
        own = pieces[0].shape[2]
        group = lax.axis_index("grp")
        for side in range(2):
            full, near, here, there = pieces[4 * side : 4 * side + 4]
            for pattern in range(patterns):
                for c in range(2):
                    device = jnp.bitwise_xor(me, 4 * pattern + 2 * side + c)
                    rows = pl.ds(pl.multiple_of(device * own, own), own)
                    if pattern < 2:
                        source = near if pattern else full
                        weights[0, rows, :] = source[0, c]
                        weights[1, rows, :] = source[1, c]
                    else:
                        weights[group, rows, :] = here[pattern - 2, c]
                        weights[1 - group, rows, :] = there[pattern - 2, c]
    else:
        weights[...] = pieces[0][...]
    in_narrow = weights.at[0]
    out_narrow = weights.at[1]
    out_copy[...] = weights[1]
    bias_row = in_bias[...]
    total = jnp.zeros_like(bias_row)
    for side in (1, 0):
        preact = dot(acts[side][0], in_narrow[...], ((1,), (0,))) + bias_row
        act_grad = dot(acts[side][1], out_narrow[...], ((1,), (0,)))
        cdf = 0.5 * (1.0 + lax.erf(preact * 0.7071067811865476))
        rows = pl.ds(side * half, half)
        activated = (preact * cdf).astype(NARROW)
        active[rows, :] = activated
        slope = cdf + preact * jnp.exp(-0.5 * preact * preact) * 0.3989422804014327
        grad = act_grad * slope
        total = total + jnp.sum(grad, axis=0, keepdims=True)
        narrow = grad.astype(NARROW)
        hidden[rows, :] = narrow
        out_grad = dot(narrow, in_narrow[...], ((1,), (1,)))
        if side:
            send[...] = out_grad.astype(NARROW)
        else:
            keep[...] = out_grad
    bias_part[...] = total


def weight_body(norm_scale, *refs):
    acts, (active, hidden, out_narrow, scale) = refs[:2], refs[2:6]
    holder, keep, send, scale_part = refs[6:]
    half = acts[0].shape[1]
    first, second = pl.ds(0, half), pl.ds(half, half)
    for which, right in enumerate((hidden, active)):
        grad = dot(acts[0][which], right[first, :], ((0,), (0,)))
        grad = grad + dot(acts[1][which], right[second, :], ((0,), (0,)))
        holder[which] = norm_scale * grad
    total = jnp.zeros_like(scale_part)
    for side, rows in enumerate((first, second)):
        mixed = dot(active[rows, :], out_narrow[...], ((1,), (1,)))
        total = total + jnp.sum(mixed * acts[side][1].astype(WIDE), axis=0, keepdims=True)
        if side:
            send[...] = mixed.astype(NARROW)
        else:
            keep[...] = mixed
    scale_part[...] = total / scale[...]


def owners_body(turns, holder, after, *targets):
    me, _, _ = place()
    own = holder.shape[1] // lax.axis_size("row")
    for pattern, target in zip(turns, targets):
        for c in range(2):
            device = jnp.bitwise_xor(me, 2 * pattern + c)
            rows = pl.ds(pl.multiple_of(device * own, own), own)
            for which in range(2):
                start = (2 * c + which) * own
                target[start : start + own, :] = holder[which, rows, :].astype(target.dtype)
        if target.shape[0] > 4 * own:
            target[4 * own : 4 * own + SMALL_ROWS, :] = after[...].astype(target.dtype)
            rest = target.shape[0] - 4 * own - SMALL_ROWS
            target[4 * own + SMALL_ROWS :, :] = jnp.zeros((rest, target.shape[1]), target.dtype)


def fold_body(kept, got, stay, leave):
    size = stay.shape[0]
    stay[...] = kept[:size] + got[:size].astype(WIDE)
    leave[...] = (kept[size:] + got[size:].astype(WIDE)).astype(NARROW)


def conv_grad_body(norm_scale, *refs):
    kept, got, normed, inv, gain, feats, core_got, outer, scale, in_bias = refs[:10]
    grad, inner_out, rim_out, stay, leave, padded, small = refs[10:]
    rows, cols, channels = feats.shape
    me, c, _ = place()
    out_grad = kept[...] + got[...].astype(WIDE)
    value = normed[...]
    normed_grad = out_grad * gain[...]
    mean = jnp.mean(normed_grad, axis=1, keepdims=True)
    along = jnp.mean(normed_grad * value, axis=1, keepdims=True)
    result = inv[:, :1] * (normed_grad - mean - value * along)
    grad[...] = result
    pixels = rows * cols
    rim = RIM * cols
    rim_out[...] = jnp.where(c == 0, result[:rim], result[pixels - rim :]).astype(NARROW)
    inner_out[...] = jnp.where(c == 0, result[pixels - rim :], result[:rim]).astype(NARROW)
    fill(padded, feats[...], core_got[core_got.shape[0] - rim :, :], outer[...])

    def put(row, lanes, total):
        small[row // SMALL_ROWS, pl.ds(row % SMALL_ROWS, 1), lanes] = norm_scale * total

    @pl.loop(0, channels // LANES)
    def _(step):
        lanes = pl.ds(pl.multiple_of(step * LANES, LANES), LANES)
        own = [grad[pl.ds(row * cols, cols), lanes] for row in range(rows)]
        for tap_col in range(TAPS):
            totals = [jnp.zeros((8, LANES), WIDE)] * TAPS
            for row in range(rows + TAPS - 1):
                line = padded[row, pl.ds(EDGE - RIM + tap_col, cols), lanes]
                for out in range(rows):
                    tap_row = row - out
                    if 0 <= tap_row < TAPS:
                        product = line * own[out]
                        for part in range(cols // 8):
                            totals[tap_row] = totals[tap_row] + product[8 * part : 8 * part + 8]
            for tap_row in range(TAPS):
                total = jnp.sum(totals[tap_row], axis=0, keepdims=True)
                put(TAPS * tap_row + tap_col, lanes, total)

    everything = slice(None)
    row = TAPS * TAPS
    put(row, everything, jnp.sum(out_grad * value, axis=0, keepdims=True))
    put(row + 1, everything, jnp.sum(out_grad, axis=0, keepdims=True))
    put(row + 2, everything, scale[...])
    for part in range(4):
        own_part = jnp.where(lax.rem(me, 4) == part, 1.0, 0.0)
        put(row + 3 + part, everything, own_part * in_bias[...])
    stay[...] = small[c]
    leave[...] = small[1 - c]


def input_grad_body(grad, inner, outer, kernel, cotan, result, padded):
    rows, cols, channels = cotan.shape
    fill(padded, grad[...].reshape(cotan.shape), inner[...], outer[...])

    @pl.loop(0, channels // LANES)
    def _(step):
        lanes = pl.ds(pl.multiple_of(step * LANES, LANES), LANES)
        start = [cotan[row, :, lanes] for row in range(rows)]
        total = taps_sum(padded, kernel, lanes, rows, cols, True, start)
        for row in range(rows):
            result[row, :, lanes] = total[row]


def output_body(feats, scale, kept, got, result):
    mixed = kept[...] + got[...].astype(WIDE)
    result[...] = feats[...] + (scale[...] * mixed).reshape(feats.shape)


def total_body(turns, *refs):
    parts, sums = refs[: len(turns)], refs[len(turns) : -3]
    stay, leave, half = refs[-3:]
    own = stay.shape[2]
    for side in range(2):
        total = jnp.zeros(parts[0].shape, WIDE)
        for part, turn in zip(parts, turns):
            if turn % 2 == side:
                total = total + part[...].astype(WIDE)
        for which in range(2):
            stay[side, which] = total[which * own : (which + 1) * own]
        leave[2 * side * own : 2 * (side + 1) * own, :] = total[2 * own :]
    total = sums[0][...]
    for one in sums[1:]:
        total = total + one[...].astype(WIDE)
    half[...] = total
    leave[4 * own :, :] = total


def final_body(stay, got, half, *refs):
    in_grad, out_grad, kernel_grad, gain, bias, scale, in_bias, held = refs
    _, c, x = place()
    quarter = stay.shape[-1]
    own = stay.shape[2]
    for side in range(2):
        part = 2 * jnp.bitwise_xor(x, side)
        near = pl.ds(pl.multiple_of((part + c) * quarter, quarter), quarter)
        far = pl.ds(pl.multiple_of((part + 1 - c) * quarter, quarter), quarter)
        for which, target in enumerate((in_grad, out_grad)):
            start = (2 * side + which) * own
            target[:, near] = stay[side, which]
            target[:, far] = got[start : start + own, :]
    held[c] = half[...]
    held[1 - c] = got[4 * own :, :]

    def take(row):
        return held[row // SMALL_ROWS, pl.ds(row % SMALL_ROWS, 1), :]

    for tap_row in range(TAPS):
        for tap_col in range(TAPS):
            kernel_grad[tap_row, pl.ds(tap_col, 1), :] = take(TAPS * tap_row + tap_col)
    row = TAPS * TAPS
    gain[...] = take(row)
    bias[...] = take(row + 1)
    scale[...] = take(row + 2)
    for part in range(4):
        in_bias[:, pl.ds(part * quarter, quarter)] = take(row + 3 + part)


def flipped(blocks, axis, bit_set):
    return jnp.where(bit_set == 1, jnp.flip(blocks, axis), blocks)


def canonical(blocks, me, bit_count):
    tail = blocks.shape[1:]
    blocks = blocks.reshape((2,) * bit_count + tail)
    for spot in range(bit_count):
        blocks = flipped(blocks, bit_count - 1 - spot, (me >> spot) & 1)
    return blocks.reshape((2**bit_count,) + tail)


def per_device(
    features, cotangent, kernel, norm_gain, norm_bias, in_weight, in_bias, out_weight, layer_scale
):
    row_count, col_count, channels = features.shape
    own_rows, hidden_count = in_weight.shape
    pixels = row_count * col_count
    count = lax.axis_size("row")
    bit_count = count.bit_length() - 1
    me = lax.axis_index("row")
    group_index = lax.axis_index("grp")
    quarter = hidden_count // 4
    norm_scale = 1.0 / math.sqrt(pixels * count)
    patterns = count // 4
    copied = own_rows % 16 == 0
    gain_row = norm_gain.reshape(1, channels)
    bias_row = norm_bias.reshape(1, channels)
    scale_row = layer_scale.reshape(1, channels)
    rim = RIM * col_count
    padded = pltpu.VMEM((row_count + 2 * RIM, col_count + 2 * EDGE, channels), WIDE)

    piece = (2, own_rows, quarter)
    once = (features, cotangent, scale_row, kernel, gain_row, bias_row)
    own, core, outer, branch, in_bias_own, feats, cotan, scale, taps, gain, bias = run(
        split_body,
        (
            shaped((2,) + piece, NARROW),
            shaped((4 * own_rows + rim, channels), NARROW),
            shaped((rim, channels), NARROW),
            shaped((pixels, channels), NARROW),
            shaped((1, quarter)),
        )
        + tuple(shaped(x.shape) for x in once),
        in_weight,
        out_weight,
        in_bias.reshape(1, hidden_count),
        *once,
        scratch=(
            pltpu.VMEM(in_weight.shape, WIDE),
            pltpu.VMEM(out_weight.shape, WIDE),
            pltpu.VMEM((1, hidden_count), WIDE),
            pltpu.SemaphoreType.DMA((9,)),
        ),
        apart=True,
    )
    core_got = swap(core, 1)
    outer_got = swap_rim(outer)
    full_shape = shaped((2, 2, own_rows, quarter), NARROW)
    joined = run(
        join_body,
        (full_shape, shaped(piece, NARROW)) * 2,
        own,
        core_got,
    )
    pieces = []
    for side in range(2):
        full, sent = joined[2 * side : 2 * side + 2]
        here = [swap(sent, 4 * p + 2 * side) for p in range(2, patterns)]
        here = run(stack_body, (shaped((patterns - 2,) + piece, NARROW),), *here, order=8)[0]
        near = swap(full, 4 + 2 * side)
        pieces += [full, near, here, swap_group(here)]

    normed, inv, sent = run(
        conv_body,
        (
            shaped((pixels, channels)),
            shaped((pixels, LANES)),
            shaped((2 * pixels + 4 * own_rows, channels), NARROW),
        ),
        feats,
        core_got,
        outer_got,
        taps,
        gain,
        bias,
        branch,
        joined[2],
        scratch=(padded, pltpu.VMEM((pixels, channels), WIDE)),
    )
    first_blocks = [pieces[k] for k in (1, 3, 5, 7)]
    acts, pieces[4] = run(
        acts_body,
        (shaped((2, 2 * pixels, channels), NARROW), full_shape),
        sent,
        swap(sent, 2),
        *first_blocks,
    )
    acts_got = swap(acts, 1)

    if not copied:
        lines = []
        for pattern in range(patterns):
            for side in range(2):
                full, near, here, there = pieces[4 * side : 4 * side + 4]
                if pattern < 2:
                    lines.append(near if pattern else full)
                else:
                    pair = jnp.stack([here[pattern - 2], there[pattern - 2]])
                    lines.append(flipped(pair, 0, group_index))
        lines = jnp.moveaxis(jnp.stack(lines), 1, 2).reshape(count, 2, own_rows, quarter)
        lines = jnp.moveaxis(canonical(lines, me, bit_count), 1, 0)
        pieces = [lines.reshape(2, channels, quarter)]
    group = 4 * pixels
    keep, send, active, hidden, out_narrow, in_bias_part = run(
        functools.partial(hidden_body, copied),
        (
            shaped((2 * pixels, channels)),
            shaped((2 * pixels, channels), NARROW),
            shaped((group, quarter), NARROW),
            shaped((group, quarter), NARROW),
            shaped((channels, quarter), NARROW),
            shaped((1, quarter)),
        ),
        acts,
        acts_got,
        in_bias_own,
        *pieces,
        scratch=(pltpu.VMEM((2, channels, quarter), NARROW),),
        mib=24,
    )
    half = (shaped((pixels, channels)), shaped((pixels, channels), NARROW))
    out_stay, out_leave = run(fold_body, half, keep, swap(send, 1))
    out_got = swap(out_leave, 2)

    holder, mixed_keep, mixed_send, scale_part = run(
        functools.partial(weight_body, norm_scale),
        (
            shaped((2, channels, quarter)),
            shaped((2 * pixels, channels)),
            shaped((2 * pixels, channels), NARROW),
            shaped((1, channels)),
        ),
        acts,
        acts_got,
        active,
        hidden,
        out_narrow,
        scale,
        mib=24,
    )
    mixed_stay, mixed_leave = run(fold_body, half, mixed_keep, swap(mixed_send, 1))
    out_got, mixed_leave = lax.optimization_barrier((out_got, mixed_leave))
    conv_grad, inner_out, rim_out, stay, leave = run(
        functools.partial(conv_grad_body, norm_scale),
        (
            shaped((pixels, channels)),
            shaped((rim, channels), NARROW),
            shaped((rim, channels), NARROW),
            shaped((SMALL_ROWS, channels)),
            shaped((SMALL_ROWS, channels)),
        ),
        out_stay,
        out_got,
        normed,
        inv,
        gain,
        feats,
        core_got,
        outer_got,
        scale_part,
        in_bias_part,
        scratch=(padded, pltpu.VMEM((2, SMALL_ROWS, channels), WIDE)),
    )
    rim_got = swap_rim(rim_out)
    inner_got = swap(inner_out, 1)
    sums = stay + swap(leave, 1)

    first_turns = (*range(2 * patterns - 1, 4, -2), 3)
    solo = 2 * patterns - 2
    next_turns = (*range(4, solo, 2), 2, 1, 0)
    owned = 4 * own_rows
    if copied:
        parts = run(
            functools.partial(owners_body, (*first_turns, solo)),
            (shaped((owned, quarter), NARROW),) * (len(first_turns) + 1),
            holder,
            out_leave,
        )
    else:
        flat = holder.reshape(2, count, own_rows, quarter)
        flat = canonical(jnp.moveaxis(flat, 1, 0), me, bit_count)
        flat = flat.reshape(2 * patterns, owned, quarter)
        parts = [flat[p].astype(NARROW) for p in (*first_turns, solo)]
    first_parts = [swap(part, 2 * p) for p, part in zip(first_turns, parts)]
    solo_part = swap(parts[-1], 2 * solo)
    first_parts[:2], sums = lax.optimization_barrier((first_parts[:2], sums))
    sums = sums + swap(sums, 2)
    sums, mixed_leave, solo_part, first_parts, rim_got = lax.optimization_barrier(
        (sums, mixed_leave, solo_part, first_parts, rim_got)
    )
    solo_sums = swap(sums.astype(NARROW), 2 * solo)
    if copied:
        joint = shaped((owned + 32, quarter), NARROW)
        *parts, side_part, near_own = run(
            functools.partial(owners_body, next_turns),
            (joint,) * (len(next_turns) - 2)
            + (shaped((owned, quarter), NARROW), shaped((owned, quarter))),
            holder,
            sums,
        )
        parts = [swap(part, 2 * p) for p, part in zip(next_turns, parts)]
        sums_parts = [part[owned : owned + SMALL_ROWS] for part in parts]
        next_parts = [part[:owned] for part in parts] + [swap(side_part, 2), near_own]
    else:
        next_parts = [swap(flat[p].astype(NARROW), 2 * p) for p in next_turns[:-1]] + [flat[0]]
        sums_parts = [swap(sums.astype(NARROW), 2 * p) for p in next_turns[:-2]]

    input_grad = run(
        input_grad_body,
        (shaped(features.shape),),
        conv_grad,
        inner_got,
        rim_got,
        taps,
        cotan,
        scratch=(padded,),
    )[0]
    output = run(
        output_body,
        (shaped(features.shape),),
        feats,
        scale,
        mixed_stay,
        swap(mixed_leave, 2),
    )[0]
    parts = [*first_parts, solo_part, *next_parts]
    sums_parts.append(solo_sums)
    parts, input_grad, output = lax.optimization_barrier((parts, input_grad, output))

    stay, leave, half_sums = run(
        functools.partial(total_body, (*first_turns, solo, *next_turns)),
        (
            shaped((2, 2, own_rows, quarter)),
            shaped((owned + SMALL_ROWS, quarter)),
            shaped((SMALL_ROWS, channels)),
        ),
        *parts,
        sums,
        *sums_parts,
    )
    (
        in_weight_grad,
        out_weight_grad,
        kernel_grad,
        gain_grad,
        bias_grad,
        scale_grad,
        in_bias_grad,
    ) = run(
        final_body,
        (
            shaped((own_rows, hidden_count)),
            shaped((own_rows, hidden_count)),
            shaped(kernel.shape),
            shaped((1, channels)),
            shaped((1, channels)),
            shaped((1, channels)),
            shaped((1, hidden_count)),
        ),
        stay,
        swap(leave, 1),
        half_sums,
        scratch=(pltpu.VMEM((2, SMALL_ROWS, channels), WIDE),),
    )
    return (
        output,
        input_grad,
        in_weight_grad,
        out_weight_grad,
        kernel_grad,
        gain_grad.reshape(channels),
        bias_grad.reshape(channels),
        in_bias_grad.reshape(hidden_count),
        scale_grad.reshape(channels),
    )


def solution(mesh):
    return jax.shard_map(
        per_device,
        mesh=mesh,
        in_specs=(
            P(("grp", "row"), None, None),
            P(("grp", "row"), None, None),
            P(),
            P(),
            P(),
            P("row", None),
            P(),
            P("row", None),
            P(),
        ),
        out_specs=(
            P(("grp", "row"), None, None),
            P(("grp", "row"), None, None),
            P(("grp", "row"), None),
            P(("grp", "row"), None),
            P("grp", None, None),
            P("grp"),
            P("grp"),
            P("grp"),
            P("grp"),
        ),
        check_vma=False,
    )
```

```python
import functools
import math

import jax
import jax.numpy as jnp
from jax import lax
from jax.experimental import pallas as pl
from jax.experimental.pallas import tpu as pltpu
from jax.sharding import PartitionSpec as P

NARROW = jnp.bfloat16
WIDE = jnp.float32
TAPS = 7
RIM = 3
EDGE = 8
LANES = 128
SMALL_ROWS = 28


def swap(value, bit):
    count = lax.axis_size("row")
    return lax.ppermute(value, "row", [(i, i ^ bit) for i in range(count)])


def swap_rim(value):
    count = lax.axis_size("row")
    pairs = [(i, i + 1) for i in range(1, count - 1, 2)]
    return lax.ppermute(value, "row", pairs + [(j, i) for i, j in pairs])


def shaped(shape, dtype=WIDE):
    return jax.ShapeDtypeStruct(shape, dtype)


def swap_group(value):
    return lax.ppermute(value, "grp", [(0, 1), (1, 0)])


def run(body, outs, *operands, scratch=(), mib=16, order=0, apart=False):
    extra = {}
    if apart:
        extra = {"in_specs": [pl.BlockSpec(memory_space=pltpu.HBM)] * len(operands)}
        operands = [pltpu.with_memory_space_constraint(x, pltpu.HBM) for x in operands]
    return pl.pallas_call(
        body,
        out_shape=outs,
        **extra,
        scratch_shapes=scratch,
        compiler_params=pltpu.CompilerParams(vmem_limit_bytes=mib * 2**20),
        cost_estimate=pl.CostEstimate(flops=order * 10**9, bytes_accessed=0, transcendentals=0),
    )(*operands)


def place():
    me = lax.axis_index("row")
    return me, lax.rem(me, 2), lax.rem(lax.div(me, 2), 2)


def dot(left, right, dims):
    return lax.dot_general(left, right, (dims, ((), ())), preferred_element_type=WIDE)


def split_body(*refs):
    inw_hbm, outw_hbm, in_bias_hbm = refs[:3]
    own, core, outer, branch, bias_part = refs[9:14]
    inw, outw, in_bias, sems = refs[20:]
    feats, cotan, scale = refs[14:17]
    pairs = list(zip(refs[3:9], refs[14:20]))
    pairs += [(inw_hbm, inw), (outw_hbm, outw), (in_bias_hbm, in_bias)]
    copies = [pltpu.make_async_copy(a, b, sems.at[k]) for k, (a, b) in enumerate(pairs)]
    for copy in copies[6:] + copies[:6]:
        copy.start()
    me, c, x = place()
    even = c == 0
    quarter = own.shape[-1]
    rows, cols, channels = feats.shape
    own_rows = inw.shape[0]
    copies[6].wait()
    copies[7].wait()
    for side in range(2):
        for part, near in ((2 * jnp.bitwise_xor(x, side) + c, True), (2 * jnp.bitwise_xor(x, side) + 1 - c, False)):
            lanes = pl.ds(pl.multiple_of(part * quarter, quarter), quarter)
            for which, source in enumerate((inw, outw)):
                value = source[:, lanes].astype(NARROW)
                if near:
                    own[side, which] = value
                else:
                    core[pl.ds((2 * side + which) * own_rows, own_rows), :] = value
    copies[0].wait()
    first = feats[:RIM].astype(NARROW).reshape(RIM * cols, channels)
    last = feats[rows - RIM :].astype(NARROW).reshape(RIM * cols, channels)
    core[4 * own_rows :, :] = jnp.where(even, last, first)
    outer[...] = jnp.where(even, first, last)
    copies[1].wait()
    copies[2].wait()
    branch[...] = (scale[...] * cotan[...].reshape(branch.shape)).astype(NARROW)
    copies[8].wait()
    lanes = pl.ds(pl.multiple_of(lax.rem(me, 4) * quarter, quarter), quarter)
    bias_part[...] = in_bias[:, lanes]
    for copy in copies[3:6]:
        copy.wait()


def join_body(mine, other, *targets):
    group = lax.axis_index("grp")
    for side in range(2):
        full, sent = targets[2 * side : 2 * side + 2]
        own_rows = mine.shape[2]
        for which in range(2):
            full[which, 0] = mine[side, which]
            full[which, 1] = other[pl.ds((2 * side + which) * own_rows, own_rows), :]
        sent[...] = full[group]


def acts_body(mine, got, *refs):
    acts, full = refs[-2:]
    pixels = acts.shape[1] // 2
    for which in range(2):
        rows = slice(which * pixels, (which + 1) * pixels)
        acts[which, :pixels] = mine[rows, :]
        acts[which, pixels:] = got[rows, :]
        own = full.shape[2]
        for core in range(2):
            start = 2 * pixels + (2 * which + core) * own
            full[which, core] = got[start : start + own, :]


def stack_body(*refs):
    for place_in, ref in enumerate(refs[:-1]):
        refs[-1][place_in] = ref[...]


def fill(padded, block, inner, outer):
    rows, cols, channels = block.shape
    _, c, _ = place()
    padded[:, :EDGE, :] = jnp.zeros_like(padded[:, :EDGE, :])
    padded[:, EDGE + cols :, :] = jnp.zeros_like(padded[:, EDGE + cols :, :])
    middle = slice(EDGE, EDGE + cols)
    inner = inner.astype(WIDE).reshape(RIM, cols, channels)
    outer = outer.astype(WIDE).reshape(RIM, cols, channels)
    padded[:RIM, middle, :] = jnp.where(c == 0, outer, inner)
    padded[RIM : RIM + rows, middle, :] = block
    padded[RIM + rows :, middle, :] = jnp.where(c == 0, inner, outer)


def taps_sum(padded, kernel, lanes, rows, cols, mirrored, start):
    total = list(start)
    for tap_col in range(TAPS):
        for row in range(rows + TAPS - 1):
            line = padded[row, pl.ds(EDGE - RIM + tap_col, cols), lanes]
            for out in range(rows):
                tap_row = row - out
                if 0 <= tap_row < TAPS:
                    if mirrored:
                        tap = kernel[TAPS - 1 - tap_row, pl.ds(TAPS - 1 - tap_col, 1), lanes]
                    else:
                        tap = kernel[tap_row, pl.ds(tap_col, 1), lanes]
                    total[out] = total[out] + line * tap
    return total


def conv_body(
    feats, core_got, outer, kernel, gain, bias, branch, full, normed, inv, acts, padded, result
):
    rows, cols, channels = feats.shape
    start = core_got.shape[0] - RIM * cols
    fill(padded, feats[...], core_got[start:, :], outer[...])

    @pl.loop(0, channels // LANES)
    def _(step):
        lanes = pl.ds(pl.multiple_of(step * LANES, LANES), LANES)
        zero = [jnp.zeros((cols, LANES), WIDE)] * rows
        total = taps_sum(padded, kernel, lanes, rows, cols, False, zero)
        for row in range(rows):
            result[pl.ds(row * cols, cols), lanes] = total[row]

    value = result[...]
    centred = value - jnp.mean(value, axis=1, keepdims=True)
    spread = lax.rsqrt(jnp.mean(centred * centred, axis=1, keepdims=True) + 1e-06)
    value = centred * spread
    normed[...] = value
    inv[...] = jnp.broadcast_to(spread, inv.shape)
    pixels = rows * cols
    acts[:pixels, :] = (value * gain[...] + bias[...]).astype(NARROW)
    acts[pixels : 2 * pixels, :] = branch[...]
    own = full.shape[2]
    for which in range(2):
        for core in range(2):
            start = 2 * pixels + (2 * which + core) * own
            acts[start : start + own, :] = full[which, core]


def hidden_body(copied, *refs):
    patterns = lax.axis_size("row") // 4
    me, _, _ = place()
    acts, in_bias = refs[:2], refs[2]
    pieces = refs[3:-7]
    keep, send, active, hidden, out_copy, bias_part, weights = refs[-7:]
    half = acts[0].shape[1]
    if copied:
        own = pieces[0].shape[2]
        group = lax.axis_index("grp")
        for side in range(2):
            full, near, here, there = pieces[4 * side : 4 * side + 4]
            for pattern in range(patterns):
                for c in range(2):
                    device = jnp.bitwise_xor(me, 4 * pattern + 2 * side + c)
                    rows = pl.ds(pl.multiple_of(device * own, own), own)
                    if pattern < 2:
                        source = near if pattern else full
                        weights[0, rows, :] = source[0, c]
                        weights[1, rows, :] = source[1, c]
                    else:
                        weights[group, rows, :] = here[pattern - 2, c]
                        weights[1 - group, rows, :] = there[pattern - 2, c]
    else:
        weights[...] = pieces[0][...]
    in_narrow = weights.at[0]
    out_narrow = weights.at[1]
    out_copy[...] = weights[1]
    bias_row = in_bias[...]
    total = jnp.zeros_like(bias_row)
    for side in (1, 0):
        preact = dot(acts[side][0], in_narrow[...], ((1,), (0,))) + bias_row
        act_grad = dot(acts[side][1], out_narrow[...], ((1,), (0,)))
        cdf = 0.5 * (1.0 + lax.erf(preact * 0.7071067811865476))
        rows = pl.ds(side * half, half)
        activated = (preact * cdf).astype(NARROW)
        active[rows, :] = activated
        slope = cdf + preact * jnp.exp(-0.5 * preact * preact) * 0.3989422804014327
        grad = act_grad * slope
        total = total + jnp.sum(grad, axis=0, keepdims=True)
        narrow = grad.astype(NARROW)
        hidden[rows, :] = narrow
        out_grad = dot(narrow, in_narrow[...], ((1,), (1,)))
        if side:
            send[...] = out_grad.astype(NARROW)
        else:
            keep[...] = out_grad
    bias_part[...] = total


def weight_body(norm_scale, *refs):
    acts, (active, hidden, out_narrow, scale) = refs[:2], refs[2:6]
    holder, keep, send, scale_part = refs[6:]
    half = acts[0].shape[1]
    first, second = pl.ds(0, half), pl.ds(half, half)
    for which, right in enumerate((hidden, active)):
        grad = dot(acts[0][which], right[first, :], ((0,), (0,)))
        grad = grad + dot(acts[1][which], right[second, :], ((0,), (0,)))
        holder[which] = norm_scale * grad
    total = jnp.zeros_like(scale_part)
    for side, rows in enumerate((first, second)):
        mixed = dot(active[rows, :], out_narrow[...], ((1,), (1,)))
        total = total + jnp.sum(mixed * acts[side][1].astype(WIDE), axis=0, keepdims=True)
        if side:
            send[...] = mixed.astype(NARROW)
        else:
            keep[...] = mixed
    scale_part[...] = total / scale[...]


def owners_body(turns, holder, after, *targets):
    me, _, _ = place()
    own = holder.shape[1] // lax.axis_size("row")
    for pattern, target in zip(turns, targets):
        for c in range(2):
            device = jnp.bitwise_xor(me, 2 * pattern + c)
            rows = pl.ds(pl.multiple_of(device * own, own), own)
            for which in range(2):
                start = (2 * c + which) * own
                target[start : start + own, :] = holder[which, rows, :].astype(target.dtype)
        if target.shape[0] > 4 * own:
            target[4 * own : 4 * own + SMALL_ROWS, :] = after[...].astype(target.dtype)
            rest = target.shape[0] - 4 * own - SMALL_ROWS
            target[4 * own + SMALL_ROWS :, :] = jnp.zeros((rest, target.shape[1]), target.dtype)


def fold_body(kept, got, stay, leave):
    size = stay.shape[0]
    stay[...] = kept[:size] + got[:size].astype(WIDE)
    leave[...] = (kept[size:] + got[size:].astype(WIDE)).astype(NARROW)


def conv_grad_body(norm_scale, *refs):
    kept, got, normed, inv, gain, feats, core_got, outer, scale, in_bias = refs[:10]
    grad, inner_out, rim_out, stay, leave, padded, small = refs[10:]
    rows, cols, channels = feats.shape
    me, c, _ = place()
    out_grad = kept[...] + got[...].astype(WIDE)
    value = normed[...]
    normed_grad = out_grad * gain[...]
    mean = jnp.mean(normed_grad, axis=1, keepdims=True)
    along = jnp.mean(normed_grad * value, axis=1, keepdims=True)
    result = inv[:, :1] * (normed_grad - mean - value * along)
    grad[...] = result
    pixels = rows * cols
    rim = RIM * cols
    rim_out[...] = jnp.where(c == 0, result[:rim], result[pixels - rim :]).astype(NARROW)
    inner_out[...] = jnp.where(c == 0, result[pixels - rim :], result[:rim]).astype(NARROW)
    fill(padded, feats[...], core_got[core_got.shape[0] - rim :, :], outer[...])

    def put(row, lanes, total):
        small[row // SMALL_ROWS, pl.ds(row % SMALL_ROWS, 1), lanes] = norm_scale * total

    @pl.loop(0, channels // LANES)
    def _(step):
        lanes = pl.ds(pl.multiple_of(step * LANES, LANES), LANES)
        own = [grad[pl.ds(row * cols, cols), lanes] for row in range(rows)]
        for tap_col in range(TAPS):
            totals = [jnp.zeros((8, LANES), WIDE)] * TAPS
            for row in range(rows + TAPS - 1):
                line = padded[row, pl.ds(EDGE - RIM + tap_col, cols), lanes]
                for out in range(rows):
                    tap_row = row - out
                    if 0 <= tap_row < TAPS:
                        product = line * own[out]
                        for part in range(cols // 8):
                            totals[tap_row] = totals[tap_row] + product[8 * part : 8 * part + 8]
            for tap_row in range(TAPS):
                total = jnp.sum(totals[tap_row], axis=0, keepdims=True)
                put(TAPS * tap_row + tap_col, lanes, total)

    everything = slice(None)
    row = TAPS * TAPS
    put(row, everything, jnp.sum(out_grad * value, axis=0, keepdims=True))
    put(row + 1, everything, jnp.sum(out_grad, axis=0, keepdims=True))
    put(row + 2, everything, scale[...])
    for part in range(4):
        own_part = jnp.where(lax.rem(me, 4) == part, 1.0, 0.0)
        put(row + 3 + part, everything, own_part * in_bias[...])
    stay[...] = small[c]
    leave[...] = small[1 - c]


def input_grad_body(grad, inner, outer, kernel, cotan, result, padded):
    rows, cols, channels = cotan.shape
    fill(padded, grad[...].reshape(cotan.shape), inner[...], outer[...])

    @pl.loop(0, channels // LANES)
    def _(step):
        lanes = pl.ds(pl.multiple_of(step * LANES, LANES), LANES)
        start = [cotan[row, :, lanes] for row in range(rows)]
        total = taps_sum(padded, kernel, lanes, rows, cols, True, start)
        for row in range(rows):
            result[row, :, lanes] = total[row]


def output_body(feats, scale, kept, got, result):
    mixed = kept[...] + got[...].astype(WIDE)
    result[...] = feats[...] + (scale[...] * mixed).reshape(feats.shape)


def total_body(turns, *refs):
    parts, sums = refs[: len(turns)], refs[len(turns) : -3]
    stay, leave, half = refs[-3:]
    own = stay.shape[2]
    for side in range(2):
        total = jnp.zeros(parts[0].shape, WIDE)
        for part, turn in zip(parts, turns):
            if turn % 2 == side:
                total = total + part[...].astype(WIDE)
        for which in range(2):
            stay[side, which] = total[which * own : (which + 1) * own]
        leave[2 * side * own : 2 * (side + 1) * own, :] = total[2 * own :]
    total = sums[0][...]
    for one in sums[1:]:
        total = total + one[...].astype(WIDE)
    half[...] = total
    leave[4 * own :, :] = total


def final_body(stay, got, half, *refs):
    in_grad, out_grad, kernel_grad, gain, bias, scale, in_bias, held = refs
    _, c, x = place()
    quarter = stay.shape[-1]
    own = stay.shape[2]
    for side in range(2):
        part = 2 * jnp.bitwise_xor(x, side)
        near = pl.ds(pl.multiple_of((part + c) * quarter, quarter), quarter)
        far = pl.ds(pl.multiple_of((part + 1 - c) * quarter, quarter), quarter)
        for which, target in enumerate((in_grad, out_grad)):
            start = (2 * side + which) * own
            target[:, near] = stay[side, which]
            target[:, far] = got[start : start + own, :]
    held[c] = half[...]
    held[1 - c] = got[4 * own :, :]

    def take(row):
        return held[row // SMALL_ROWS, pl.ds(row % SMALL_ROWS, 1), :]

    for tap_row in range(TAPS):
        for tap_col in range(TAPS):
            kernel_grad[tap_row, pl.ds(tap_col, 1), :] = take(TAPS * tap_row + tap_col)
    row = TAPS * TAPS
    gain[...] = take(row)
    bias[...] = take(row + 1)
    scale[...] = take(row + 2)
    for part in range(4):
        in_bias[:, pl.ds(part * quarter, quarter)] = take(row + 3 + part)


def flipped(blocks, axis, bit_set):
    return jnp.where(bit_set == 1, jnp.flip(blocks, axis), blocks)


def canonical(blocks, me, bit_count):
    tail = blocks.shape[1:]
    blocks = blocks.reshape((2,) * bit_count + tail)
    for spot in range(bit_count):
        blocks = flipped(blocks, bit_count - 1 - spot, (me >> spot) & 1)
    return blocks.reshape((2**bit_count,) + tail)


def per_device(
    features, cotangent, kernel, norm_gain, norm_bias, in_weight, in_bias, out_weight, layer_scale
):
    row_count, col_count, channels = features.shape
    own_rows, hidden_count = in_weight.shape
    pixels = row_count * col_count
    count = lax.axis_size("row")
    bit_count = count.bit_length() - 1
    me = lax.axis_index("row")
    group_index = lax.axis_index("grp")
    quarter = hidden_count // 4
    norm_scale = 1.0 / math.sqrt(pixels * count)
    patterns = count // 4
    copied = own_rows % 16 == 0
    gain_row = norm_gain.reshape(1, channels)
    bias_row = norm_bias.reshape(1, channels)
    scale_row = layer_scale.reshape(1, channels)
    rim = RIM * col_count
    padded = pltpu.VMEM((row_count + 2 * RIM, col_count + 2 * EDGE, channels), WIDE)

    piece = (2, own_rows, quarter)
    once = (features, cotangent, scale_row, kernel, gain_row, bias_row)
    own, core, outer, branch, in_bias_own, feats, cotan, scale, taps, gain, bias = run(
        split_body,
        (
            shaped((2,) + piece, NARROW),
            shaped((4 * own_rows + rim, channels), NARROW),
            shaped((rim, channels), NARROW),
            shaped((pixels, channels), NARROW),
            shaped((1, quarter)),
        )
        + tuple(shaped(x.shape) for x in once),
        in_weight,
        out_weight,
        in_bias.reshape(1, hidden_count),
        *once,
        scratch=(
            pltpu.VMEM(in_weight.shape, WIDE),
            pltpu.VMEM(out_weight.shape, WIDE),
            pltpu.VMEM((1, hidden_count), WIDE),
            pltpu.SemaphoreType.DMA((9,)),
        ),
        apart=True,
    )
    core_got = swap(core, 1)
    outer_got = swap_rim(outer)
    full_shape = shaped((2, 2, own_rows, quarter), NARROW)
    joined = run(
        join_body,
        (full_shape, shaped(piece, NARROW)) * 2,
        own,
        core_got,
    )
    pieces = []
    for side in range(2):
        full, sent = joined[2 * side : 2 * side + 2]
        here = [swap(sent, 4 * p + 2 * side) for p in range(2, patterns)]
        here = run(stack_body, (shaped((patterns - 2,) + piece, NARROW),), *here, order=8)[0]
        near = swap(full, 4 + 2 * side)
        pieces += [full, near, here, swap_group(here)]

    normed, inv, sent = run(
        conv_body,
        (
            shaped((pixels, channels)),
            shaped((pixels, LANES)),
            shaped((2 * pixels + 4 * own_rows, channels), NARROW),
        ),
        feats,
        core_got,
        outer_got,
        taps,
        gain,
        bias,
        branch,
        joined[2],
        scratch=(padded, pltpu.VMEM((pixels, channels), WIDE)),
    )
    first_blocks = [pieces[k] for k in (1, 3, 5, 7)]
    acts, pieces[4] = run(
        acts_body,
        (shaped((2, 2 * pixels, channels), NARROW), full_shape),
        sent,
        swap(sent, 2),
        *first_blocks,
    )
    acts_got = swap(acts, 1)

    if not copied:
        lines = []
        for pattern in range(patterns):
            for side in range(2):
                full, near, here, there = pieces[4 * side : 4 * side + 4]
                if pattern < 2:
                    lines.append(near if pattern else full)
                else:
                    pair = jnp.stack([here[pattern - 2], there[pattern - 2]])
                    lines.append(flipped(pair, 0, group_index))
        lines = jnp.moveaxis(jnp.stack(lines), 1, 2).reshape(count, 2, own_rows, quarter)
        lines = jnp.moveaxis(canonical(lines, me, bit_count), 1, 0)
        pieces = [lines.reshape(2, channels, quarter)]
    group = 4 * pixels
    keep, send, active, hidden, out_narrow, in_bias_part = run(
        functools.partial(hidden_body, copied),
        (
            shaped((2 * pixels, channels)),
            shaped((2 * pixels, channels), NARROW),
            shaped((group, quarter), NARROW),
            shaped((group, quarter), NARROW),
            shaped((channels, quarter), NARROW),
            shaped((1, quarter)),
        ),
        acts,
        acts_got,
        in_bias_own,
        *pieces,
        scratch=(pltpu.VMEM((2, channels, quarter), NARROW),),
        mib=24,
    )
    half = (shaped((pixels, channels)), shaped((pixels, channels), NARROW))
    out_stay, out_leave = run(fold_body, half, keep, swap(send, 1))
    out_got = swap(out_leave, 2)

    holder, mixed_keep, mixed_send, scale_part = run(
        functools.partial(weight_body, norm_scale),
        (
            shaped((2, channels, quarter)),
            shaped((2 * pixels, channels)),
            shaped((2 * pixels, channels), NARROW),
            shaped((1, channels)),
        ),
        acts,
        acts_got,
        active,
        hidden,
        out_narrow,
        scale,
        mib=24,
    )
    mixed_stay, mixed_leave = run(fold_body, half, mixed_keep, swap(mixed_send, 1))
    out_got, mixed_leave = lax.optimization_barrier((out_got, mixed_leave))
    conv_grad, inner_out, rim_out, stay, leave = run(
        functools.partial(conv_grad_body, norm_scale),
        (
            shaped((pixels, channels)),
            shaped((rim, channels), NARROW),
            shaped((rim, channels), NARROW),
            shaped((SMALL_ROWS, channels)),
            shaped((SMALL_ROWS, channels)),
        ),
        out_stay,
        out_got,
        normed,
        inv,
        gain,
        feats,
        core_got,
        outer_got,
        scale_part,
        in_bias_part,
        scratch=(padded, pltpu.VMEM((2, SMALL_ROWS, channels), WIDE)),
    )
    rim_got = swap_rim(rim_out)
    inner_got = swap(inner_out, 1)
    sums = stay + swap(leave, 1)

    first_turns = (*range(2 * patterns - 1, 4, -2), 3)
    solo = 2 * patterns - 2
    next_turns = (*range(4, solo, 2), 2, 1, 0)
    owned = 4 * own_rows
    if copied:
        parts = run(
            functools.partial(owners_body, (*first_turns, solo)),
            (shaped((owned, quarter), NARROW),) * (len(first_turns) + 1),
            holder,
            out_leave,
        )
    else:
        flat = holder.reshape(2, count, own_rows, quarter)
        flat = canonical(jnp.moveaxis(flat, 1, 0), me, bit_count)
        flat = flat.reshape(2 * patterns, owned, quarter)
        parts = [flat[p].astype(NARROW) for p in (*first_turns, solo)]
    first_parts = [swap(part, 2 * p) for p, part in zip(first_turns, parts)]
    solo_part = swap(parts[-1], 2 * solo)
    first_parts[:2], sums = lax.optimization_barrier((first_parts[:2], sums))
    sums = sums + swap(sums, 2)
    input_grad = run(
        input_grad_body,
        (shaped(features.shape),),
        conv_grad,
        inner_got,
        rim_got,
        taps,
        cotan,
        scratch=(padded,),
    )[0]
    sums, mixed_leave, solo_part, first_parts, input_grad = lax.optimization_barrier(
        (sums, mixed_leave, solo_part, first_parts, input_grad)
    )
    solo_sums = swap(sums.astype(NARROW), 2 * solo)
    if copied:
        joint = shaped((owned + 32, quarter), NARROW)
        *parts, side_part, near_own = run(
            functools.partial(owners_body, next_turns),
            (joint,) * (len(next_turns) - 2)
            + (shaped((owned, quarter), NARROW), shaped((owned, quarter))),
            holder,
            sums,
        )
        parts = [swap(part, 2 * p) for p, part in zip(next_turns, parts)]
        sums_parts = [part[owned : owned + SMALL_ROWS] for part in parts]
        next_parts = [part[:owned] for part in parts] + [swap(side_part, 2), near_own]
    else:
        next_parts = [swap(flat[p].astype(NARROW), 2 * p) for p in next_turns[:-1]] + [flat[0]]
        sums_parts = [swap(sums.astype(NARROW), 2 * p) for p in next_turns[:-2]]

    output = run(
        output_body,
        (shaped(features.shape),),
        feats,
        scale,
        mixed_stay,
        swap(mixed_leave, 2),
    )[0]
    parts = [*first_parts, solo_part, *next_parts]
    sums_parts.append(solo_sums)
    parts, input_grad, output = lax.optimization_barrier((parts, input_grad, output))

    stay, leave, half_sums = run(
        functools.partial(total_body, (*first_turns, solo, *next_turns)),
        (
            shaped((2, 2, own_rows, quarter)),
            shaped((owned + SMALL_ROWS, quarter)),
            shaped((SMALL_ROWS, channels)),
        ),
        *parts,
        sums,
        *sums_parts,
    )
    (
        in_weight_grad,
        out_weight_grad,
        kernel_grad,
        gain_grad,
        bias_grad,
        scale_grad,
        in_bias_grad,
    ) = run(
        final_body,
        (
            shaped((own_rows, hidden_count)),
            shaped((own_rows, hidden_count)),
            shaped(kernel.shape),
            shaped((1, channels)),
            shaped((1, channels)),
            shaped((1, channels)),
            shaped((1, hidden_count)),
        ),
        stay,
        swap(leave, 1),
        half_sums,
        scratch=(pltpu.VMEM((2, SMALL_ROWS, channels), WIDE),),
    )
    return (
        output,
        input_grad,
        in_weight_grad,
        out_weight_grad,
        kernel_grad,
        gain_grad.reshape(channels),
        bias_grad.reshape(channels),
        in_bias_grad.reshape(hidden_count),
        scale_grad.reshape(channels),
    )


def solution(mesh):
    return jax.shard_map(
        per_device,
        mesh=mesh,
        in_specs=(
            P(("grp", "row"), None, None),
            P(("grp", "row"), None, None),
            P(),
            P(),
            P(),
            P("row", None),
            P(),
            P("row", None),
            P(),
        ),
        out_specs=(
            P(("grp", "row"), None, None),
            P(("grp", "row"), None, None),
            P(("grp", "row"), None),
            P(("grp", "row"), None),
            P("grp", None, None),
            P("grp"),
            P("grp"),
            P("grp"),
            P("grp"),
        ),
        check_vma=False,
    )
```

```python
import functools
import math

import jax
import jax.numpy as jnp
from jax import lax
from jax.experimental import pallas as pl
from jax.experimental.pallas import tpu as pltpu
from jax.sharding import PartitionSpec as P

NARROW = jnp.bfloat16
WIDE = jnp.float32
TAPS = 7
RIM = 3
EDGE = 8
LANES = 128
SMALL_ROWS = 28


def swap(value, bit):
    count = lax.axis_size("row")
    return lax.ppermute(value, "row", [(i, i ^ bit) for i in range(count)])


def swap_rim(value):
    count = lax.axis_size("row")
    pairs = [(i, i + 1) for i in range(1, count - 1, 2)]
    return lax.ppermute(value, "row", pairs + [(j, i) for i, j in pairs])


def shaped(shape, dtype=WIDE):
    return jax.ShapeDtypeStruct(shape, dtype)


def swap_group(value):
    return lax.ppermute(value, "grp", [(0, 1), (1, 0)])


def run(body, outs, *operands, scratch=(), mib=16, order=0, apart=False):
    extra = {}
    if apart:
        extra = {"in_specs": [pl.BlockSpec(memory_space=pltpu.HBM)] * len(operands)}
        operands = [pltpu.with_memory_space_constraint(x, pltpu.HBM) for x in operands]
    return pl.pallas_call(
        body,
        out_shape=outs,
        **extra,
        scratch_shapes=scratch,
        compiler_params=pltpu.CompilerParams(vmem_limit_bytes=mib * 2**20),
        cost_estimate=pl.CostEstimate(flops=order * 10**9, bytes_accessed=0, transcendentals=0),
    )(*operands)


def place():
    me = lax.axis_index("row")
    return me, lax.rem(me, 2), lax.rem(lax.div(me, 2), 2)


def dot(left, right, dims):
    return lax.dot_general(left, right, (dims, ((), ())), preferred_element_type=WIDE)


def split_body(*refs):
    inw_hbm, outw_hbm, in_bias_hbm = refs[:3]
    own, core, outer, branch, bias_part = refs[9:14]
    inw, outw, in_bias, sems = refs[20:]
    feats, cotan, scale = refs[14:17]
    pairs = list(zip(refs[3:9], refs[14:20]))
    pairs += [(inw_hbm, inw), (outw_hbm, outw), (in_bias_hbm, in_bias)]
    copies = [pltpu.make_async_copy(a, b, sems.at[k]) for k, (a, b) in enumerate(pairs)]
    for copy in copies[6:] + copies[:6]:
        copy.start()
    me, c, x = place()
    even = c == 0
    quarter = own.shape[-1]
    rows, cols, channels = feats.shape
    own_rows = inw.shape[0]
    copies[6].wait()
    copies[7].wait()
    for side in range(2):
        for part, near in ((2 * jnp.bitwise_xor(x, side) + c, True), (2 * jnp.bitwise_xor(x, side) + 1 - c, False)):
            lanes = pl.ds(pl.multiple_of(part * quarter, quarter), quarter)
            for which, source in enumerate((inw, outw)):
                value = source[:, lanes].astype(NARROW)
                if near:
                    own[side, which] = value
                else:
                    core[pl.ds((2 * side + which) * own_rows, own_rows), :] = value
    copies[0].wait()
    first = feats[:RIM].astype(NARROW).reshape(RIM * cols, channels)
    last = feats[rows - RIM :].astype(NARROW).reshape(RIM * cols, channels)
    core[4 * own_rows :, :] = jnp.where(even, last, first)
    outer[...] = jnp.where(even, first, last)
    copies[1].wait()
    copies[2].wait()
    branch[...] = (scale[...] * cotan[...].reshape(branch.shape)).astype(NARROW)
    copies[8].wait()
    lanes = pl.ds(pl.multiple_of(lax.rem(me, 4) * quarter, quarter), quarter)
    bias_part[...] = in_bias[:, lanes]
    for copy in copies[3:6]:
        copy.wait()


def join_body(mine, other, *targets):
    group = lax.axis_index("grp")
    for side in range(2):
        full, sent = targets[2 * side : 2 * side + 2]
        own_rows = mine.shape[2]
        for which in range(2):
            full[which, 0] = mine[side, which]
            full[which, 1] = other[pl.ds((2 * side + which) * own_rows, own_rows), :]
        sent[...] = full[group]


def acts_body(mine, got, *refs):
    acts, full = refs[-2:]
    pixels = acts.shape[1] // 2
    for which in range(2):
        rows = slice(which * pixels, (which + 1) * pixels)
        acts[which, :pixels] = mine[rows, :]
        acts[which, pixels:] = got[rows, :]
        own = full.shape[2]
        for core in range(2):
            start = 2 * pixels + (2 * which + core) * own
            full[which, core] = got[start : start + own, :]


def stack_body(*refs):
    for place_in, ref in enumerate(refs[:-1]):
        refs[-1][place_in] = ref[...]


def fill(padded, block, inner, outer):
    rows, cols, channels = block.shape
    _, c, _ = place()
    padded[:, :EDGE, :] = jnp.zeros_like(padded[:, :EDGE, :])
    padded[:, EDGE + cols :, :] = jnp.zeros_like(padded[:, EDGE + cols :, :])
    middle = slice(EDGE, EDGE + cols)
    inner = inner.astype(WIDE).reshape(RIM, cols, channels)
    outer = outer.astype(WIDE).reshape(RIM, cols, channels)
    padded[:RIM, middle, :] = jnp.where(c == 0, outer, inner)
    padded[RIM : RIM + rows, middle, :] = block
    padded[RIM + rows :, middle, :] = jnp.where(c == 0, inner, outer)


def taps_sum(padded, kernel, lanes, rows, cols, mirrored, start):
    total = list(start)
    for tap_col in range(TAPS):
        for row in range(rows + TAPS - 1):
            line = padded[row, pl.ds(EDGE - RIM + tap_col, cols), lanes]
            for out in range(rows):
                tap_row = row - out
                if 0 <= tap_row < TAPS:
                    if mirrored:
                        tap = kernel[TAPS - 1 - tap_row, pl.ds(TAPS - 1 - tap_col, 1), lanes]
                    else:
                        tap = kernel[tap_row, pl.ds(tap_col, 1), lanes]
                    total[out] = total[out] + line * tap
    return total


def conv_body(
    feats, core_got, outer, kernel, gain, bias, branch, full, normed, inv, acts, padded, result
):
    rows, cols, channels = feats.shape
    start = core_got.shape[0] - RIM * cols
    fill(padded, feats[...], core_got[start:, :], outer[...])

    @pl.loop(0, channels // LANES)
    def _(step):
        lanes = pl.ds(pl.multiple_of(step * LANES, LANES), LANES)
        zero = [jnp.zeros((cols, LANES), WIDE)] * rows
        total = taps_sum(padded, kernel, lanes, rows, cols, False, zero)
        for row in range(rows):
            result[pl.ds(row * cols, cols), lanes] = total[row]

    value = result[...]
    centred = value - jnp.mean(value, axis=1, keepdims=True)
    spread = lax.rsqrt(jnp.mean(centred * centred, axis=1, keepdims=True) + 1e-06)
    value = centred * spread
    normed[...] = value
    inv[...] = jnp.broadcast_to(spread, inv.shape)
    pixels = rows * cols
    acts[:pixels, :] = (value * gain[...] + bias[...]).astype(NARROW)
    acts[pixels : 2 * pixels, :] = branch[...]
    own = full.shape[2]
    for which in range(2):
        for core in range(2):
            start = 2 * pixels + (2 * which + core) * own
            acts[start : start + own, :] = full[which, core]


def hidden_body(copied, *refs):
    patterns = lax.axis_size("row") // 4
    me, _, _ = place()
    acts, in_bias = refs[:2], refs[2]
    pieces = refs[3:-7]
    keep, send, active, hidden, out_copy, bias_part, weights = refs[-7:]
    half = acts[0].shape[1]
    if copied:
        own = pieces[0].shape[2]
        group = lax.axis_index("grp")
        for side in range(2):
            full, near, here, there = pieces[4 * side : 4 * side + 4]
            for pattern in range(patterns):
                for c in range(2):
                    device = jnp.bitwise_xor(me, 4 * pattern + 2 * side + c)
                    rows = pl.ds(pl.multiple_of(device * own, own), own)
                    if pattern < 2:
                        source = near if pattern else full
                        weights[0, rows, :] = source[0, c]
                        weights[1, rows, :] = source[1, c]
                    else:
                        weights[group, rows, :] = here[pattern - 2, c]
                        weights[1 - group, rows, :] = there[pattern - 2, c]
    else:
        weights[...] = pieces[0][...]
    in_narrow = weights.at[0]
    out_narrow = weights.at[1]
    out_copy[...] = weights[1]
    bias_row = in_bias[...]
    total = jnp.zeros_like(bias_row)
    for side in (1, 0):
        preact = dot(acts[side][0], in_narrow[...], ((1,), (0,))) + bias_row
        act_grad = dot(acts[side][1], out_narrow[...], ((1,), (0,)))
        cdf = 0.5 * (1.0 + lax.erf(preact * 0.7071067811865476))
        rows = pl.ds(side * half, half)
        activated = (preact * cdf).astype(NARROW)
        active[rows, :] = activated
        slope = cdf + preact * jnp.exp(-0.5 * preact * preact) * 0.3989422804014327
        grad = act_grad * slope
        total = total + jnp.sum(grad, axis=0, keepdims=True)
        narrow = grad.astype(NARROW)
        hidden[rows, :] = narrow
        out_grad = dot(narrow, in_narrow[...], ((1,), (1,)))
        if side:
            send[...] = out_grad.astype(NARROW)
        else:
            keep[...] = out_grad
    bias_part[...] = total


def weight_body(norm_scale, *refs):
    acts, (active, hidden, out_narrow, scale) = refs[:2], refs[2:6]
    holder, keep, send, scale_part = refs[6:]
    half = acts[0].shape[1]
    first, second = pl.ds(0, half), pl.ds(half, half)
    for which, right in enumerate((hidden, active)):
        grad = dot(acts[0][which], right[first, :], ((0,), (0,)))
        grad = grad + dot(acts[1][which], right[second, :], ((0,), (0,)))
        holder[which] = norm_scale * grad
    total = jnp.zeros_like(scale_part)
    for side, rows in enumerate((first, second)):
        mixed = dot(active[rows, :], out_narrow[...], ((1,), (1,)))
        total = total + jnp.sum(mixed * acts[side][1].astype(WIDE), axis=0, keepdims=True)
        if side:
            send[...] = mixed.astype(NARROW)
        else:
            keep[...] = mixed
    scale_part[...] = total / scale[...]


def owners_body(turns, holder, after, *targets):
    me, _, _ = place()
    own = holder.shape[1] // lax.axis_size("row")
    for pattern, target in zip(turns, targets):
        for c in range(2):
            device = jnp.bitwise_xor(me, 2 * pattern + c)
            rows = pl.ds(pl.multiple_of(device * own, own), own)
            for which in range(2):
                start = (2 * c + which) * own
                target[start : start + own, :] = holder[which, rows, :].astype(target.dtype)
        if target.shape[0] > 4 * own:
            target[4 * own : 4 * own + SMALL_ROWS, :] = after[...].astype(target.dtype)
            rest = target.shape[0] - 4 * own - SMALL_ROWS
            target[4 * own + SMALL_ROWS :, :] = jnp.zeros((rest, target.shape[1]), target.dtype)


def fold_body(kept, got, stay, leave):
    size = stay.shape[0]
    stay[...] = kept[:size] + got[:size].astype(WIDE)
    leave[...] = (kept[size:] + got[size:].astype(WIDE)).astype(NARROW)


def conv_grad_body(norm_scale, *refs):
    kept, got, normed, inv, gain, feats, core_got, outer, scale, in_bias = refs[:10]
    grad, inner_out, rim_out, stay, leave, padded, small = refs[10:]
    rows, cols, channels = feats.shape
    me, c, _ = place()
    out_grad = kept[...] + got[...].astype(WIDE)
    value = normed[...]
    normed_grad = out_grad * gain[...]
    mean = jnp.mean(normed_grad, axis=1, keepdims=True)
    along = jnp.mean(normed_grad * value, axis=1, keepdims=True)
    result = inv[:, :1] * (normed_grad - mean - value * along)
    grad[...] = result
    pixels = rows * cols
    rim = RIM * cols
    rim_out[...] = jnp.where(c == 0, result[:rim], result[pixels - rim :]).astype(NARROW)
    inner_out[...] = jnp.where(c == 0, result[pixels - rim :], result[:rim]).astype(NARROW)
    fill(padded, feats[...], core_got[core_got.shape[0] - rim :, :], outer[...])

    def put(row, lanes, total):
        small[row // SMALL_ROWS, pl.ds(row % SMALL_ROWS, 1), lanes] = norm_scale * total

    @pl.loop(0, channels // LANES)
    def _(step):
        lanes = pl.ds(pl.multiple_of(step * LANES, LANES), LANES)
        own = [grad[pl.ds(row * cols, cols), lanes] for row in range(rows)]
        for tap_col in range(TAPS):
            totals = [jnp.zeros((8, LANES), WIDE)] * TAPS
            for row in range(rows + TAPS - 1):
                line = padded[row, pl.ds(EDGE - RIM + tap_col, cols), lanes]
                for out in range(rows):
                    tap_row = row - out
                    if 0 <= tap_row < TAPS:
                        product = line * own[out]
                        for part in range(cols // 8):
                            totals[tap_row] = totals[tap_row] + product[8 * part : 8 * part + 8]
            for tap_row in range(TAPS):
                total = jnp.sum(totals[tap_row], axis=0, keepdims=True)
                put(TAPS * tap_row + tap_col, lanes, total)

    everything = slice(None)
    row = TAPS * TAPS
    put(row, everything, jnp.sum(out_grad * value, axis=0, keepdims=True))
    put(row + 1, everything, jnp.sum(out_grad, axis=0, keepdims=True))
    put(row + 2, everything, scale[...])
    for part in range(4):
        own_part = jnp.where(lax.rem(me, 4) == part, 1.0, 0.0)
        put(row + 3 + part, everything, own_part * in_bias[...])
    stay[...] = small[c]
    leave[...] = small[1 - c]


def input_grad_body(grad, inner, outer, kernel, cotan, result, padded):
    rows, cols, channels = cotan.shape
    fill(padded, grad[...].reshape(cotan.shape), inner[...], outer[...])

    @pl.loop(0, channels // LANES)
    def _(step):
        lanes = pl.ds(pl.multiple_of(step * LANES, LANES), LANES)
        start = [cotan[row, :, lanes] for row in range(rows)]
        total = taps_sum(padded, kernel, lanes, rows, cols, True, start)
        for row in range(rows):
            result[row, :, lanes] = total[row]


def output_body(feats, scale, kept, got, result):
    mixed = kept[...] + got[...].astype(WIDE)
    result[...] = feats[...] + (scale[...] * mixed).reshape(feats.shape)


def total_body(turns, *refs):
    parts, sums = refs[: len(turns)], refs[len(turns) : -3]
    stay, leave, half = refs[-3:]
    own = stay.shape[2]
    for side in range(2):
        total = jnp.zeros(parts[0].shape, WIDE)
        for part, turn in zip(parts, turns):
            if turn % 2 == side:
                total = total + part[...].astype(WIDE)
        for which in range(2):
            stay[side, which] = total[which * own : (which + 1) * own]
        leave[2 * side * own : 2 * (side + 1) * own, :] = total[2 * own :]
    total = sums[0][...]
    for one in sums[1:]:
        total = total + one[...].astype(WIDE)
    half[...] = total
    leave[4 * own :, :] = total


def final_body(stay, got, half, *refs):
    in_grad, out_grad, kernel_grad, gain, bias, scale, in_bias, held = refs
    _, c, x = place()
    quarter = stay.shape[-1]
    own = stay.shape[2]
    for side in range(2):
        part = 2 * jnp.bitwise_xor(x, side)
        near = pl.ds(pl.multiple_of((part + c) * quarter, quarter), quarter)
        far = pl.ds(pl.multiple_of((part + 1 - c) * quarter, quarter), quarter)
        for which, target in enumerate((in_grad, out_grad)):
            start = (2 * side + which) * own
            target[:, near] = stay[side, which]
            target[:, far] = got[start : start + own, :]
    held[c] = half[...]
    held[1 - c] = got[4 * own :, :]

    def take(row):
        return held[row // SMALL_ROWS, pl.ds(row % SMALL_ROWS, 1), :]

    for tap_row in range(TAPS):
        for tap_col in range(TAPS):
            kernel_grad[tap_row, pl.ds(tap_col, 1), :] = take(TAPS * tap_row + tap_col)
    row = TAPS * TAPS
    gain[...] = take(row)
    bias[...] = take(row + 1)
    scale[...] = take(row + 2)
    for part in range(4):
        in_bias[:, pl.ds(part * quarter, quarter)] = take(row + 3 + part)


def flipped(blocks, axis, bit_set):
    return jnp.where(bit_set == 1, jnp.flip(blocks, axis), blocks)


def canonical(blocks, me, bit_count):
    tail = blocks.shape[1:]
    blocks = blocks.reshape((2,) * bit_count + tail)
    for spot in range(bit_count):
        blocks = flipped(blocks, bit_count - 1 - spot, (me >> spot) & 1)
    return blocks.reshape((2**bit_count,) + tail)


def per_device(
    features, cotangent, kernel, norm_gain, norm_bias, in_weight, in_bias, out_weight, layer_scale
):
    row_count, col_count, channels = features.shape
    own_rows, hidden_count = in_weight.shape
    pixels = row_count * col_count
    count = lax.axis_size("row")
    bit_count = count.bit_length() - 1
    me = lax.axis_index("row")
    group_index = lax.axis_index("grp")
    quarter = hidden_count // 4
    norm_scale = 1.0 / math.sqrt(pixels * count)
    patterns = count // 4
    copied = own_rows % 16 == 0
    gain_row = norm_gain.reshape(1, channels)
    bias_row = norm_bias.reshape(1, channels)
    scale_row = layer_scale.reshape(1, channels)
    rim = RIM * col_count
    padded = pltpu.VMEM((row_count + 2 * RIM, col_count + 2 * EDGE, channels), WIDE)

    piece = (2, own_rows, quarter)
    once = (features, cotangent, scale_row, kernel, gain_row, bias_row)
    own, core, outer, branch, in_bias_own, feats, cotan, scale, taps, gain, bias = run(
        split_body,
        (
            shaped((2,) + piece, NARROW),
            shaped((4 * own_rows + rim, channels), NARROW),
            shaped((rim, channels), NARROW),
            shaped((pixels, channels), NARROW),
            shaped((1, quarter)),
        )
        + tuple(shaped(x.shape) for x in once),
        in_weight,
        out_weight,
        in_bias.reshape(1, hidden_count),
        *once,
        scratch=(
            pltpu.VMEM(in_weight.shape, WIDE),
            pltpu.VMEM(out_weight.shape, WIDE),
            pltpu.VMEM((1, hidden_count), WIDE),
            pltpu.SemaphoreType.DMA((9,)),
        ),
        apart=True,
    )
    core_got = swap(core, 1)
    outer_got = swap_rim(outer)
    full_shape = shaped((2, 2, own_rows, quarter), NARROW)
    joined = run(
        join_body,
        (full_shape, shaped(piece, NARROW)) * 2,
        own,
        core_got,
    )
    pieces = []
    for side in range(2):
        full, sent = joined[2 * side : 2 * side + 2]
        here = [swap(sent, 4 * p + 2 * side) for p in range(2, patterns)]
        here = run(stack_body, (shaped((patterns - 2,) + piece, NARROW),), *here, order=8)[0]
        near = swap(full, 4 + 2 * side)
        pieces += [full, near, here, swap_group(here)]

    normed, inv, sent = run(
        conv_body,
        (
            shaped((pixels, channels)),
            shaped((pixels, LANES)),
            shaped((2 * pixels + 4 * own_rows, channels), NARROW),
        ),
        feats,
        core_got,
        outer_got,
        taps,
        gain,
        bias,
        branch,
        joined[2],
        scratch=(padded, pltpu.VMEM((pixels, channels), WIDE)),
    )
    first_blocks = [pieces[k] for k in (1, 3, 5, 7)]
    acts, pieces[4] = run(
        acts_body,
        (shaped((2, 2 * pixels, channels), NARROW), full_shape),
        sent,
        swap(sent, 2),
        *first_blocks,
    )
    acts_got = swap(acts, 1)

    if not copied:
        lines = []
        for pattern in range(patterns):
            for side in range(2):
                full, near, here, there = pieces[4 * side : 4 * side + 4]
                if pattern < 2:
                    lines.append(near if pattern else full)
                else:
                    pair = jnp.stack([here[pattern - 2], there[pattern - 2]])
                    lines.append(flipped(pair, 0, group_index))
        lines = jnp.moveaxis(jnp.stack(lines), 1, 2).reshape(count, 2, own_rows, quarter)
        lines = jnp.moveaxis(canonical(lines, me, bit_count), 1, 0)
        pieces = [lines.reshape(2, channels, quarter)]
    group = 4 * pixels
    keep, send, active, hidden, out_narrow, in_bias_part = run(
        functools.partial(hidden_body, copied),
        (
            shaped((2 * pixels, channels)),
            shaped((2 * pixels, channels), NARROW),
            shaped((group, quarter), NARROW),
            shaped((group, quarter), NARROW),
            shaped((channels, quarter), NARROW),
            shaped((1, quarter)),
        ),
        acts,
        acts_got,
        in_bias_own,
        *pieces,
        scratch=(pltpu.VMEM((2, channels, quarter), NARROW),),
        mib=24,
    )
    half = (shaped((pixels, channels)), shaped((pixels, channels), NARROW))
    out_stay, out_leave = run(fold_body, half, keep, swap(send, 1))
    out_got = swap(out_leave, 2)

    holder, mixed_keep, mixed_send, scale_part = run(
        functools.partial(weight_body, norm_scale),
        (
            shaped((2, channels, quarter)),
            shaped((2 * pixels, channels)),
            shaped((2 * pixels, channels), NARROW),
            shaped((1, channels)),
        ),
        acts,
        acts_got,
        active,
        hidden,
        out_narrow,
        scale,
        mib=24,
    )
    mixed_stay, mixed_leave = run(fold_body, half, mixed_keep, swap(mixed_send, 1))
    out_got, mixed_leave = lax.optimization_barrier((out_got, mixed_leave))
    conv_grad, inner_out, rim_out, stay, leave = run(
        functools.partial(conv_grad_body, norm_scale),
        (
            shaped((pixels, channels)),
            shaped((rim, channels), NARROW),
            shaped((rim, channels), NARROW),
            shaped((SMALL_ROWS, channels)),
            shaped((SMALL_ROWS, channels)),
        ),
        out_stay,
        out_got,
        normed,
        inv,
        gain,
        feats,
        core_got,
        outer_got,
        scale_part,
        in_bias_part,
        scratch=(padded, pltpu.VMEM((2, SMALL_ROWS, channels), WIDE)),
    )
    rim_got = swap_rim(rim_out)
    inner_got = swap(inner_out, 1)
    sums = stay + swap(leave, 1)

    first_turns = (*range(2 * patterns - 1, 4, -2), 3)
    solo = 2 * patterns - 2
    next_turns = (*range(4, solo, 2), 2, 1, 0)
    owned = 4 * own_rows
    if copied:
        parts = run(
            functools.partial(owners_body, (*first_turns, solo)),
            (shaped((owned, quarter), NARROW),) * (len(first_turns) + 1),
            holder,
            out_leave,
        )
    else:
        flat = holder.reshape(2, count, own_rows, quarter)
        flat = canonical(jnp.moveaxis(flat, 1, 0), me, bit_count)
        flat = flat.reshape(2 * patterns, owned, quarter)
        parts = [flat[p].astype(NARROW) for p in (*first_turns, solo)]
    first_parts = [swap(part, 2 * p) for p, part in zip(first_turns, parts)]
    solo_part = swap(parts[-1], 2 * solo)
    first_parts[:2], sums = lax.optimization_barrier((first_parts[:2], sums))
    sums = sums + swap(sums, 2)
    sums, mixed_leave, solo_part, first_parts, rim_got, inner_got = lax.optimization_barrier(
        (sums, mixed_leave, solo_part, first_parts, rim_got, inner_got)
    )
    solo_sums = swap(sums.astype(NARROW), 2 * solo)
    if copied:
        joint = shaped((owned + 32, quarter), NARROW)
        *parts, side_part, near_own = run(
            functools.partial(owners_body, next_turns),
            (joint,) * (len(next_turns) - 2)
            + (shaped((owned, quarter), NARROW), shaped((owned, quarter))),
            holder,
            sums,
        )
        parts = [swap(part, 2 * p) for p, part in zip(next_turns, parts)]
        sums_parts = [part[owned : owned + SMALL_ROWS] for part in parts]
        next_parts = [part[:owned] for part in parts] + [swap(side_part, 2), near_own]
    else:
        next_parts = [swap(flat[p].astype(NARROW), 2 * p) for p in next_turns[:-1]] + [flat[0]]
        sums_parts = [swap(sums.astype(NARROW), 2 * p) for p in next_turns[:-2]]

    input_grad = run(
        input_grad_body,
        (shaped(features.shape),),
        conv_grad,
        inner_got,
        rim_got,
        taps,
        cotan,
        scratch=(padded,),
    )[0]
    output = run(
        output_body,
        (shaped(features.shape),),
        feats,
        scale,
        mixed_stay,
        swap(mixed_leave, 2),
    )[0]
    parts = [*first_parts, solo_part, *next_parts]
    sums_parts.append(solo_sums)
    parts, input_grad, output = lax.optimization_barrier((parts, input_grad, output))

    stay, leave, half_sums = run(
        functools.partial(total_body, (*first_turns, solo, *next_turns)),
        (
            shaped((2, 2, own_rows, quarter)),
            shaped((owned + SMALL_ROWS, quarter)),
            shaped((SMALL_ROWS, channels)),
        ),
        *parts,
        sums,
        *sums_parts,
    )
    (
        in_weight_grad,
        out_weight_grad,
        kernel_grad,
        gain_grad,
        bias_grad,
        scale_grad,
        in_bias_grad,
    ) = run(
        final_body,
        (
            shaped((own_rows, hidden_count)),
            shaped((own_rows, hidden_count)),
            shaped(kernel.shape),
            shaped((1, channels)),
            shaped((1, channels)),
            shaped((1, channels)),
            shaped((1, hidden_count)),
        ),
        stay,
        swap(leave, 1),
        half_sums,
        scratch=(pltpu.VMEM((2, SMALL_ROWS, channels), WIDE),),
    )
    return (
        output,
        input_grad,
        in_weight_grad,
        out_weight_grad,
        kernel_grad,
        gain_grad.reshape(channels),
        bias_grad.reshape(channels),
        in_bias_grad.reshape(hidden_count),
        scale_grad.reshape(channels),
    )


def solution(mesh):
    return jax.shard_map(
        per_device,
        mesh=mesh,
        in_specs=(
            P(("grp", "row"), None, None),
            P(("grp", "row"), None, None),
            P(),
            P(),
            P(),
            P("row", None),
            P(),
            P("row", None),
            P(),
        ),
        out_specs=(
            P(("grp", "row"), None, None),
            P(("grp", "row"), None, None),
            P(("grp", "row"), None),
            P(("grp", "row"), None),
            P("grp", None, None),
            P("grp"),
            P("grp"),
            P("grp"),
            P("grp"),
        ),
        check_vma=False,
    )
```
